32 devices in a mesh: dp: 2 (over x), seq: 16 (over z, y, core).
Axes of the slice: x: 2, y: 2, z: 4, core: 2. Of those that a mesh axis runs over, the one named last changes fastest.
Arguments:
- head_queries: bfloat16 [2, 2048, 3072], P('dp', 'seq')
- head_keys: bfloat16 [2, 2048, 3072], P('dp', 'seq')
- head_values: bfloat16 [2, 2048, 3072], P('dp', 'seq'), may hold values from -6 to 6
- output_gradient: bfloat16 [2, 2048, 3072], P('dp', 'seq'), may hold values from -96 to 96
- key_adapter_input: bfloat16 [2, 2048, 64], P('dp', 'seq'), may hold values from -0.09375 to 0.09375
- value_adapter_input: bfloat16 [2, 2048, 64], P('dp', 'seq'), may hold values from -0.09375 to 0.09375
- key_block_lists: int32 [24, 16, 5], replicated, may hold values from 0 to 15, as said below
- live_block_counts: int32 [24, 16], replicated, may hold values from 1 to 5, as said below
Outputs:
- key_gradient: bfloat16 [2, 2048, 3072], P('dp', 'seq')
- value_gradient: bfloat16 [2, 2048, 3072], P('dp', 'seq')
- key_adapter_gradient: float32 [3072, 64], P(('dp', 'seq'))
- value_adapter_gradient: float32 [3072, 64], P(('dp', 'seq'))
The draws below stay inside these ranges and needn't reach their ends.
Inputs may be any that keep to these rules, and one draw needn't show every extreme that they name: Entry 0 of key_block_lists[h, b] is b; the first live_block_counts[h, b] entries are distinct blocks within 2 of b; later entries equal b. live_block_counts[h, b] is the smaller of a count of head h and the number of blocks within 2 of b.
All inputs are finite; a program needn't handle non-finite values.
Results may differ from the reference program's by a relative error of at most 0.04.
Values may be sent and summed in bfloat16 or wider, within the bound.
No kernel may reach another device: no remote copies, remote signals or barrier semaphores. Data moves between devices by JAX's collectives and lax.ppermute only.
A program may use at most 64 MiB of HBM per device.

```python
import jax
import jax.numpy as jnp
from jax import lax

HEAD_COUNT = 24
HEAD_WIDTH = 128
ADAPTER_RANK = 64
BLK = 128
REACH = 2
TILES = 5
CLIP_TOKENS = 2048
CLIP_COUNT = 2
TOTAL_TOKENS = 4096


def pattern_draw(base_key):
    nblocks = CLIP_TOKENS // BLK
    tile_count = 2 * REACH + 1
    per_head = jax.random.randint(jax.random.fold_in(base_key, 11), (HEAD_COUNT,), 2, tile_count + 1)
    widest = jax.random.randint(jax.random.fold_in(base_key, 12), (), 0, HEAD_COUNT)
    narrow = (widest + 1 + jax.random.randint(jax.random.fold_in(base_key, 13), (), 0, HEAD_COUNT - 1)) % HEAD_COUNT
    per_head = per_head.at[widest].set(tile_count).at[narrow].set(1)
    blocks = jnp.arange(nblocks, dtype=jnp.int32)
    offsets = jnp.arange(tile_count, dtype=jnp.int32) - REACH
    target = blocks[:, None] + offsets[None, :]
    inside = (target >= 0) & (target < nblocks)
    rolls = jax.random.randint(jax.random.fold_in(base_key, 14), (HEAD_COUNT, nblocks, tile_count), 0, 65536) * tile_count + offsets[None, None, :] + REACH
    rolls = jnp.where(offsets[None, None, :] == 0, -1, rolls)
    rolls = jnp.where(inside[None], rolls, rolls + 65536 * tile_count * 2)
    ranked = jnp.argsort(rolls, axis=-1, stable=True)
    chosen = jnp.take_along_axis(jnp.broadcast_to(target[None], (HEAD_COUNT, nblocks, tile_count)), ranked, axis=-1)
    available = jnp.sum(inside.astype(jnp.int32), axis=1)
    counts = jnp.minimum(per_head[:, None], available[None, :])
    in_use = jnp.arange(tile_count, dtype=jnp.int32)[None, None, :] < counts[:, :, None]
    entries = jnp.where(in_use, chosen, blocks[None, :, None])
    return (entries.astype(jnp.int32), counts.astype(jnp.int32))


def attention_draw(base_key):
    shape = (CLIP_COUNT, CLIP_TOKENS, HEAD_COUNT * HEAD_WIDTH)
    queries = jax.random.normal(jax.random.fold_in(base_key, 21), shape, jnp.float32)
    keyset = jax.random.normal(jax.random.fold_in(base_key, 22), shape, jnp.float32)
    return (queries, keyset)


def draw_head_queries(key, part):
    return attention_draw(key)[0].astype(jnp.bfloat16)


def draw_head_keys(key, part):
    return attention_draw(key)[1].astype(jnp.bfloat16)


def draw_key_block_lists(key, part):
    return pattern_draw(key)[0]


def draw_live_block_counts(key, part):
    return pattern_draw(key)[1]


def raised(values, stream_key, source, target, blocks, factor):
    owner, partner = [(jnp.arange(values.shape[position]) // (values.shape[position] // blocks)).reshape([-1 if axis == position else 1 for axis in range(values.ndim)]) for position in (source, target)]
    chosen = jax.random.permutation(stream_key, blocks)[partner]
    strong = (owner == chosen) | (owner == (partner + blocks // 2) % blocks)
    return jnp.where(strong, factor * values, values)


def shard_levels(own_key, shape, pieces, smallest, high):
    gain, own = 1.0, jax.random.fold_in(own_key, 6)
    for position, blocks in pieces:
        heights = jnp.exp(jax.random.uniform(jax.random.fold_in(own, position), (blocks,), jnp.float32, smallest / len(pieces), high / len(pieces)))
        gain = gain * jnp.repeat(heights, shape[position] // blocks).reshape([-1 if axis == position else 1 for axis in range(len(shape))])
    return gain


def scatter_about(key, shape, scale, bound, pieces=(), kind=jnp.bfloat16):
    values = jax.random.normal(key, shape, jnp.float32) * scale
    if len(pieces) > 0:
        values = shard_levels(key, shape, pieces, -0.22, 0.18) * values
    return jnp.clip(values, min=-bound, max=bound).astype(kind)


def gaussian_with(stream_key, shape, scale, limit, pieces, heavy, kind=jnp.bfloat16):
    result = scale * jax.random.normal(stream_key, shape, jnp.float32)
    if pieces:
        result = result * shard_levels(stream_key, shape, pieces, -0.22, 0.18)
    return jnp.clip(raised(result, jax.random.fold_in(stream_key, 3), *heavy), -limit, limit).astype(kind)


def setup_inputs(seed: int = 0) -> dict:
    keys = jax.random.split(jax.random.key(seed), 9)
    head_queries = draw_head_queries(jax.random.fold_in(keys[8], 71), 0)
    head_keys = draw_head_keys(jax.random.fold_in(keys[8], 71), 0)
    head_values = scatter_about(keys[2], (CLIP_COUNT, CLIP_TOKENS, HEAD_COUNT * HEAD_WIDTH), 1.0, 6.0, ((0, 2), (1, 16)))
    output_gradient = gaussian_with(keys[3], (CLIP_COUNT, CLIP_TOKENS, HEAD_COUNT * HEAD_WIDTH), 16.0, 96.0, ((0, 2), (1, 16)), (1, 2, 16, 2.0))
    key_adapter_input = scatter_about(keys[4], (CLIP_COUNT, CLIP_TOKENS, ADAPTER_RANK), (TOTAL_TOKENS ** -0.5), 0.09375, ((0, 2), (1, 16)))
    value_adapter_input = scatter_about(keys[5], (CLIP_COUNT, CLIP_TOKENS, ADAPTER_RANK), (TOTAL_TOKENS ** -0.5), 0.09375, ((0, 2), (1, 16)))
    key_block_lists = draw_key_block_lists(jax.random.fold_in(keys[8], 71), 0)
    live_block_counts = draw_live_block_counts(jax.random.fold_in(keys[8], 71), 0)
    return {"head_queries": head_queries, "head_keys": head_keys, "head_values": head_values, "output_gradient": output_gradient, "key_adapter_input": key_adapter_input, "value_adapter_input": value_adapter_input, "key_block_lists": key_block_lists, "live_block_counts": live_block_counts}


def head_backward(query_tiles, key_tiles, value_tiles, grad_tiles, head_lists, head_counts):
    scaling = HEAD_WIDTH ** -0.5
    block_total = query_tiles.shape[0]
    picked_keys = jnp.take(key_tiles, head_lists, axis=0).astype(jnp.float32)
    picked_values = jnp.take(value_tiles, head_lists, axis=0).astype(jnp.float32)
    query_float = query_tiles.astype(jnp.float32)
    grad_float = grad_tiles.astype(jnp.float32)
    scores = jnp.einsum('bxd,btyd->btxy', query_float, picked_keys) * scaling
    in_use = (jnp.arange(TILES, dtype=jnp.int32)[None, :] < head_counts[:, None])[:, :, None, None]
    row_max = jnp.max(jnp.where(in_use, scores, -jnp.inf), axis=(1, 3), keepdims=True)
    exponent = jnp.where(in_use, jnp.exp(scores - row_max), 0.0)
    soft_probs = exponent / jnp.sum(exponent, axis=(1, 3), keepdims=True)
    soft_rounded = soft_probs.astype(jnp.bfloat16)
    dprobs = jnp.einsum('bxd,btyd->btxy', grad_float, picked_values)
    row_delta = jnp.sum(soft_rounded.astype(jnp.float32) * dprobs, axis=(1, 3), keepdims=True)
    score_grad = (soft_probs * (dprobs - row_delta)).astype(jnp.bfloat16)
    value_add = jnp.einsum('btxy,bxd->btyd', soft_rounded.astype(jnp.float32), grad_float)
    key_add = jnp.einsum('btxy,bxd->btyd', score_grad.astype(jnp.float32), query_float) * scaling
    value_acc = jnp.zeros((block_total, BLK, HEAD_WIDTH), jnp.float32).at[head_lists].add(value_add)
    key_acc = jnp.zeros((block_total, BLK, HEAD_WIDTH), jnp.float32).at[head_lists].add(key_add)
    return key_acc.astype(jnp.bfloat16), value_acc.astype(jnp.bfloat16)


def reference(head_queries, head_keys, head_values, output_gradient, key_adapter_input, value_adapter_input, key_block_lists, live_block_counts):
    nblocks = CLIP_TOKENS // BLK

    def arrange(array):
        return array.reshape(CLIP_COUNT, nblocks, BLK, HEAD_COUNT, HEAD_WIDTH).transpose(0, 3, 1, 2, 4).reshape(CLIP_COUNT * HEAD_COUNT, nblocks, BLK, HEAD_WIDTH)

    queries = arrange(head_queries)
    keyset = arrange(head_keys)
    valueset = arrange(head_values)
    gradset = arrange(output_gradient)

    def one_pair(pair_index):
        head_id = pair_index % HEAD_COUNT
        return head_backward(queries[pair_index], keyset[pair_index], valueset[pair_index], gradset[pair_index], key_block_lists[head_id], live_block_counts[head_id])

    key_parts, value_parts = lax.map(one_pair, jnp.arange(CLIP_COUNT * HEAD_COUNT, dtype=jnp.int32))

    def restore(array):
        return array.reshape(CLIP_COUNT, HEAD_COUNT, nblocks, BLK, HEAD_WIDTH).transpose(0, 2, 3, 1, 4).reshape(CLIP_COUNT, CLIP_TOKENS, HEAD_COUNT * HEAD_WIDTH)

    key_gradient = restore(key_parts)
    value_gradient = restore(value_parts)
    contract_dims = (((0,), (0,)), ((), ()))
    key_adapter_gradient = lax.dot_general(key_gradient.reshape(CLIP_COUNT * CLIP_TOKENS, HEAD_COUNT * HEAD_WIDTH), key_adapter_input.reshape(CLIP_COUNT * CLIP_TOKENS, ADAPTER_RANK), contract_dims, preferred_element_type=jnp.float32)
    value_adapter_gradient = lax.dot_general(value_gradient.reshape(CLIP_COUNT * CLIP_TOKENS, HEAD_COUNT * HEAD_WIDTH), value_adapter_input.reshape(CLIP_COUNT * CLIP_TOKENS, ADAPTER_RANK), contract_dims, preferred_element_type=jnp.float32)
    return key_gradient, value_gradient, key_adapter_gradient, value_adapter_gradient
```

```python
import functools

import jax
import jax.numpy as jnp
from jax import lax
from jax.experimental import pallas as pl
from jax.experimental.pallas import tpu as pltpu
from jax.sharding import PartitionSpec as P

HEAD_COUNT = 24
HEAD_WIDTH = 128
BLK = 128
REACH = 2
TILES = 5
RANK = 64
TEAM = 4
HEADS = HEAD_COUNT // TEAM
CHUNKS = (3, 3)
WINDOW = TEAM + 2 * REACH
SCALING = HEAD_WIDTH**-0.5
LOG2E = 1.4426950408889634
ANY = pl.BlockSpec(memory_space=pl.ANY)
VMEM = pl.BlockSpec(memory_space=pltpu.VMEM)
SMEM = pl.BlockSpec(memory_space=pltpu.SMEM)


def cols(first, count):
    if isinstance(first, int):
        return pl.ds(first * HEAD_WIDTH, count * HEAD_WIDTH)
    return pl.ds(pl.multiple_of(first * HEAD_WIDTH, HEAD_WIDTH), count * HEAD_WIDTH)


def rows(first, count):
    if isinstance(first, int):
        return pl.ds(first * BLK, count * BLK)
    return pl.ds(pl.multiple_of(first * BLK, BLK), count * BLK)


def first_heads():
    return [sum(CHUNKS[:c]) for c in range(len(CHUNKS))]


def pack_kernel(with_adapters, *refs):
    a_ref, b_ref = refs[:2]
    ins = 4 if with_adapters else 2
    outs = refs[ins : ins + TEAM * len(CHUNKS)]
    sems = refs[ins + len(outs)]
    member = lax.rem(lax.axis_index("seq"), TEAM)
    copies = []

    def start(source, target):
        copy = pltpu.make_async_copy(source, target, sems.at[len(copies)])
        copy.start()
        copies.append(copy)

    for c, (first, count) in enumerate(zip(first_heads(), CHUNKS)):
        for k in (2, 3, 1, 0):
            owner = jnp.bitwise_xor(member, k)
            out = outs[c * TEAM + k]
            head = owner * HEADS + first
            start(a_ref.at[0, :, cols(head, count)], out.at[:, cols(0, count)])
            start(b_ref.at[0, :, cols(head, count)], out.at[:, cols(count, count)])
    if with_adapters:
        tile = refs[ins + len(outs) + 1]
        tile[:, :RANK] = refs[2][0]
        tile[:, RANK:] = refs[3][0]
        for k in range(TEAM):
            start(tile, outs[k].at[:, cols(2 * CHUNKS[0], 1)])
    for copy in copies:
        copy.wait()


def pack(first, second, adapters=()):
    tokens = first.shape[1]
    out_shape = []
    for c, count in enumerate(CHUNKS):
        tiles = 2 * count + (1 if adapters and c == 0 else 0)
        out_shape += [jax.ShapeDtypeStruct((tokens, tiles * HEAD_WIDTH), first.dtype)] * TEAM
    copies = 2 * len(out_shape) + (TEAM if adapters else 0)
    scratch = [pltpu.SemaphoreType.DMA((copies,))]
    if adapters:
        scratch.append(pltpu.VMEM((tokens, 2 * RANK), first.dtype))
    outs = pl.pallas_call(
        functools.partial(pack_kernel, bool(adapters)),
        out_shape=out_shape,
        in_specs=[ANY, ANY] + [VMEM] * len(adapters),
        out_specs=[ANY] * len(out_shape),
        scratch_shapes=scratch,
        name="pack_kv" if adapters else "pack_qg",
    )(first, second, *adapters)
    return [outs[c * TEAM : (c + 1) * TEAM] for c in range(len(CHUNKS))]


def compute_kernel(count, first, leading, *refs):
    bias_ref = refs[0]
    kv = refs[1 : 1 + TEAM]
    halo = refs[1 + TEAM : 1 + 2 * TEAM]
    qg = refs[1 + 2 * TEAM : 1 + 3 * TEAM]
    rest = refs[1 + 3 * TEAM :]
    if leading:
        own_ref, a_ref, b_ref, term_ref, adapt_ref = rest[:5]
        rest = rest[5:]
    else:
        adapt_ref, own_ref, a_ref, b_ref, term_ref = rest[:5]
        rest = rest[5:]
    kw, vw, qs, gs, acc_k, acc_v, pm, dm = rest
    position = lax.axis_index("seq")
    member = lax.rem(position, TEAM)
    even = lax.rem(position // TEAM, 2) == 0

    places = []
    for j in range(TEAM):
        owner = jnp.bitwise_xor(member, j)
        places.append((owner, owner + REACH, lax.rem(owner + REACH + TEAM, WINDOW)))

    if leading:
        column = cols(2 * count, 1)
        for j, (_, near, far) in enumerate(places):
            acc_k[rows(near, 1), :] = kv[j][:, column].astype(jnp.float32)
            acc_k[rows(far, 1), :] = halo[j][:, column].astype(jnp.float32)
        adapt_ref[...] = acc_k[...].T.astype(adapt_ref.dtype)

    zero = jnp.zeros((BLK, BLK), pm.dtype)
    pm[rows(TEAM + 1, 1), :BLK] = zero
    dm[rows(TEAM + 1, 1), :BLK] = zero
    pm[rows(0, 1), BLK:] = zero
    dm[rows(0, 1), BLK:] = zero

    def one_head(h, carry):
        for j, (owner, near, far) in enumerate(places):
            kw[rows(near, 1), :] = kv[j][:, cols(h, 1)]
            vw[rows(near, 1), :] = kv[j][:, cols(count + h, 1)]
            kw[rows(far, 1), :] = halo[j][:, cols(h, 1)]
            vw[rows(far, 1), :] = halo[j][:, cols(count + h, 1)]
            qs[rows(owner, 1), :] = qg[j][:, cols(h, 1)]
            gs[rows(owner, 1), :] = qg[j][:, cols(count + h, 1)]
        for pair in range(TEAM // 2):
            span = rows(2 * pair, TILES + 1)
            queries = qs[rows(2 * pair, 2), :]
            grads = gs[rows(2 * pair, 2), :]
            on_last = (((1,), (1,)), ((), ()))
            scores = lax.dot_general(kw[span, :], queries, on_last, preferred_element_type=jnp.float32)
            dprobs = lax.dot_general(vw[span, :], grads, on_last, preferred_element_type=jnp.float32)
            for u in range(2):
                base = ((first + h) * TEAM + 2 * pair + u) * TILES
                lanes = slice(u * BLK, (u + 1) * BLK)
                logits = []
                for t in range(TILES):
                    tile = scores[(u + t) * BLK : (u + t + 1) * BLK, lanes]
                    logits.append(tile * (SCALING * LOG2E) + bias_ref[base + t])
                logits = jnp.concatenate(logits, axis=0)
                top = jnp.max(logits, axis=0, keepdims=True)
                weights = jnp.exp2(logits - top)
                inverse = 1.0 / jnp.sum(weights, axis=0, keepdims=True)
                probs = weights * inverse
                dp = dprobs[u * BLK : (u + TILES) * BLK, lanes]
                delta = jnp.sum(probs * dp, axis=0, keepdims=True)
                pm[rows(u, TILES), lanes] = probs.astype(pm.dtype)
                dm[rows(u, TILES), lanes] = (probs * (dp - delta)).astype(dm.dtype)
            value_add = jnp.dot(pm[...], grads, preferred_element_type=jnp.float32)
            key_add = jnp.dot(dm[...], queries, preferred_element_type=jnp.float32) * SCALING
            if pair == 0:
                acc_v[rows(0, TILES + 1), :] = value_add
                acc_k[rows(0, TILES + 1), :] = key_add
            else:
                split = TEAM * BLK
                acc_v[rows(2, TEAM), :] += value_add[:split]
                acc_k[rows(2, TEAM), :] += key_add[:split]
                acc_v[rows(2 + TEAM, 2), :] = value_add[split:]
                acc_k[rows(2 + TEAM, 2), :] = key_add[split:]
        for acc, place, half in ((acc_k, cols(h, 1), 0), (acc_v, cols(count + h, 1), RANK)):
            own_ref[:, place] = acc[rows(REACH, TEAM), :]
            lower = acc[rows(0, REACH), :].astype(a_ref.dtype)
            upper = acc[rows(REACH + TEAM, REACH), :].astype(a_ref.dtype)
            a_ref[:, place] = jnp.where(even, upper, lower)
            b_ref[:, place] = jnp.where(even, lower, upper)
            term_ref[half : half + RANK, cols(h, 1)] = jnp.dot(
                adapt_ref[half : half + RANK, :],
                acc[...].astype(adapt_ref.dtype),
                preferred_element_type=jnp.float32,
            )
        return carry

    lax.fori_loop(0, count, one_head, 0)


def compute(c, bias, kv, halo, qg, adapt):
    count, first = CHUNKS[c], first_heads()[c]
    leading = c == 0
    kind = qg[0].dtype
    width = 2 * count * HEAD_WIDTH
    out_shape = [
        jax.ShapeDtypeStruct((TEAM * BLK, width), jnp.float32),
        jax.ShapeDtypeStruct((REACH * BLK, width), kind),
        jax.ShapeDtypeStruct((REACH * BLK, width), kind),
        jax.ShapeDtypeStruct((2 * RANK, count * HEAD_WIDTH), jnp.float32),
    ]
    inputs = [bias, *kv, *halo, *qg]
    if leading:
        out_shape.append(jax.ShapeDtypeStruct((2 * RANK, WINDOW * BLK), kind))
    else:
        inputs.append(adapt)
    tall, team = WINDOW * BLK, TEAM * BLK
    return pl.pallas_call(
        functools.partial(compute_kernel, count, first, leading),
        out_shape=out_shape,
        in_specs=[SMEM] + [VMEM] * (len(inputs) - 1),
        out_specs=[VMEM] * len(out_shape),
        scratch_shapes=[
            pltpu.VMEM((tall, HEAD_WIDTH), kind),
            pltpu.VMEM((tall, HEAD_WIDTH), kind),
            pltpu.VMEM((team, HEAD_WIDTH), kind),
            pltpu.VMEM((team, HEAD_WIDTH), kind),
            pltpu.VMEM((tall, HEAD_WIDTH), jnp.float32),
            pltpu.VMEM((tall, HEAD_WIDTH), jnp.float32),
            pltpu.VMEM(((TILES + 1) * BLK, 2 * BLK), kind),
            pltpu.VMEM(((TILES + 1) * BLK, 2 * BLK), kind),
        ],
        compiler_params=pltpu.CompilerParams(vmem_limit_bytes=24 << 20),
        cost_estimate=pl.CostEstimate(
            flops=count * 4 * 2 * 2 * 6 * BLK * 2 * BLK * HEAD_WIDTH, bytes_accessed=8 << 20, transcendentals=0
        ),
        name=f"gradients_{c}",
    )(*inputs)


def combine_kernel(own_ref, a_ref, b_ref, *outs):
    position = lax.axis_index("seq")
    member = lax.rem(position, TEAM)
    even = lax.rem(position // TEAM, 2)
    for k in range(TEAM):
        owner = jnp.bitwise_xor(member, k)
        from_a = owner // 2 != even
        row = rows(lax.rem(owner, 2), 1)
        part = jnp.where(from_a, a_ref[row, :], b_ref[row, :]).astype(jnp.float32)
        outs[k][...] = (own_ref[rows(owner, 1), :] + part).astype(outs[k].dtype)


def combine(c, own, a, b):
    shape = jax.ShapeDtypeStruct((BLK, own.shape[1]), a.dtype)
    return pl.pallas_call(
        combine_kernel,
        out_shape=[shape] * TEAM,
        in_specs=[VMEM] * 3,
        out_specs=[VMEM] * TEAM,
        compiler_params=pltpu.CompilerParams(vmem_limit_bytes=16 << 20),
        name=f"combine_{c}",
    )(own, a, b)


def unpack_kernel(*refs):
    ins = refs[: TEAM * len(CHUNKS)]
    key_ref, value_ref, sems = refs[len(ins) :]
    member = lax.rem(lax.axis_index("seq"), TEAM)
    copies = []
    for c, (first, count) in enumerate(zip(first_heads(), CHUNKS)):
        for k in range(TEAM):
            head = jnp.bitwise_xor(member, k) * HEADS + first
            for part, out in enumerate((key_ref, value_ref)):
                copy = pltpu.make_async_copy(
                    ins[c * TEAM + k].at[:, cols(part * count, count)],
                    out.at[0, :, cols(head, count)],
                    sems.at[len(copies)],
                )
                copy.start()
                copies.append(copy)
    for copy in copies:
        copy.wait()


def unpack(home):
    flat = [block for chunk in home for block in chunk]
    shape = jax.ShapeDtypeStruct((1, flat[0].shape[0], HEAD_COUNT * HEAD_WIDTH), flat[0].dtype)
    return pl.pallas_call(
        unpack_kernel,
        out_shape=[shape, shape],
        in_specs=[ANY] * len(flat),
        out_specs=[ANY, ANY],
        scratch_shapes=[pltpu.SemaphoreType.DMA((2 * len(flat),))],
        name="unpack",
    )(*flat)


def pieces_kernel(pieces, bit_of, *refs):
    terms = refs[: len(CHUNKS)]
    keep_ref, send_ref, whole = refs[len(CHUNKS) :]
    for first, term in zip(first_heads(), terms):
        whole[:, cols(first, term.shape[1] // HEAD_WIDTH)] = term[...]
    upper = bit_of() == 1
    width = whole.shape[1] // pieces
    half = pieces // 2
    for j in range(half):
        low = whole[:, j * width : (j + 1) * width]
        high = whole[:, (half + j) * width : (half + j + 1) * width]
        keep_ref[j] = jnp.where(upper, high, low)
        send_ref[j] = jnp.where(upper, low, high)


def reduce_terms(terms):
    clips, seq = lax.axis_size("dp"), lax.axis_size("seq")
    teams = seq // TEAM
    pieces = clips * teams
    rounds = [("dp", clips >> s, 1) for s in range(1, clips.bit_length())]
    rounds += [("seq", teams >> s, TEAM) for s in range(1, teams.bit_length())]

    def bit_value(axis, bit, unit):
        return lax.axis_index(axis) // (bit * unit) % 2

    def first_bit():
        axis, bit, unit = rounds[0]
        return lax.rem(lax.axis_index(axis) // (bit * unit), 2)

    width = HEADS * HEAD_WIDTH // pieces
    shape = jax.ShapeDtypeStruct((pieces // 2, 2 * RANK, width), jnp.float32)
    held, sent = pl.pallas_call(
        functools.partial(pieces_kernel, pieces, first_bit),
        out_shape=[shape, shape],
        in_specs=[VMEM] * len(terms),
        out_specs=[VMEM, VMEM],
        scratch_shapes=[pltpu.VMEM((2 * RANK, HEADS * HEAD_WIDTH), jnp.float32)],
        compiler_params=pltpu.CompilerParams(vmem_limit_bytes=16 << 20),
        name="pieces",
    )(*terms)
    for index, (axis, bit, unit) in enumerate(rounds):
        if index > 0:
            half = held.shape[0] // 2
            value = bit_value(axis, bit, unit)
            sent = lax.dynamic_slice_in_dim(held, (1 - value) * half, half, 0)
            held = lax.dynamic_slice_in_dim(held, value * half, half, 0)
        route = [(i, i ^ (bit * unit)) for i in range(lax.axis_size(axis))]
        held = held + lax.ppermute(sent, axis, route)
    route = []
    for clip in range(clips):
        for position in range(seq):
            piece = clip * teams + position // TEAM
            route.append((clip * seq + position, position % TEAM * pieces + piece))
    return lax.ppermute(held[0], ("dp", "seq"), route)


def body(
    head_queries,
    head_keys,
    head_values,
    output_gradient,
    key_adapter_input,
    value_adapter_input,
    key_block_lists,
    live_block_counts,
):
    seq = lax.axis_size("seq")
    teams = seq // TEAM
    position = lax.axis_index("seq")
    member = position % TEAM
    team = position // TEAM

    def partner(block, k):
        return lax.ppermute(block, "seq", [(i, i ^ k) for i in range(seq)]) if k else block

    near = []
    for p in range(seq):
        t = p // TEAM + (1 if p % TEAM >= TEAM // 2 else -1)
        if 0 <= t < teams:
            near.append((p, t * TEAM + p % TEAM))
    far = [(target, source) for source, target in near]
    swaps = []
    for start in (0, 1):
        pairs = []
        for t in range(start, teams - 1, 2):
            for m in range(TEAM):
                pairs += [(t * TEAM + m, (t + 1) * TEAM + m), ((t + 1) * TEAM + m, t * TEAM + m)]
        swaps.append(pairs)

    kv_sent = pack(head_keys, head_values, (key_adapter_input, value_adapter_input))
    kv = [[partner(chunk[k], k) for k in range(TEAM)] for chunk in kv_sent]
    qg_sent = pack(head_queries, output_gradient)
    qg = [[partner(chunk[k], k) for k in range(TEAM)] for chunk in qg_sent]
    halo = [[lax.ppermute(chunk[k], "seq", near if k < 2 else far) for k in range(TEAM)] for chunk in kv]

    lists = lax.dynamic_slice(key_block_lists, (member * HEADS, team * TEAM, 0), (HEADS, TEAM, TILES))
    counts = lax.dynamic_slice(live_block_counts, (member * HEADS, team * TEAM), (HEADS, TEAM))
    own_block = team * TEAM + jnp.arange(TEAM, dtype=jnp.int32)
    window = own_block[:, None] - REACH + jnp.arange(TILES, dtype=jnp.int32)
    listed = lists[:, :, :, None] == window[None, :, None, :]
    in_use = jnp.arange(TILES, dtype=jnp.int32) < counts[:, :, None]
    live = jnp.any(listed & in_use[:, :, :, None], axis=2)
    bias = jnp.where(live, 0.0, -jnp.inf).astype(jnp.float32).reshape(-1)

    adapt = None
    home, terms = [], []
    for c in range(len(CHUNKS)):
        results = compute(c, bias, kv[c], halo[c], qg[c], adapt)
        own, to_a, to_b, term = results[:4]
        if c == 0:
            adapt = results[4]
        terms.append(term)
        from_a = lax.ppermute(to_a, "seq", swaps[0])
        from_b = lax.ppermute(to_b, "seq", swaps[1])
        blocks = combine(c, own, from_a, from_b)
        home.append([partner(block, k) for k, block in enumerate(blocks)])
    summed = reduce_terms(terms)
    key_gradient, value_gradient = unpack(home)
    return key_gradient, value_gradient, summed[:RANK].T, summed[RANK:].T


def solution(mesh):
    tokens = P("dp", "seq", None)
    shares = P(("dp", "seq"), None)
    return jax.shard_map(
        body,
        mesh=mesh,
        in_specs=(tokens,) * 6 + (P(), P()),
        out_specs=(tokens, tokens, shares, shares),
        check_vma=False,
    )
```

```python
import functools

import jax
import jax.numpy as jnp
from jax import lax
from jax.experimental import pallas as pl
from jax.experimental.pallas import tpu as pltpu
from jax.sharding import PartitionSpec as P

HEAD_COUNT = 24
HEAD_WIDTH = 128
BLK = 128
REACH = 2
TILES = 5
RANK = 64
TEAM = 4
HEADS = HEAD_COUNT // TEAM
CHUNKS = (3, 3)
WINDOW = TEAM + 2 * REACH
SCALING = HEAD_WIDTH**-0.5
LOG2E = 1.4426950408889634
ANY = pl.BlockSpec(memory_space=pl.ANY)
VMEM = pl.BlockSpec(memory_space=pltpu.VMEM)
SMEM = pl.BlockSpec(memory_space=pltpu.SMEM)


def call(kernel, name, out_shape, inputs, in_specs=None, scratch=(), vmem=4):
    return pl.pallas_call(
        kernel,
        out_shape=out_shape,
        in_specs=in_specs or [VMEM] * len(inputs),
        out_specs=[VMEM] * len(out_shape),
        scratch_shapes=list(scratch),
        compiler_params=pltpu.CompilerParams(vmem_limit_bytes=vmem << 20),
        cost_estimate=pl.CostEstimate(flops=1, bytes_accessed=1, transcendentals=0),
        name=name,
    )(*inputs)


def cols(first, count):
    if not isinstance(first, int):
        first = pl.multiple_of(first * HEAD_WIDTH, HEAD_WIDTH)
    else:
        first = first * HEAD_WIDTH
    return pl.ds(first, count * HEAD_WIDTH)


def rows(first, count):
    if not isinstance(first, int):
        first = pl.multiple_of(first * BLK, BLK)
    else:
        first = first * BLK
    return pl.ds(first, count * BLK)


def place():
    position = lax.axis_index("seq")
    return lax.rem(position, TEAM), position // TEAM


def pack_kernel(adapters, *refs):
    a_ref, b_ref = refs[:2]
    outs = refs[-TEAM:]
    member, _ = place()
    for k in range(TEAM):
        head = jnp.bitwise_xor(member, k) * HEADS
        outs[k][:, cols(0, HEADS)] = a_ref[0, :, cols(head, HEADS)]
        outs[k][:, cols(HEADS, HEADS)] = b_ref[0, :, cols(head, HEADS)]
    if adapters:
        for k in range(TEAM):
            outs[k][:RANK, cols(2 * HEADS, 1)] = refs[2][0]
            outs[k][RANK:, cols(2 * HEADS, 1)] = refs[3][0]


def pack(first, second, adapters=(), after=()):
    tiles = 2 * HEADS + (1 if adapters else 0)
    shape = jax.ShapeDtypeStruct((BLK, tiles * HEAD_WIDTH), first.dtype)
    inputs = [first, second, *adapters, *after]
    specs = [VMEM] * (2 + len(adapters)) + [ANY] * len(after)
    name = "pack_kv" if adapters else "pack_qg"
    return call(functools.partial(pack_kernel, bool(adapters)), name, [shape] * TEAM, inputs, specs)


def stack_kernel(first_ref, second_ref, out_ref):
    out_ref[rows(0, 1), :] = first_ref[...]
    out_ref[rows(1, 1), :] = second_ref[...]


def stack(first, second, name):
    shape = jax.ShapeDtypeStruct((2 * BLK, first.shape[1]), first.dtype)
    return call(stack_kernel, name, [shape], [first, second])[0]


def compute_kernel(first, count, lists_ref, counts_ref, *refs):
    kv, near_ref, far_ref, qg = refs[:TEAM], refs[TEAM], refs[TEAM + 1], refs[TEAM + 2 : 2 * TEAM + 2]
    own_ref, a_ref, b_ref, term_ref, kw, vw, qs, gs, acc_k, acc_v, pm, dm, adapt = refs[2 * TEAM + 2 :]
    member, team = place()
    even = lax.rem(team, 2) == 0

    places = []
    for j in range(TEAM):
        owner = jnp.bitwise_xor(member, j)
        halo = (near_ref if j < 2 else far_ref, rows(j % 2, 1))
        places.append((owner, owner + REACH, lax.rem(owner + REACH + TEAM, WINDOW), halo))

    for j, (_, near, far, (halo, row)) in enumerate(places):
        adapt[:, rows(near, 1)] = kv[j][:, cols(2 * HEADS, 1)]
        adapt[:, rows(far, 1)] = halo[row, cols(2 * HEADS, 1)]

    zero = jnp.zeros((BLK, BLK), pm.dtype)
    for matrix in (pm, dm):
        matrix[rows(TILES, 1), :BLK] = zero
        matrix[rows(0, 1), BLK:] = zero

    def one_head(h, carry):
        head = first + h
        for j, (owner, near, far, (halo, row)) in enumerate(places):
            kw[rows(near, 1), :] = kv[j][:, cols(head, 1)]
            vw[rows(near, 1), :] = kv[j][:, cols(HEADS + head, 1)]
            kw[rows(far, 1), :] = halo[row, cols(head, 1)]
            vw[rows(far, 1), :] = halo[row, cols(HEADS + head, 1)]
            qs[rows(owner, 1), :] = qg[j][:, cols(head, 1)]
            gs[rows(owner, 1), :] = qg[j][:, cols(HEADS + head, 1)]
        for pair in range(TEAM // 2):
            span = rows(2 * pair, TILES + 1)
            queries = qs[rows(2 * pair, 2), :]
            grads = gs[rows(2 * pair, 2), :]
            on_last = (((1,), (1,)), ((), ()))
            scores = lax.dot_general(kw[span, :], queries, on_last, preferred_element_type=jnp.float32)
            dprobs = lax.dot_general(vw[span, :], grads, on_last, preferred_element_type=jnp.float32)
            for u in range(2):
                block = team * TEAM + 2 * pair + u
                whole_head = member * HEADS + head
                used = counts_ref[block, whole_head]
                live = jnp.int32(0)
                for t in range(TILES):
                    offset = lists_ref[t, block, whole_head] - block + REACH
                    live = live | jnp.where(t < used, jnp.left_shift(1, offset), 0)
                lanes = slice(u * BLK, (u + 1) * BLK)
                logits = []
                for t in range(TILES):
                    tile = scores[(u + t) * BLK : (u + t + 1) * BLK, lanes]
                    masked = jnp.where((live >> t) & 1 == 1, 0.0, -jnp.inf)
                    logits.append(tile * (SCALING * LOG2E) + masked)
                logits = jnp.concatenate(logits, axis=0)
                top = jnp.max(logits, axis=0, keepdims=True)
                weights = jnp.exp2(logits - top)
                inverse = 1.0 / jnp.sum(weights, axis=0, keepdims=True)
                probs = weights * inverse
                dp = dprobs[u * BLK : (u + TILES) * BLK, lanes]
                delta = jnp.sum(probs * dp, axis=0, keepdims=True)
                pm[rows(u, TILES), lanes] = probs.astype(pm.dtype)
                dm[rows(u, TILES), lanes] = (probs * (dp - delta)).astype(dm.dtype)
            value_add = jnp.dot(pm[...], grads, preferred_element_type=jnp.float32)
            key_add = jnp.dot(dm[...], queries, preferred_element_type=jnp.float32) * SCALING
            if pair == 0:
                acc_v[rows(0, TILES + 1), :] = value_add
                acc_k[rows(0, TILES + 1), :] = key_add
            else:
                split = TEAM * BLK
                acc_v[rows(2, TEAM), :] += value_add[:split]
                acc_k[rows(2, TEAM), :] += key_add[:split]
                acc_v[rows(2 + TEAM, 2), :] = value_add[split:]
                acc_k[rows(2 + TEAM, 2), :] = key_add[split:]
        for acc, column, half in ((acc_k, cols(h, 1), 0), (acc_v, cols(count + h, 1), RANK)):
            own_ref[:, column] = acc[rows(REACH, TEAM), :]
            lower = acc[rows(0, REACH), :].astype(a_ref.dtype)
            upper = acc[rows(REACH + TEAM, REACH), :].astype(a_ref.dtype)
            a_ref[:, column] = jnp.where(even, upper, lower)
            b_ref[:, column] = jnp.where(even, lower, upper)
            term_ref[half : half + RANK, cols(h, 1)] = jnp.dot(
                adapt[half : half + RANK, :], acc[...].astype(adapt.dtype), preferred_element_type=jnp.float32
            )
        return carry

    if UNROLL:
        for h in range(count):
            one_head(h, 0)
    else:
        lax.fori_loop(0, count, one_head, 0)


UNROLL = True


def compute(c, lists, counts, kv, near, far, qg):
    first, count = sum(CHUNKS[:c]), CHUNKS[c]
    kind = qg[0].dtype
    width = 2 * count * HEAD_WIDTH
    out_shape = [
        jax.ShapeDtypeStruct((TEAM * BLK, width), jnp.float32),
        jax.ShapeDtypeStruct((REACH * BLK, width), kind),
        jax.ShapeDtypeStruct((REACH * BLK, width), kind),
        jax.ShapeDtypeStruct((2 * RANK, count * HEAD_WIDTH), jnp.float32),
    ]
    inputs = [lists, counts, *kv, near, far, *qg]
    tall, team = WINDOW * BLK, TEAM * BLK
    scratch = [
        pltpu.VMEM((tall, HEAD_WIDTH), kind),
        pltpu.VMEM((tall, HEAD_WIDTH), kind),
        pltpu.VMEM((team, HEAD_WIDTH), kind),
        pltpu.VMEM((team, HEAD_WIDTH), kind),
        pltpu.VMEM((tall, HEAD_WIDTH), jnp.float32),
        pltpu.VMEM((tall, HEAD_WIDTH), jnp.float32),
        pltpu.VMEM(((TILES + 1) * BLK, 2 * BLK), kind),
        pltpu.VMEM(((TILES + 1) * BLK, 2 * BLK), kind),
        pltpu.VMEM((2 * RANK, tall), kind),
    ]
    specs = [SMEM] * 2 + [VMEM] * (len(inputs) - 2)
    kernel = functools.partial(compute_kernel, first, count)
    return call(kernel, f"gradients_{c}", out_shape, inputs, specs, scratch, 8)


def combine_kernel(own_ref, a_ref, b_ref, *outs):
    member, team = place()
    even = lax.rem(team, 2)
    for k in range(TEAM):
        owner = jnp.bitwise_xor(member, k)
        row = rows(lax.rem(owner, 2), 1)
        from_a = owner // 2 != even

        def add(part_ref, k=k, owner=owner, row=row):
            part = part_ref[row, :].astype(jnp.float32)
            outs[k][...] = (own_ref[rows(owner, 1), :] + part).astype(outs[k].dtype)

        pl.when(from_a)(functools.partial(add, a_ref))
        pl.when(jnp.logical_not(from_a))(functools.partial(add, b_ref))


def combine(c, own, a, b):
    shape = jax.ShapeDtypeStruct((BLK, own.shape[1]), a.dtype)
    return call(combine_kernel, f"combine_{c}", [shape] * TEAM, [own, a, b])


def unpack_kernel(*refs):
    ins, outs = refs[: TEAM * len(CHUNKS)], refs[TEAM * len(CHUNKS) :]
    member, _ = place()
    for c, count in enumerate(CHUNKS):
        for k in range(TEAM):
            head = jnp.bitwise_xor(member, k) * HEADS + sum(CHUNKS[:c])
            for part, out in enumerate(outs):
                out[0, :, cols(head, count)] = ins[c * TEAM + k][:, cols(part * count, count)]


def unpack(home):
    flat = [block for chunk in home for block in chunk]
    shape = jax.ShapeDtypeStruct((1, BLK, HEAD_COUNT * HEAD_WIDTH), flat[0].dtype)
    return call(unpack_kernel, "unpack", [shape, shape], flat)


def bit_value(axis, bit, unit):
    return lax.rem(lax.axis_index(axis) // (bit * unit), 2)


def pieces_kernel(pieces, bit, *refs):
    terms = refs[: len(CHUNKS)]
    keep_ref, send_ref, whole = refs[len(CHUNKS) :]
    for c, term in enumerate(terms):
        whole[:, cols(sum(CHUNKS[:c]), CHUNKS[c])] = term[...]
    upper = bit_value(*bit) == 1
    width = whole.shape[1] // pieces
    half = pieces // 2
    for j in range(half):
        low = whole[:, j * width : (j + 1) * width]
        high = whole[:, (half + j) * width : (half + j + 1) * width]
        keep_ref[j] = jnp.where(upper, high, low)
        send_ref[j] = jnp.where(upper, low, high)


def fold_kernel(bit, held_ref, got_ref, *outs):
    half = held_ref.shape[0] // 2
    if bit is None:
        outs[0][...] = held_ref[0] + got_ref[0]
        return
    value = bit_value(*bit)
    for out, first in ((outs[0], value * half), (outs[1], (1 - value) * half)):
        out[...] = held_ref[pl.ds(first, half)] + got_ref[pl.ds(first, half)]


def split_kernel(in_ref, key_ref, value_ref):
    key_ref[...] = in_ref[:RANK, :]
    value_ref[...] = in_ref[RANK:, :]


def reduce_terms(terms):
    clips, seq = lax.axis_size("dp"), lax.axis_size("seq")
    teams = seq // TEAM
    pieces = clips * teams
    rounds = [("dp", clips >> s, 1) for s in range(1, clips.bit_length())]
    rounds += [("seq", teams >> s, TEAM) for s in range(1, teams.bit_length())]
    width = HEADS * HEAD_WIDTH // pieces
    shape = jax.ShapeDtypeStruct((pieces // 2, 2 * RANK, width), jnp.float32)
    scratch = [pltpu.VMEM((2 * RANK, HEADS * HEAD_WIDTH), jnp.float32)]
    kernel = functools.partial(pieces_kernel, pieces, rounds[0])
    held, sent = call(kernel, "pieces", [shape, shape], terms, scratch=scratch)
    for index, (axis, bit, unit) in enumerate(rounds):
        route = [(i, i ^ (bit * unit)) for i in range(lax.axis_size(axis))]
        got = lax.ppermute(sent, axis, route)
        following = rounds[index + 1] if index + 1 < len(rounds) else None
        if following:
            shape = jax.ShapeDtypeStruct((held.shape[0] // 2, 2 * RANK, width), jnp.float32)
            out_shape = [shape, shape]
        else:
            out_shape = [jax.ShapeDtypeStruct((2 * RANK, width), jnp.float32)]
        folded = call(functools.partial(fold_kernel, following), f"fold_{index}", out_shape, [held, got])
        held, sent = folded[0], folded[-1]
    route = []
    for clip in range(clips):
        for position in range(seq):
            piece = clip * teams + position // TEAM
            route.append((clip * seq + position, position % TEAM * pieces + piece))
    shape = jax.ShapeDtypeStruct((RANK, width), jnp.float32)
    return call(split_kernel, "split", [shape, shape], [lax.ppermute(held, ("dp", "seq"), route)])


def body(
    head_queries,
    head_keys,
    head_values,
    output_gradient,
    key_adapter_input,
    value_adapter_input,
    key_block_lists,
    live_block_counts,
):
    seq = lax.axis_size("seq")
    teams = seq // TEAM

    def partner(block, k):
        return lax.ppermute(block, "seq", [(i, i ^ k) for i in range(seq)]) if k else block

    near_route = []
    for p in range(seq):
        t = p // TEAM + (1 if p % TEAM >= TEAM // 2 else -1)
        if 0 <= t < teams:
            near_route.append((p, t * TEAM + p % TEAM))
    far_route = [(target, source) for source, target in near_route]
    swaps = []
    for start in (0, 1):
        pairs = []
        for t in range(start, teams - 1, 2):
            for m in range(TEAM):
                pairs += [(t * TEAM + m, (t + 1) * TEAM + m), ((t + 1) * TEAM + m, t * TEAM + m)]
        swaps.append(pairs)

    lists = key_block_lists.transpose(2, 1, 0)
    counts = live_block_counts.T
    adapters = (key_adapter_input.transpose(0, 2, 1), value_adapter_input.transpose(0, 2, 1))
    kv_out = pack(head_keys, head_values, adapters)
    kv = [partner(block, k) for k, block in enumerate(kv_out)]
    qg_out = pack(head_queries, output_gradient, after=kv_out[:1])
    qg = [partner(block, k) for k, block in enumerate(qg_out)]
    near = lax.ppermute(stack(kv[0], kv[1], "near"), "seq", near_route)
    far = lax.ppermute(stack(kv[2], kv[3], "far"), "seq", far_route)

    home, terms = [], []
    for c in range(len(CHUNKS)):
        own, to_a, to_b, term = compute(c, lists, counts, kv, near, far, qg)
        terms.append(term)
        from_a = lax.ppermute(to_a, "seq", swaps[0])
        from_b = lax.ppermute(to_b, "seq", swaps[1])
        blocks = combine(c, own, from_a, from_b)
        home.append([partner(block, k) for k, block in enumerate(blocks)])
    key_term, value_term = reduce_terms(terms)
    key_gradient, value_gradient = unpack(home)
    return key_gradient, value_gradient, key_term.T, value_term.T


def solution(mesh):
    tokens = P("dp", "seq", None)
    shares = P(("dp", "seq"), None)
    return jax.shard_map(
        body,
        mesh=mesh,
        in_specs=(tokens,) * 6 + (P(), P()),
        out_specs=(tokens, tokens, shares, shares),
        check_vma=False,
    )
```

```python
import functools

import jax
import jax.numpy as jnp
from jax import lax
from jax.experimental import pallas as pl
from jax.experimental.pallas import tpu as pltpu
from jax.sharding import PartitionSpec as P

HEAD_COUNT = 24
HEAD_WIDTH = 128
BLK = 128
REACH = 2
TILES = 5
RANK = 64
TEAM = 4
HEADS = HEAD_COUNT // TEAM
CHUNKS = (3, 3)
LOADS = 4
WINDOW = TEAM + 2 * REACH
SCALING = HEAD_WIDTH**-0.5
LOG2E = 1.4426950408889634
ANY = pl.BlockSpec(memory_space=pl.ANY)
PACK_VMEM = 62
VMEM = pl.BlockSpec(memory_space=pltpu.VMEM)
SMEM = pl.BlockSpec(memory_space=pltpu.SMEM)


def call(kernel, name, out_shape, inputs, in_specs=None, scratch=(), vmem=4):
    return pl.pallas_call(
        kernel,
        out_shape=out_shape,
        in_specs=in_specs or [VMEM] * len(inputs),
        out_specs=[VMEM] * len(out_shape),
        scratch_shapes=list(scratch),
        compiler_params=pltpu.CompilerParams(vmem_limit_bytes=vmem << 20),
        cost_estimate=pl.CostEstimate(flops=1, bytes_accessed=1, transcendentals=0),
        name=name,
    )(*inputs)


def cols(first, count):
    if not isinstance(first, int):
        first = pl.multiple_of(first * HEAD_WIDTH, HEAD_WIDTH)
    else:
        first = first * HEAD_WIDTH
    return pl.ds(first, count * HEAD_WIDTH)


def rows(first, count):
    if not isinstance(first, int):
        first = pl.multiple_of(first * BLK, BLK)
    else:
        first = first * BLK
    return pl.ds(first, count * BLK)


def place():
    position = lax.axis_index("seq")
    return lax.rem(position, TEAM), position // TEAM


def spans():
    return [(sum(CHUNKS[:c]), count) for c, count in enumerate(CHUNKS)]


class Tiles:
    def __init__(self, ref, span=(0, HEADS), row=0):
        self.ref, (self.first, self.count), self.row = ref, span, row

    def tile(self, head, part):
        place = 2 * self.count if part == 2 else part * self.count + head - self.first
        return self.ref[rows(self.row, 1), cols(place, 1)]


def pack_spans(adapters):
    plan = []
    for k in range(TEAM):
        for span in [(0, HEADS)] if k < 2 else spans():
            plan.append((k, span, bool(adapters) and span[0] == 0))
    return plan


def fill(plan, a_ref, b_ref, adapter_refs, outs, part):
    member, _ = place()
    for (k, (first, count), adapted), out in zip(plan, outs):
        head = jnp.bitwise_xor(member, k) * HEADS + first
        out[part, cols(0, count)] = a_ref[part, cols(head, count)]
        out[part, cols(count, count)] = b_ref[part, cols(head, count)]
    return adapter_refs


def pack_kv_kernel(plan, keys, values, key_in, value_in, *refs):
    outs, (tall, small, sems) = refs[:-3], refs[-3:]
    size = BLK // LOADS
    copies = []
    for part in range(LOADS):
        for index, source in enumerate((keys, values)):
            piece = pl.ds(part * size, size)
            copies.append((source.at[0, piece, :], tall.at[index, piece, :]))
    copies += [(key_in.at[0], small.at[0]), (value_in.at[0], small.at[1])]
    copies = [pltpu.make_async_copy(*pair, sems.at[i]) for i, pair in enumerate(copies)]
    for copy in copies:
        copy.start()
    for part in range(LOADS):
        for copy in copies[2 * part : 2 * part + 2]:
            copy.wait()
        fill(plan, tall.at[0], tall.at[1], None, outs, pl.ds(part * size, size))
    for copy in copies[2 * LOADS :]:
        copy.wait()
    for (k, (_, count), adapted), out in zip(plan, outs):
        if adapted:
            out[:RANK, cols(2 * count, 1)] = small[0]
            out[RANK:, cols(2 * count, 1)] = small[1]


def pack_qg_kernel(plan, queries, grads, _, *outs):
    fill(plan, queries.at[0], grads.at[0], None, outs, slice(None))


def pack(first, second, adapters=(), after=()):
    plan = pack_spans(adapters)
    kind = first.dtype
    out_shape = [
        jax.ShapeDtypeStruct((BLK, (2 * count + adapted) * HEAD_WIDTH), kind) for _, (_, count), adapted in plan
    ]
    if adapters:
        scratch = [
            pltpu.VMEM((2, BLK, HEAD_COUNT * HEAD_WIDTH), kind),
            pltpu.VMEM((2, RANK, BLK), kind),
            pltpu.SemaphoreType.DMA((2 * LOADS + 2,)),
        ]
        kernel = functools.partial(pack_kv_kernel, plan)
        outs = call(kernel, "pack_kv", out_shape, [first, second, *adapters], [ANY] * 4, scratch, PACK_VMEM)
    else:
        kernel = functools.partial(pack_qg_kernel, plan)
        outs = call(kernel, "pack_qg", out_shape, [first, second, *after], [VMEM, VMEM, ANY])
    chunks = len(CHUNKS)
    return [outs[0], outs[1], outs[2 : 2 + chunks], outs[2 + chunks :]]


def stack_kernel(span, first_ref, second_ref, *refs):
    out = refs[-1]
    for row, ref in enumerate((first_ref, second_ref)):
        if span is None:
            out[rows(row, 1), :] = ref[...]
            continue
        first, count = span
        out[rows(row, 1), cols(0, count)] = ref[:, cols(first, count)]
        out[rows(row, 1), cols(count, count)] = ref[:, cols(HEADS + first, count)]
        if first == 0:
            out[rows(row, 1), cols(2 * count, 1)] = ref[:, cols(2 * HEADS, 1)]


def stack(first, second, name, span=None, after=()):
    width = (2 * span[1] + (span[0] == 0)) * HEAD_WIDTH if span else first.shape[1]
    shape = jax.ShapeDtypeStruct((2 * BLK, width), first.dtype)
    specs = [VMEM] * 2 + [ANY] * len(after)
    kernel = functools.partial(stack_kernel, span)
    return call(kernel, name, [shape], [first, second, *after], specs)[0]


def mask_kernel(lists_ref, counts_ref, _, mask_ref):
    member, team = place()
    for h in range(HEADS):
        head = member * HEADS + h
        for b in range(TEAM):
            block = team * TEAM + b
            used = counts_ref[block, head]
            live = jnp.int32(0)
            for t in range(TILES):
                offset = lists_ref[t, block, head] - block + REACH
                live = live | jnp.where(t < used, jnp.left_shift(1, offset), 0)
            for t in range(TILES):
                value = jnp.where((live >> t) & 1 == 1, 0.0, -jnp.inf)
                row = (h * TEAM + b) * TILES + t
                mask_ref[row : row + 1, :] = jnp.full((1, BLK), value, jnp.float32)


def make_mask(lists, counts, after):
    shape = jax.ShapeDtypeStruct((HEADS * TEAM * TILES, BLK), jnp.float32)
    return call(mask_kernel, "mask", [shape], [lists, counts, after], [SMEM, SMEM, ANY])[0]


def compute_kernel(c, mask_ref, *refs):
    first, count = spans()[c]
    kv_refs, qg_refs, (near_ref, far_ref) = refs[:TEAM], refs[TEAM : 2 * TEAM], refs[2 * TEAM : 2 * TEAM + 2]
    if c == 0:
        own_ref, a_ref, b_ref, term_ref, adapt, kw, vw, qs, gs, pm, dm = refs[2 * TEAM + 2 :]
    else:
        adapt, own_ref, a_ref, b_ref, term_ref, kw, vw, qs, gs, pm, dm = refs[2 * TEAM + 2 :]
    kind = adapt.dtype
    member, team = place()
    even = lax.rem(team, 2) == 0
    kv, qg, halo, places = [], [], [], []
    for j in range(TEAM):
        span = (0, HEADS) if j < 2 else (first, count)
        kv.append(Tiles(kv_refs[j], span))
        qg.append(Tiles(qg_refs[j], span))
        halo.append(Tiles(near_ref if j < 2 else far_ref, (first, count), j % 2))
        owner = jnp.bitwise_xor(member, j)
        places.append((owner, owner + REACH, lax.rem(owner + REACH + TEAM, WINDOW)))

    if c == 0:
        for j, (_, near, far) in enumerate(places):
            adapt[:, rows(near, 1)] = kv[j].tile(0, 2)
            adapt[:, rows(far, 1)] = halo[j].tile(0, 2)

    zero = jnp.zeros((BLK, BLK), kind)
    for index in range(count * 2):
        for matrix in (pm, dm):
            matrix[index, rows(TILES, 1), :BLK] = zero
            matrix[index, rows(0, 1), BLK:] = zero

    on_last = (((1,), (1,)), ((), ()))

    def product(left, right, dims=(((1,), (0,)), ((), ()))):
        return lax.dot_general(left, right, dims, preferred_element_type=jnp.float32)

    def load(h):
        head = first + h
        for j, (owner, near, far) in enumerate(places):
            kw[h, rows(near, 1), :] = kv[j].tile(head, 0)
            vw[h, rows(near, 1), :] = kv[j].tile(head, 1)
            kw[h, rows(far, 1), :] = halo[j].tile(head, 0)
            vw[h, rows(far, 1), :] = halo[j].tile(head, 1)
            qs[h, rows(owner, 1), :] = qg[j].tile(head, 0)
            gs[h, rows(owner, 1), :] = qg[j].tile(head, 1)

    def scored(h, pair):
        span, two = rows(2 * pair, TILES + 1), rows(2 * pair, 2)
        return product(kw[h, span, :], qs[h, two, :], on_last), product(vw[h, span, :], gs[h, two, :], on_last)

    def soften(h, pair, scores, dprobs):
        index = h * 2 + pair
        for u in range(2):
            base = ((first + h) * TEAM + 2 * pair + u) * TILES
            masks = [mask_ref[base + t : base + t + 1, :] for t in range(TILES)]
            lanes = slice(u * BLK, (u + 1) * BLK)
            tiles = [slice((u + t) * BLK, (u + t + 1) * BLK) for t in range(TILES)]
            top = jnp.full((1, BLK), -jnp.inf, jnp.float32)
            for mask, tile in zip(masks, tiles):
                top = jnp.maximum(top, jnp.max(scores[tile, lanes], axis=0, keepdims=True) + mask)
            top = top * (SCALING * LOG2E)
            weights = []
            for mask, tile in zip(masks, tiles):
                weights.append(jnp.exp2(scores[tile, lanes] * (SCALING * LOG2E) - (top - mask)))
            total = sum(jnp.sum(weight, axis=0, keepdims=True) for weight in weights)
            mixed = sum(
                jnp.sum(weight * dprobs[tile, lanes], axis=0, keepdims=True) for weight, tile in zip(weights, tiles)
            )
            inverse = 1.0 / total
            delta = mixed * inverse
            for weight, tile in zip(weights, tiles):
                probs = weight * inverse
                pm[index, tile, lanes] = probs.astype(kind)
                dm[index, tile, lanes] = (probs * (dprobs[tile, lanes] - delta)).astype(kind)

    def spread(h, pair):
        index, two = h * 2 + pair, rows(2 * pair, 2)
        return product(dm[index], qs[h, two, :]) * SCALING, product(pm[index], gs[h, two, :])

    def finish(h, adds):
        split, edge = TEAM * BLK, REACH * BLK
        for part, column, half in ((0, cols(h, 1), 0), (1, cols(count + h, 1), RANK)):
            low, high = adds[0][part], adds[1][part]
            middle = low[edge:] + high[:split]
            lower, upper = low[:edge].astype(kind), high[split:].astype(kind)
            own_ref[:, column] = middle
            a_ref[:, column] = jnp.where(even, upper, lower)
            b_ref[:, column] = jnp.where(even, lower, upper)
            window = jnp.concatenate([lower, middle.astype(kind), upper], axis=0)
            term_ref[half : half + RANK, cols(h, 1)] = product(adapt[half : half + RANK, :], window)

    items = [(h, pair) for h in range(count) for pair in range(TEAM // 2)]
    for h in range(count):
        load(h)
    waiting, adds = scored(*items[0]), []
    for index, item in enumerate(items):
        current = waiting
        if index + 1 < len(items):
            waiting = scored(*items[index + 1])
        soften(*item, *current)
        adds.append(spread(*item))
        if len(adds) == TEAM // 2:
            finish(item[0], adds)
            adds = []


def compute(c, mask, kv, qg, near, far, adapt):
    count = CHUNKS[c]
    kind = near.dtype
    width = 2 * count * HEAD_WIDTH
    tall, team = WINDOW * BLK, TEAM * BLK
    out_shape = [
        jax.ShapeDtypeStruct((team, width), jnp.float32),
        jax.ShapeDtypeStruct((REACH * BLK, width), kind),
        jax.ShapeDtypeStruct((REACH * BLK, width), kind),
        jax.ShapeDtypeStruct((2 * RANK, count * HEAD_WIDTH), jnp.float32),
    ]
    inputs = [mask, *kv, *qg, near, far]
    if c == 0:
        out_shape.append(jax.ShapeDtypeStruct((2 * RANK, tall), kind))
    else:
        inputs.append(adapt)
    scratch = [
        pltpu.VMEM((count, tall, HEAD_WIDTH), kind),
        pltpu.VMEM((count, tall, HEAD_WIDTH), kind),
        pltpu.VMEM((count, team, HEAD_WIDTH), kind),
        pltpu.VMEM((count, team, HEAD_WIDTH), kind),
        pltpu.VMEM((count * 2, (TILES + 1) * BLK, 2 * BLK), kind),
        pltpu.VMEM((count * 2, (TILES + 1) * BLK, 2 * BLK), kind),
    ]
    return call(
        functools.partial(compute_kernel, c), f"gradients_{c}", out_shape, inputs, scratch=scratch, vmem=16
    )


def combine_kernel(earlier, own_ref, a_ref, b_ref, *refs):
    outs = refs[-TEAM:]
    member, team = place()
    even = lax.rem(team, 2)
    width = own_ref.shape[1]
    start = outs[1].shape[1] - width
    for index in range(earlier):
        ref = refs[index]
        before = sum(refs[i].shape[1] for i in range(index))
        outs[1][:, before : before + ref.shape[1]] = ref[...]
    for k in range(TEAM):
        owner = jnp.bitwise_xor(member, k)
        row = rows(lax.rem(owner, 2), 1)
        from_a = owner // 2 != even
        column = slice(start, start + width) if k == 1 else slice(None)

        def add(part_ref, out=outs[k], owner=owner, row=row, column=column):
            part = part_ref[row, :].astype(jnp.float32)
            out[:, column] = (own_ref[rows(owner, 1), :] + part).astype(out.dtype)

        pl.when(from_a)(functools.partial(add, a_ref))
        pl.when(jnp.logical_not(from_a))(functools.partial(add, b_ref))


def combine(c, own, a, b, earlier, after):
    block = jax.ShapeDtypeStruct((BLK, own.shape[1]), a.dtype)
    wide = jax.ShapeDtypeStruct((BLK, own.shape[1] + sum(x.shape[1] for x in earlier)), a.dtype)
    specs = [VMEM] * (3 + len(earlier)) + [ANY] * len(after)
    kernel = functools.partial(combine_kernel, len(earlier))
    inputs = [own, a, b, *earlier, *after]
    return call(kernel, f"combine_{c}", [block, wide, block, block], inputs, specs)


def unpack_kernel(*refs):
    outs, other, blocks = refs[-2:], refs[-3], refs[:-3]
    member, _ = place()
    before = 0
    for c, (first, count) in enumerate(spans()):
        sources = [(0, blocks[3 * c], 0), (1, other, before), (2, blocks[3 * c + 1], 0), (3, blocks[3 * c + 2], 0)]
        for k, ref, column in sources:
            head = jnp.bitwise_xor(member, k) * HEADS + first
            for part, out in enumerate(outs):
                out[0, :, cols(head, count)] = ref[:, cols(column + part * count, count)]
        before += 2 * count


def unpack(home, other):
    flat = [block for chunk in home for block in chunk] + [other]
    shape = jax.ShapeDtypeStruct((1, BLK, HEAD_COUNT * HEAD_WIDTH), other.dtype)
    return call(unpack_kernel, "unpack", [shape, shape], flat)


def bit_value(axis, bit, unit):
    return lax.rem(lax.axis_index(axis) // (bit * unit), 2)


def pieces_kernel(bit, *refs):
    terms = refs[: len(CHUNKS)]
    keep_ref, send_ref, whole = refs[len(CHUNKS) :]
    for (first, count), term in zip(spans(), terms):
        whole[:, cols(first, count)] = term[...]
    upper = bit_value(*bit) == 1
    half = whole.shape[1] // 2
    low, high = whole[:, :half], whole[:, half:]
    keep_ref[...] = jnp.where(upper, high, low)
    send_ref[...] = jnp.where(upper, low, high)


def fold_kernel(bit, held_ref, got_ref, *refs):
    keep_ref, send_ref = refs[-2:]
    half, width = keep_ref.shape[0], keep_ref.shape[2]
    value = bit_value(*bit)
    if len(held_ref.shape) == 2:
        total = held_ref[...] + got_ref[...]
        for j in range(half):
            low = total[:, j * width : (j + 1) * width]
            high = total[:, (half + j) * width : (half + j + 1) * width]
            keep_ref[j] = jnp.where(value == 1, high, low)
            send_ref[j] = jnp.where(value == 1, low, high)
    else:
        for out, first in ((keep_ref, value * half), (send_ref, (1 - value) * half)):
            out[...] = held_ref[pl.ds(first, half)] + got_ref[pl.ds(first, half)]


def final_kernel(first_ref, second_ref, key_ref, value_ref):
    key_ref[...] = first_ref[0, :RANK, :] + second_ref[0, :RANK, :]
    value_ref[...] = first_ref[0, RANK:, :] + second_ref[0, RANK:, :]


class Reduction:
    def __init__(self, terms):
        self.clips, seq = lax.axis_size("dp"), lax.axis_size("seq")
        self.teams = seq // TEAM
        self.pieces = self.clips * self.teams
        self.rounds = [("dp", self.clips >> s, 1) for s in range(1, self.clips.bit_length())]
        self.rounds += [("seq", self.teams >> s, TEAM) for s in range(1, self.teams.bit_length())]
        self.width = HEADS * HEAD_WIDTH // self.pieces
        shape = jax.ShapeDtypeStruct((2 * RANK, HEADS * HEAD_WIDTH // 2), jnp.float32)
        scratch = [pltpu.VMEM((2 * RANK, HEADS * HEAD_WIDTH), jnp.float32)]
        kernel = functools.partial(pieces_kernel, self.rounds[0])
        self.held, self.sent = call(kernel, "pieces", [shape, shape], terms, scratch=scratch)
        self.index = 0

    def step(self, after=()):
        index = self.index
        axis, bit, unit = self.rounds[index]
        route = [(i, i ^ (bit * unit)) for i in range(lax.axis_size(axis))]
        got = lax.ppermute(self.sent, axis, route)
        shape = jax.ShapeDtypeStruct((self.pieces >> (index + 2), 2 * RANK, self.width), jnp.float32)
        specs = [VMEM] * 2 + [ANY] * len(after)
        kernel = functools.partial(fold_kernel, self.rounds[index + 1])
        inputs = [self.held, got, *after]
        self.held, self.sent = call(kernel, f"fold_{index}", [shape, shape], inputs, specs)
        self.index += 1

    def finish(self):
        arrived = []
        for flip, piece in enumerate((self.held, self.sent)):
            route = []
            for clip in range(self.clips):
                for position in range(self.teams * TEAM):
                    index = (clip * self.teams + position // TEAM) ^ flip
                    source = clip * self.teams * TEAM + position
                    route.append((source, position % TEAM * self.pieces + index))
            arrived.append(lax.ppermute(piece, ("dp", "seq"), route))
        shape = jax.ShapeDtypeStruct((RANK, self.width), jnp.float32)
        return call(final_kernel, "final", [shape, shape], arrived)


def body(
    head_queries,
    head_keys,
    head_values,
    output_gradient,
    key_adapter_input,
    value_adapter_input,
    key_block_lists,
    live_block_counts,
):
    seq = lax.axis_size("seq")
    teams = seq // TEAM

    def partner(block, k):
        return lax.ppermute(block, "seq", [(i, i ^ k) for i in range(seq)]) if k else block

    near_route = []
    for p in range(seq):
        t = p // TEAM + (1 if p % TEAM >= TEAM // 2 else -1)
        if 0 <= t < teams:
            near_route.append((p, t * TEAM + p % TEAM))
    far_route = [(target, source) for source, target in near_route]
    swaps = []
    for start in (0, 1):
        pairs = []
        for t in range(start, teams - 1, 2):
            for m in range(TEAM):
                pairs += [(t * TEAM + m, (t + 1) * TEAM + m), ((t + 1) * TEAM + m, t * TEAM + m)]
        swaps.append(pairs)

    lists = key_block_lists.transpose(2, 1, 0)
    counts = live_block_counts.T
    adapters = (key_adapter_input.transpose(0, 2, 1), value_adapter_input.transpose(0, 2, 1))
    def spread(packed):
        own, other, across, diagonal = packed
        return [own, partner(other, 1), [partner(x, 2) for x in across], [partner(x, 3) for x in diagonal]]

    kv_out = pack(head_keys, head_values, adapters)
    kv = spread(kv_out)
    qg_out = pack(head_queries, output_gradient, after=kv_out[:1])
    qg = spread(qg_out)
    mask = make_mask(lists, counts, kv_out[0])
    near, far = [], []
    for c, span in enumerate(spans()):
        near.append(lax.ppermute(stack(kv[0], kv[1], f"near_{c}", span, [mask, qg[1]]), "seq", near_route))
        far.append(lax.ppermute(stack(kv[2][c], kv[3][c], f"far_{c}"), "seq", far_route))

    adapt, parts, terms = None, [], []
    for c in range(len(CHUNKS)):
        kv_c, qg_c = ([x[0], x[1], x[2][c], x[3][c]] for x in (kv, qg))
        own, to_a, to_b, term, *more = compute(c, mask, kv_c, qg_c, near[c], far[c], adapt)
        adapt = more[0] if more else adapt
        terms.append(term)
        parts.append((own, lax.ppermute(to_a, "seq", swaps[0]), lax.ppermute(to_b, "seq", swaps[1])))
    reduction = Reduction(terms)
    home, others, after = [], [], []
    for c, part in enumerate(parts):
        last = c + 1 == len(CHUNKS)
        blocks = combine(c, *part, others if last else [], after)
        others.append(blocks[1])
        home.append([blocks[0], partner(blocks[2], 2), partner(blocks[3], 3)])
        after = home[-1][1:]
        for _ in range(2):
            if not last and reduction.index + 1 < len(reduction.rounds):
                reduction.step(blocks[:1])
                after.append(reduction.held)
    while reduction.index + 1 < len(reduction.rounds):
        reduction.step()
    key_term, value_term = reduction.finish()
    key_gradient, value_gradient = unpack(home, partner(others[-1], 1))
    return key_gradient, value_gradient, key_term.T, value_term.T


def solution(mesh):
    tokens = P("dp", "seq", None)
    shares = P(("dp", "seq"), None)
    return jax.shard_map(
        body,
        mesh=mesh,
        in_specs=(tokens,) * 6 + (P(), P()),
        out_specs=(tokens, tokens, shares, shares),
        check_vma=False,
    )
```

```python
import functools

import jax
import jax.numpy as jnp
from jax import lax
from jax.experimental import pallas as pl
from jax.experimental.pallas import tpu as pltpu
from jax.sharding import PartitionSpec as P

HEAD_COUNT = 24
HEAD_WIDTH = 128
BLK = 128
REACH = 2
TILES = 5
RANK = 64
TEAM = 4
HEADS = HEAD_COUNT // TEAM
CHUNKS = (3, 3)
LOADS = 4
WINDOW = TEAM + 2 * REACH
SCALING = HEAD_WIDTH**-0.5
LOG2E = 1.4426950408889634
ANY = pl.BlockSpec(memory_space=pl.ANY)
PACK_VMEM = 56
VMEM = pl.BlockSpec(memory_space=pltpu.VMEM)
SMEM = pl.BlockSpec(memory_space=pltpu.SMEM)
MARK = jax.ShapeDtypeStruct((8, HEAD_WIDTH), jnp.float32)


def call(kernel, name, out_shape, inputs, in_specs=None, scratch=(), vmem=4):
    return pl.pallas_call(
        kernel,
        out_shape=out_shape,
        in_specs=in_specs or [VMEM] * len(inputs),
        out_specs=[VMEM] * len(out_shape),
        scratch_shapes=list(scratch),
        compiler_params=pltpu.CompilerParams(vmem_limit_bytes=vmem << 20),
        cost_estimate=pl.CostEstimate(flops=1, bytes_accessed=1, transcendentals=0),
        name=name,
    )(*inputs)


def cols(first, count):
    if not isinstance(first, int):
        first = pl.multiple_of(first * HEAD_WIDTH, HEAD_WIDTH)
    else:
        first = first * HEAD_WIDTH
    return pl.ds(first, count * HEAD_WIDTH)


def rows(first, count):
    if not isinstance(first, int):
        first = pl.multiple_of(first * BLK, BLK)
    else:
        first = first * BLK
    return pl.ds(first, count * BLK)


def place():
    position = lax.axis_index("seq")
    return lax.rem(position, TEAM), position // TEAM


def spans():
    return [(sum(CHUNKS[:c]), count) for c, count in enumerate(CHUNKS)]


SIDE, OWN, ACROSS = (1, 3), (0,), (2,)


def pack_plan(kinds, adapters):
    return [(span, owners, bool(adapters) and span[0] == 0) for span in spans() for owners in kinds]


def fill(plan, a_ref, b_ref, outs, part):
    member, _ = place()
    for ((first, count), owners, _), out in zip(plan, outs):
        for index, k in enumerate(owners):
            head = jnp.bitwise_xor(member, k) * HEADS + first
            out[part, cols(2 * index * count, count)] = a_ref[part, cols(head, count)]
            out[part, cols((2 * index + 1) * count, count)] = b_ref[part, cols(head, count)]


def fill_adapters(plan, key_tile, value_tile, outs):
    for (_, _, adapted), out in zip(plan, outs):
        if adapted:
            column = cols(out.shape[1] // HEAD_WIDTH - 1, 1)
            out[:RANK, column] = key_tile
            out[RANK:, column] = value_tile


def pack_first_kernel(plan, keys, values, key_in, value_in, *refs):
    outs, (mark, tall, small, sems) = refs[:-4], refs[-4:]
    mark[...] = jnp.zeros_like(mark)
    size = BLK // LOADS
    copies = []
    for part in range(LOADS):
        for index, source in enumerate((keys, values)):
            piece = pl.ds(part * size, size)
            copies.append((source.at[0, piece, :], tall.at[index, piece, :]))
    copies += [(key_in.at[0], small.at[0]), (value_in.at[0], small.at[1])]
    copies = [pltpu.make_async_copy(*pair, sems.at[i]) for i, pair in enumerate(copies)]
    for copy in copies:
        copy.start()
    for part in range(LOADS):
        for copy in copies[2 * part : 2 * part + 2]:
            copy.wait()
        fill(plan, tall.at[0], tall.at[1], outs, pl.ds(part * size, size))
    for copy in copies[2 * LOADS :]:
        copy.wait()
    fill_adapters(plan, small[0], small[1], outs)


def pack_kernel(plan, adapters, a_ref, b_ref, *refs):
    outs = refs[-len(plan) :]
    fill(plan, a_ref.at[0], b_ref.at[0], outs, slice(None))
    if adapters:
        fill_adapters(plan, refs[0][0], refs[1][0], outs)


def pack(name, kinds, first, second, adapters=(), after=(), at_once=False):
    plan = pack_plan(kinds, adapters)
    kind = first.dtype
    out_shape = [
        jax.ShapeDtypeStruct((BLK, (2 * count * len(owners) + adapted) * HEAD_WIDTH), kind)
        for (_, count), owners, adapted in plan
    ]
    inputs = [first, second, *adapters, *after]
    if at_once:
        scratch = [
            pltpu.VMEM((2, BLK, HEAD_COUNT * HEAD_WIDTH), kind),
            pltpu.VMEM((2, RANK, BLK), kind),
            pltpu.SemaphoreType.DMA((2 * LOADS + 2,)),
        ]
        kernel = functools.partial(pack_first_kernel, plan)
        out_shape.append(MARK)
        outs = call(kernel, name, out_shape, inputs, [ANY] * 4, scratch, PACK_VMEM)
    else:
        kernel = functools.partial(pack_kernel, plan, bool(adapters))
        specs = [VMEM] * (2 + len(adapters)) + [ANY] * len(after)
        outs = call(kernel, name, out_shape, inputs, specs)
    return [outs[len(kinds) * c : len(kinds) * (c + 1)] for c in range(len(CHUNKS))], outs[-1]


def route_kernel(mine_ref, across_ref, got_ref, *refs):
    chip_ref, send_ref = refs[-2:]
    half, extra = 2 * HEAD_WIDTH, mine_ref.shape[1] % (2 * HEAD_WIDTH)
    half = mine_ref.shape[1] - extra
    chip_ref[rows(0, 1), :] = mine_ref[...]
    chip_ref[rows(1, 1), :half] = got_ref[:, :half]
    send_ref[rows(0, 1), :] = across_ref[...]
    send_ref[rows(1, 1), :half] = got_ref[:, half : 2 * half]
    if extra:
        for out in (chip_ref, send_ref):
            out[rows(1, 1), half:] = got_ref[:, 2 * half :]


def route(name, mine, across, got, after=()):
    shape = jax.ShapeDtypeStruct((2 * BLK, mine.shape[1]), mine.dtype)
    specs = [VMEM] * 3 + [ANY] * len(after)
    return call(route_kernel, name, [shape, shape], [mine, across, got, *after], specs)


def mask_kernel(lists_ref, counts_ref, _, mask_ref):
    member, team = place()
    for h in range(HEADS):
        head = member * HEADS + h
        for b in range(TEAM):
            block = team * TEAM + b
            used = counts_ref[block, head]
            live = jnp.int32(0)
            for t in range(TILES):
                offset = lists_ref[t, block, head] - block + REACH
                live = live | jnp.where(t < used, jnp.left_shift(1, offset), 0)
            for t in range(TILES):
                value = jnp.where((live >> t) & 1 == 1, 0.0, -jnp.inf)
                row = (h * TEAM + b) * TILES + t
                mask_ref[row : row + 1, :] = jnp.full((1, BLK), value, jnp.float32)


def make_mask(lists, counts, after):
    shape = jax.ShapeDtypeStruct((HEADS * TEAM * TILES, BLK), jnp.float32)
    return call(mask_kernel, "mask", [shape], [lists, counts, after], [SMEM, SMEM, ANY])[0]


def compute_kernel(c, mask_ref, *refs):
    first, count = spans()[c]
    kv, halo, qg = refs[:2], refs[2:4], refs[4:6]
    if c == 0:
        own_ref, a_ref, b_ref, term_ref, adapt, kw, vw, qs, gs, pm, dm = refs[6:]
    else:
        adapt, own_ref, a_ref, b_ref, term_ref, kw, vw, qs, gs, pm, dm = refs[6:]
    kind = adapt.dtype
    member, team = place()
    even = lax.rem(team, 2) == 0
    places = []
    for j in range(TEAM):
        owner = jnp.bitwise_xor(member, j)
        places.append((owner, owner + REACH, lax.rem(owner + REACH + TEAM, WINDOW)))

    def tile(refs, j, h, part):
        return refs[j // 2][rows(j % 2, 1), cols(part * count + h, 1)]

    if c == 0:
        for j, (_, near, far) in enumerate(places):
            adapt[:, rows(near, 1)] = tile(kv, j, 0, 2)
            adapt[:, rows(far, 1)] = tile(halo, j, 0, 2)

    zero = jnp.zeros((BLK, BLK), kind)
    for index in range(count * 2):
        for matrix in (pm, dm):
            matrix[index, rows(TILES, 1), :BLK] = zero
            matrix[index, rows(0, 1), BLK:] = zero

    on_last = (((1,), (1,)), ((), ()))

    def product(left, right, dims=(((1,), (0,)), ((), ()))):
        return lax.dot_general(left, right, dims, preferred_element_type=jnp.float32)

    def load(h):
        for j, (owner, near, far) in enumerate(places):
            kw[h, rows(near, 1), :] = tile(kv, j, h, 0)
            vw[h, rows(near, 1), :] = tile(kv, j, h, 1)
            kw[h, rows(far, 1), :] = tile(halo, j, h, 0)
            vw[h, rows(far, 1), :] = tile(halo, j, h, 1)
            qs[h, rows(owner, 1), :] = tile(qg, j, h, 0)
            gs[h, rows(owner, 1), :] = tile(qg, j, h, 1)

    def scored(h, pair):
        span, two = rows(2 * pair, TILES + 1), rows(2 * pair, 2)
        return product(kw[h, span, :], qs[h, two, :], on_last), product(vw[h, span, :], gs[h, two, :], on_last)

    def soften(h, pair, scores, dprobs):
        index = h * 2 + pair
        for u in range(2):
            base = ((first + h) * TEAM + 2 * pair + u) * TILES
            masks = [mask_ref[base + t : base + t + 1, :] for t in range(TILES)]
            lanes = slice(u * BLK, (u + 1) * BLK)
            tiles = [slice((u + t) * BLK, (u + t + 1) * BLK) for t in range(TILES)]
            top = jnp.full((1, BLK), -jnp.inf, jnp.float32)
            for mask, tile in zip(masks, tiles):
                top = jnp.maximum(top, jnp.max(scores[tile, lanes], axis=0, keepdims=True) + mask)
            top = top * (SCALING * LOG2E)
            weights = []
            for mask, tile in zip(masks, tiles):
                weights.append(jnp.exp2(scores[tile, lanes] * (SCALING * LOG2E) - (top - mask)))
            total = sum(jnp.sum(weight, axis=0, keepdims=True) for weight in weights)
            mixed = sum(
                jnp.sum(weight * dprobs[tile, lanes], axis=0, keepdims=True) for weight, tile in zip(weights, tiles)
            )
            inverse = 1.0 / total
            delta = mixed * inverse
            for weight, tile in zip(weights, tiles):
                probs = weight * inverse
                pm[index, tile, lanes] = probs.astype(kind)
                dm[index, tile, lanes] = (probs * (dprobs[tile, lanes] - delta)).astype(kind)

    def spread(h, pair):
        index, two = h * 2 + pair, rows(2 * pair, 2)
        return product(dm[index], qs[h, two, :]) * SCALING, product(pm[index], gs[h, two, :])

    def finish(h, adds):
        split, edge = TEAM * BLK, REACH * BLK
        for part, column, half in ((0, cols(h, 1), 0), (1, cols(count + h, 1), RANK)):
            low, high = adds[0][part], adds[1][part]
            middle = low[edge:] + high[:split]
            lower, upper = low[:edge].astype(kind), high[split:].astype(kind)
            own_ref[:, column] = middle
            a_ref[:, column] = jnp.where(even, upper, lower)
            b_ref[:, column] = jnp.where(even, lower, upper)
            window = jnp.concatenate([lower, middle.astype(kind), upper], axis=0)
            term_ref[half : half + RANK, cols(h, 1)] = product(adapt[half : half + RANK, :], window)

    items = [(h, pair) for h in range(count) for pair in range(TEAM // 2)]
    for h in range(count):
        load(h)
    waiting, adds = scored(*items[0]), []
    for index, item in enumerate(items):
        current = waiting
        if index + 1 < len(items):
            waiting = scored(*items[index + 1])
        soften(*item, *current)
        adds.append(spread(*item))
        if len(adds) == TEAM // 2:
            finish(item[0], adds)
            adds = []


def compute(c, mask, kv, halo, qg, adapt):
    count = CHUNKS[c]
    kind = kv[0].dtype
    width = 2 * count * HEAD_WIDTH
    tall, team = WINDOW * BLK, TEAM * BLK
    out_shape = [
        jax.ShapeDtypeStruct((team, width), jnp.float32),
        jax.ShapeDtypeStruct((REACH * BLK, width), kind),
        jax.ShapeDtypeStruct((REACH * BLK, width), kind),
        jax.ShapeDtypeStruct((2 * RANK, count * HEAD_WIDTH), jnp.float32),
    ]
    inputs = [mask, *kv, *halo, *qg]
    if c == 0:
        out_shape.append(jax.ShapeDtypeStruct((2 * RANK, tall), kind))
    else:
        inputs.append(adapt)
    scratch = [
        pltpu.VMEM((count, tall, HEAD_WIDTH), kind),
        pltpu.VMEM((count, tall, HEAD_WIDTH), kind),
        pltpu.VMEM((count, team, HEAD_WIDTH), kind),
        pltpu.VMEM((count, team, HEAD_WIDTH), kind),
        pltpu.VMEM((count * 2, (TILES + 1) * BLK, 2 * BLK), kind),
        pltpu.VMEM((count * 2, (TILES + 1) * BLK, 2 * BLK), kind),
    ]
    return call(
        functools.partial(compute_kernel, c), f"gradients_{c}", out_shape, inputs, scratch=scratch, vmem=16
    )


def combine_kernel(earlier, own_ref, a_ref, b_ref, *refs):
    outs = refs[-TEAM:]
    member, team = place()
    even = lax.rem(team, 2)
    width = own_ref.shape[1]
    start = outs[1].shape[1] - width
    for index in range(earlier):
        ref = refs[index]
        before = sum(refs[i].shape[1] for i in range(index))
        outs[1][:, before : before + ref.shape[1]] = ref[...]
    for k in range(TEAM):
        owner = jnp.bitwise_xor(member, k)
        row = rows(lax.rem(owner, 2), 1)
        from_a = owner // 2 != even
        column = slice(start, start + width) if k == 1 else slice(None)

        def add(part_ref, out=outs[k], owner=owner, row=row, column=column):
            part = part_ref[row, :].astype(jnp.float32)
            out[:, column] = (own_ref[rows(owner, 1), :] + part).astype(out.dtype)

        pl.when(from_a)(functools.partial(add, a_ref))
        pl.when(jnp.logical_not(from_a))(functools.partial(add, b_ref))


def combine(c, own, a, b, earlier, after):
    block = jax.ShapeDtypeStruct((BLK, own.shape[1]), a.dtype)
    wide = jax.ShapeDtypeStruct((BLK, own.shape[1] + sum(x.shape[1] for x in earlier)), a.dtype)
    specs = [VMEM] * (3 + len(earlier)) + [ANY] * len(after)
    kernel = functools.partial(combine_kernel, len(earlier))
    inputs = [own, a, b, *earlier, *after]
    return call(kernel, f"combine_{c}", [block, wide, block, block], inputs, specs)


def unpack_kernel(*refs):
    outs, other, blocks = refs[-3:-1], refs[-4], refs[:-4]
    refs[-1][...] = jnp.zeros_like(refs[-1])
    member, _ = place()
    before = 0
    for c, (first, count) in enumerate(spans()):
        sources = [(0, blocks[3 * c], 0), (1, other, before), (2, blocks[3 * c + 1], 0), (3, blocks[3 * c + 2], 0)]
        for k, ref, column in sources:
            head = jnp.bitwise_xor(member, k) * HEADS + first
            for part, out in enumerate(outs):
                out[0, :, cols(head, count)] = ref[:, cols(column + part * count, count)]
        before += 2 * count


def unpack(home, other):
    flat = [block for chunk in home for block in chunk] + [other]
    shape = jax.ShapeDtypeStruct((1, BLK, HEAD_COUNT * HEAD_WIDTH), other.dtype)
    return call(unpack_kernel, "unpack", [shape, shape, MARK], flat)


def bit_value(axis, bit, unit):
    return lax.rem(lax.axis_index(axis) // (bit * unit), 2)


def pieces_kernel(bit, *refs):
    terms = refs[: len(CHUNKS)]
    keep_ref, send_ref, whole = refs[len(CHUNKS) :]
    for (first, count), term in zip(spans(), terms):
        whole[:, cols(first, count)] = term[...]
    upper = bit_value(*bit) == 1
    half = whole.shape[1] // 2
    low, high = whole[:, :half], whole[:, half:]
    keep_ref[...] = jnp.where(upper, high, low)
    send_ref[...] = jnp.where(upper, low, high)


def fold_kernel(bit, held_ref, got_ref, *refs):
    keep_ref, send_ref = refs[-2:]
    half, width = keep_ref.shape[0], keep_ref.shape[2]
    value = bit_value(*bit)
    if len(held_ref.shape) == 2:
        total = held_ref[...] + got_ref[...]
        for j in range(half):
            low = total[:, j * width : (j + 1) * width]
            high = total[:, (half + j) * width : (half + j + 1) * width]
            keep_ref[j] = jnp.where(value == 1, high, low)
            send_ref[j] = jnp.where(value == 1, low, high)
    else:
        for out, first in ((keep_ref, value * half), (send_ref, (1 - value) * half)):
            out[...] = held_ref[pl.ds(first, half)] + got_ref[pl.ds(first, half)]


def final_kernel(first_ref, second_ref, _, key_ref, value_ref):
    key_ref[...] = first_ref[0, :RANK, :] + second_ref[0, :RANK, :]
    value_ref[...] = first_ref[0, RANK:, :] + second_ref[0, RANK:, :]


class Reduction:
    def __init__(self, terms):
        self.clips, seq = lax.axis_size("dp"), lax.axis_size("seq")
        self.teams = seq // TEAM
        self.pieces = self.clips * self.teams
        self.rounds = [("dp", self.clips >> s, 1) for s in range(1, self.clips.bit_length())]
        self.rounds += [("seq", self.teams >> s, TEAM) for s in range(1, self.teams.bit_length())]
        self.width = HEADS * HEAD_WIDTH // self.pieces
        shape = jax.ShapeDtypeStruct((2 * RANK, HEADS * HEAD_WIDTH // 2), jnp.float32)
        scratch = [pltpu.VMEM((2 * RANK, HEADS * HEAD_WIDTH), jnp.float32)]
        kernel = functools.partial(pieces_kernel, self.rounds[0])
        self.held, self.sent = call(kernel, "pieces", [shape, shape], terms, scratch=scratch)
        self.index = 0

    def step(self, after=()):
        index = self.index
        axis, bit, unit = self.rounds[index]
        route = [(i, i ^ (bit * unit)) for i in range(lax.axis_size(axis))]
        got = lax.ppermute(self.sent, axis, route)
        shape = jax.ShapeDtypeStruct((self.pieces >> (index + 2), 2 * RANK, self.width), jnp.float32)
        specs = [VMEM] * 2 + [ANY] * len(after)
        kernel = functools.partial(fold_kernel, self.rounds[index + 1])
        inputs = [self.held, got, *after]
        self.held, self.sent = call(kernel, f"fold_{index}", [shape, shape], inputs, specs)
        self.index += 1

    def finish(self, after):
        arrived = []
        for flip, piece in enumerate((self.held, self.sent)):
            route = []
            for clip in range(self.clips):
                for position in range(self.teams * TEAM):
                    index = (clip * self.teams + position // TEAM) ^ flip
                    source = clip * self.teams * TEAM + position
                    route.append((source, position % TEAM * self.pieces + index))
            arrived.append(lax.ppermute(piece, ("dp", "seq"), route))
        shape = jax.ShapeDtypeStruct((RANK, self.width), jnp.float32)
        return call(final_kernel, "final", [shape, shape], [*arrived, after], [VMEM, VMEM, ANY])


def body(
    head_queries,
    head_keys,
    head_values,
    output_gradient,
    key_adapter_input,
    value_adapter_input,
    key_block_lists,
    live_block_counts,
):
    seq = lax.axis_size("seq")
    teams = seq // TEAM

    def partner(block, k):
        return lax.ppermute(block, "seq", [(i, i ^ k) for i in range(seq)]) if k else block

    near_route = []
    for p in range(seq):
        t = p // TEAM + (1 if p % TEAM >= TEAM // 2 else -1)
        if 0 <= t < teams:
            near_route.append((p, t * TEAM + p % TEAM))
    far_route = [(target, source) for source, target in near_route]
    swaps = []
    for start in (0, 1):
        pairs = []
        for t in range(start, teams - 1, 2):
            for m in range(TEAM):
                pairs += [(t * TEAM + m, (t + 1) * TEAM + m), ((t + 1) * TEAM + m, t * TEAM + m)]
        swaps.append(pairs)

    lists = key_block_lists.transpose(2, 1, 0)
    counts = live_block_counts.T
    adapters = (key_adapter_input.transpose(0, 2, 1), value_adapter_input.transpose(0, 2, 1))
    sides, mark = pack("pack_side", (SIDE,), head_keys, head_values, adapters, at_once=True)
    kv_side = [partner(side, 1) for (side,) in sides]
    kv_out, _ = pack("pack_kv", (OWN, ACROSS), head_keys, head_values, adapters, [mark])
    mask = make_mask(lists, counts, kv_out[0][0])
    qg_out, _ = pack("pack_qg", (SIDE, OWN, ACROSS), head_queries, output_gradient, after=[mask])
    qg_side = [partner(side, 1) for side, _, _ in qg_out]
    kv, halo, qg = [], [], []
    for c in range(len(CHUNKS)):
        (mine, across), got = kv_out[c], kv_side[c]
        chip, send = route(f"route_kv_{c}", mine, across, got)
        kv.append((chip, partner(send, 2)))
    for c in range(len(CHUNKS)):
        (_, mine, across), got = qg_out[c], qg_side[c]
        chip, send = route(f"route_qg_{c}", mine, across, got, [kv[0][1]])
        qg.append((chip, partner(send, 2)))
        halo.append((lax.ppermute(kv[c][0], "seq", near_route), lax.ppermute(kv[c][1], "seq", far_route)))
    adapt, parts, terms = None, [], []
    for c in range(len(CHUNKS)):
        own, to_a, to_b, term, *more = compute(c, mask, kv[c], halo[c], qg[c], adapt)
        adapt = more[0] if more else adapt
        terms.append(term)
        parts.append((own, lax.ppermute(to_a, "seq", swaps[0]), lax.ppermute(to_b, "seq", swaps[1])))
    reduction = Reduction(terms)
    home, others, after = [], [], []
    for c, part in enumerate(parts):
        last = c + 1 == len(CHUNKS)
        blocks = combine(c, *part, others if last else [], after)
        others.append(blocks[1])
        home.append([blocks[0], partner(blocks[2], 2), partner(blocks[3], 3)])
        after = home[-1][1:]
        for _ in range(2):
            if not last and reduction.index + 1 < len(reduction.rounds):
                reduction.step(blocks[:1])
                after.append(reduction.held)
    while reduction.index + 1 < len(reduction.rounds):
        reduction.step()
    key_gradient, value_gradient, mark = unpack(home, partner(others[-1], 1))
    key_term, value_term = reduction.finish(mark)
    return key_gradient, value_gradient, key_term.T, value_term.T


def solution(mesh):
    tokens = P("dp", "seq", None)
    shares = P(("dp", "seq"), None)
    return jax.shard_map(
        body,
        mesh=mesh,
        in_specs=(tokens,) * 6 + (P(), P()),
        out_specs=(tokens, tokens, shares, shares),
        check_vma=False,
    )
```

```python
import functools

import jax
import jax.numpy as jnp
from jax import lax
from jax.experimental import pallas as pl
from jax.experimental.pallas import tpu as pltpu
from jax.sharding import PartitionSpec as P

HEAD_COUNT = 24
HEAD_WIDTH = 128
BLK = 128
REACH = 2
TILES = 5
RANK = 64
TEAM = 4
HEADS = HEAD_COUNT // TEAM
CHUNKS = (3, 3)
WINDOW = TEAM + 2 * REACH
SCALING = HEAD_WIDTH**-0.5
LOG2E = 1.4426950408889634
ANY = pl.BlockSpec(memory_space=pl.ANY)
PACK_VMEM = 56
VMEM = pl.BlockSpec(memory_space=pltpu.VMEM)
SMEM = pl.BlockSpec(memory_space=pltpu.SMEM)
MARK = jax.ShapeDtypeStruct((8, HEAD_WIDTH), jnp.float32)


def call(kernel, name, out_shape, inputs, in_specs=None, scratch=(), vmem=4):
    return pl.pallas_call(
        kernel,
        out_shape=out_shape,
        in_specs=in_specs or [VMEM] * len(inputs),
        out_specs=[VMEM] * len(out_shape),
        scratch_shapes=list(scratch),
        compiler_params=pltpu.CompilerParams(vmem_limit_bytes=vmem << 20),
        cost_estimate=pl.CostEstimate(flops=1, bytes_accessed=1, transcendentals=0),
        name=name,
    )(*inputs)


def cols(first, count):
    if not isinstance(first, int):
        first = pl.multiple_of(first * HEAD_WIDTH, HEAD_WIDTH)
    else:
        first = first * HEAD_WIDTH
    return pl.ds(first, count * HEAD_WIDTH)


def rows(first, count):
    if not isinstance(first, int):
        first = pl.multiple_of(first * BLK, BLK)
    else:
        first = first * BLK
    return pl.ds(first, count * BLK)


def padded(columns):
    return pl.cdiv(columns, HEAD_WIDTH) * HEAD_WIDTH


def first_head(c, member):
    return (c * TEAM + member) * CHUNKS[c]


def place():
    position = lax.axis_index("seq")
    return lax.rem(position, TEAM), position // TEAM


def spans():
    return [(sum(CHUNKS[:c]), count) for c, count in enumerate(CHUNKS)]


SIDE, OWN, ACROSS = (1, 3), (0,), (2,)


def pack_plan(kinds, adapters):
    return [(span, owners, bool(adapters) and span[0] == 0) for span in spans() for owners in kinds]


def fill(plan, a_ref, b_ref, outs, part):
    member, _ = place()
    for ((first, count), owners, _), out in zip(plan, outs):
        for index, k in enumerate(owners):
            head = first_head(first // count, jnp.bitwise_xor(member, k))
            out[part, cols(2 * index * count, count)] = a_ref[part, cols(head, count)]
            out[part, cols((2 * index + 1) * count, count)] = b_ref[part, cols(head, count)]


def fill_adapters(plan, key_tile, value_tile, outs):
    for (_, _, adapted), out in zip(plan, outs):
        if adapted:
            column = cols(out.shape[1] // HEAD_WIDTH - 1, 1)
            out[:RANK, column] = key_tile
            out[RANK:, column] = value_tile


def pack_first_kernel(plan, keys, values, key_in, value_in, *refs):
    outs, (small, sems) = refs[:-2], refs[-2:]
    member, _ = place()
    copies = [(key_in.at[0], small.at[0]), (value_in.at[0], small.at[1])]
    for ((first, count), owners, _), out in zip(plan, outs):
        for index, k in enumerate(owners):
            head = first_head(first // count, jnp.bitwise_xor(member, k))
            for part, source in enumerate((keys, values)):
                target = out.at[:, cols((2 * index + part) * count, count)]
                copies.append((source.at[0, :, cols(head, count)], target))
    copies = [pltpu.make_async_copy(*pair, sems.at[i]) for i, pair in enumerate(copies)]
    for copy in copies:
        copy.start()
    for copy in copies[:2]:
        copy.wait()
    fill_adapters(plan, small[0], small[1], outs)
    for copy in copies[2:]:
        copy.wait()


def pack_kernel(plan, adapters, a_ref, b_ref, *refs):
    outs = refs[-len(plan) :]
    fill(plan, a_ref.at[0], b_ref.at[0], outs, slice(None))
    if adapters:
        fill_adapters(plan, refs[0][0], refs[1][0], outs)


def pack(name, kinds, first, second, adapters=(), after=(), at_once=False):
    plan = pack_plan(kinds, adapters)
    kind = first.dtype
    out_shape = [
        jax.ShapeDtypeStruct((BLK, (2 * count * len(owners) + adapted) * HEAD_WIDTH), kind)
        for (_, count), owners, adapted in plan
    ]
    inputs = [first, second, *adapters, *after]
    if at_once:
        scratch = [
            pltpu.VMEM((2, RANK, BLK), kind),
            pltpu.SemaphoreType.DMA((2 + sum(2 * len(owners) for _, owners, _ in plan),)),
        ]
        kernel = functools.partial(pack_first_kernel, plan)
        outs = call(kernel, name, out_shape, inputs, [ANY] * 4, scratch, PACK_VMEM)
    else:
        kernel = functools.partial(pack_kernel, plan, bool(adapters))
        specs = [VMEM] * (2 + len(adapters)) + [ANY] * len(after)
        outs = call(kernel, name, out_shape, inputs, specs)
    return [outs[len(kinds) * c : len(kinds) * (c + 1)] for c in range(len(CHUNKS))]


def route_kernel(mine_ref, across_ref, got_ref, *refs):
    chip_ref, send_ref = refs[-2:]
    half, extra = 2 * HEAD_WIDTH, mine_ref.shape[1] % (2 * HEAD_WIDTH)
    half = mine_ref.shape[1] - extra
    chip_ref[rows(0, 1), :] = mine_ref[...]
    chip_ref[rows(1, 1), :half] = got_ref[:, :half]
    send_ref[rows(0, 1), :] = across_ref[...]
    send_ref[rows(1, 1), :half] = got_ref[:, half : 2 * half]
    if extra:
        for out in (chip_ref, send_ref):
            out[rows(1, 1), half:] = got_ref[:, 2 * half :]


def route(name, mine, across, got, after=()):
    shape = jax.ShapeDtypeStruct((2 * BLK, mine.shape[1]), mine.dtype)
    specs = [VMEM] * 3 + [ANY] * len(after)
    return call(route_kernel, name, [shape, shape], [mine, across, got, *after], specs)


def mask_kernel(lists_ref, counts_ref, _, mask_ref):
    member, team = place()
    for h in range(HEADS):
        head = first_head(h // CHUNKS[0], member) + h % CHUNKS[0]
        for b in range(TEAM):
            block = team * TEAM + b
            used = counts_ref[block, head]
            live = jnp.int32(0)
            for t in range(TILES):
                offset = lists_ref[t, block, head] - block + REACH
                live = live | jnp.where(t < used, jnp.left_shift(1, offset), 0)
            for t in range(TILES):
                value = jnp.where((live >> t) & 1 == 1, 0.0, -jnp.inf)
                row = (h * TEAM + b) * TILES + t
                mask_ref[row : row + 1, :] = jnp.full((1, BLK), value, jnp.float32)


def make_mask(lists, counts, after):
    shape = jax.ShapeDtypeStruct((HEADS * TEAM * TILES, BLK), jnp.float32)
    return call(mask_kernel, "mask", [shape], [lists, counts, after], [SMEM, SMEM, ANY])[0]


def compute_kernel(c, mask_ref, *refs):
    first, count = spans()[c]
    kv, halo, qg, rest = refs[:2], refs[2:4], refs[4:6], refs[6:]
    kw, vw, qs, gs, pm, dm, term = rest[-7:]
    if c == 0:
        own_ref, a_ref, b_ref, keep_ref, clip_ref, both_ref, adapt = rest[:-7]
    else:
        adapt, *earlier, own_ref, a_ref, b_ref, keep_ref, clip_ref, both_ref = rest[:-7]
    kind = adapt.dtype
    member, team = place()
    even = lax.rem(team, 2) == 0
    places = []
    for j in range(TEAM):
        owner = jnp.bitwise_xor(member, j)
        places.append((owner, owner + REACH, lax.rem(owner + REACH + TEAM, WINDOW)))

    def tile(refs, j, h, part):
        return refs[j // 2][rows(j % 2, 1), cols(part * count + h, 1)]

    if c == 0:
        for j, (_, near, far) in enumerate(places):
            adapt[:, rows(near, 1)] = tile(kv, j, 0, 2)
            adapt[:, rows(far, 1)] = tile(halo, j, 0, 2)

    zero = jnp.zeros((BLK, BLK), kind)
    for index in range(count * 2):
        for matrix in (pm, dm):
            matrix[index, rows(TILES, 1), :BLK] = zero
            matrix[index, rows(0, 1), BLK:] = zero

    on_last = (((1,), (1,)), ((), ()))

    def product(left, right, dims=(((1,), (0,)), ((), ()))):
        return lax.dot_general(left, right, dims, preferred_element_type=jnp.float32)

    def load(h):
        for j, (owner, near, far) in enumerate(places):
            kw[h, rows(near, 1), :] = tile(kv, j, h, 0)
            vw[h, rows(near, 1), :] = tile(kv, j, h, 1)
            kw[h, rows(far, 1), :] = tile(halo, j, h, 0)
            vw[h, rows(far, 1), :] = tile(halo, j, h, 1)
            qs[h, rows(owner, 1), :] = tile(qg, j, h, 0)
            gs[h, rows(owner, 1), :] = tile(qg, j, h, 1)

    def scored(h, pair):
        span, two = rows(2 * pair, TILES + 1), rows(2 * pair, 2)
        return product(kw[h, span, :], qs[h, two, :], on_last), product(vw[h, span, :], gs[h, two, :], on_last)

    def soften(h, pair, scores, dprobs):
        index = h * 2 + pair
        for u in range(2):
            base = ((first + h) * TEAM + 2 * pair + u) * TILES
            masks = [mask_ref[base + t : base + t + 1, :] for t in range(TILES)]
            lanes = slice(u * BLK, (u + 1) * BLK)
            tiles = [slice((u + t) * BLK, (u + t + 1) * BLK) for t in range(TILES)]
            top = jnp.full((1, BLK), -jnp.inf, jnp.float32)
            for mask, tile in zip(masks, tiles):
                top = jnp.maximum(top, jnp.max(scores[tile, lanes], axis=0, keepdims=True) + mask)
            top = top * (SCALING * LOG2E)
            weights = []
            for mask, tile in zip(masks, tiles):
                weights.append(jnp.exp2(scores[tile, lanes] * (SCALING * LOG2E) - (top - mask)))
            total = sum(jnp.sum(weight, axis=0, keepdims=True) for weight in weights)
            mixed = sum(
                jnp.sum(weight * dprobs[tile, lanes], axis=0, keepdims=True) for weight, tile in zip(weights, tiles)
            )
            inverse = 1.0 / total
            delta = mixed * inverse
            for weight, tile in zip(weights, tiles):
                probs = weight * inverse
                pm[index, tile, lanes] = probs.astype(kind)
                dm[index, tile, lanes] = (probs * (dprobs[tile, lanes] - delta)).astype(kind)

    def spread(h, pair):
        index, two = h * 2 + pair, rows(2 * pair, 2)
        return product(dm[index], qs[h, two, :]) * SCALING, product(pm[index], gs[h, two, :])

    def finish(h, adds):
        split, edge = TEAM * BLK, REACH * BLK
        for part, column, half in ((0, cols(h, 1), 0), (1, cols(count + h, 1), RANK)):
            low, high = adds[0][part], adds[1][part]
            middle = low[edge:] + high[:split]
            lower, upper = low[:edge].astype(kind), high[split:].astype(kind)
            own_ref[:, column] = middle
            a_ref[:, column] = jnp.where(even, upper, lower)
            b_ref[:, column] = jnp.where(even, lower, upper)
            window = jnp.concatenate([lower, middle.astype(kind), upper], axis=0)
            term[half : half + RANK, cols(h, 1)] = product(adapt[half : half + RANK, :], window)

    items = [(h, pair) for h in range(count) for pair in range(TEAM // 2)]
    for h in range(count):
        load(h)
    waiting, adds = scored(*items[0]), []
    for index, item in enumerate(items):
        current = waiting
        if index + 1 < len(items):
            waiting = scored(*items[index + 1])
        soften(*item, *current)
        adds.append(spread(*item))
        if len(adds) == TEAM // 2:
            finish(item[0], adds)
            adds = []
    width = term.shape[1] // 4
    quarters = [term[:, i * width : (i + 1) * width] for i in range(4)]
    upper = bit_value("dp", lax.axis_size("dp") // 2, 1) == 1

    def quarter(other_team, other_clip):
        odd, high = jnp.logical_not(even) ^ other_team, upper ^ other_clip
        return jnp.where(odd, jnp.where(high, *quarters[3:1:-1]), jnp.where(high, *quarters[1::-1]))

    keep_ref[:, :width] = quarter(False, False)
    leave = quarter(True, False)
    whole = leave.astype(kind)
    place_ = pl.ds(2 * count * HEAD_WIDTH, width)
    a_ref[rows(0, 1), place_] = whole
    a_ref[rows(1, 1), place_] = (leave - whole.astype(jnp.float32)).astype(kind)
    for out, part in ((clip_ref, quarter(False, True)), (both_ref, quarter(True, True))):
        if c == 0:
            out[:, :width] = part
        else:
            out[1, :, :width] = part
    if c == 1:
        clip_ref[0] = earlier[0][...]
        both_ref[0] = earlier[1][...]


def compute(c, mask, kv, halo, qg, earlier):
    count = CHUNKS[c]
    kind = kv[0].dtype
    width = 2 * count * HEAD_WIDTH
    tall, team = WINDOW * BLK, TEAM * BLK
    out_shape = [
        jax.ShapeDtypeStruct((team, width), jnp.float32),
        jax.ShapeDtypeStruct((REACH * BLK, width + HEAD_WIDTH), kind),
        jax.ShapeDtypeStruct((REACH * BLK, width), kind),
    ]
    part = (2 * RANK, padded(count * HEAD_WIDTH // 4))
    many = part if c == 0 else (2, *part)
    out_shape += [jax.ShapeDtypeStruct(shape, jnp.float32) for shape in (part, many, many)]
    if c == 0:
        out_shape.append(jax.ShapeDtypeStruct((2 * RANK, tall), kind))
    inputs = [mask, *kv, *halo, *qg, *earlier]
    scratch = [
        pltpu.VMEM((count, tall, HEAD_WIDTH), kind),
        pltpu.VMEM((count, tall, HEAD_WIDTH), kind),
        pltpu.VMEM((count, team, HEAD_WIDTH), kind),
        pltpu.VMEM((count, team, HEAD_WIDTH), kind),
        pltpu.VMEM((count * 2, (TILES + 1) * BLK, 2 * BLK), kind),
        pltpu.VMEM((count * 2, (TILES + 1) * BLK, 2 * BLK), kind),
        pltpu.VMEM((2 * RANK, count * HEAD_WIDTH), jnp.float32),
    ]
    return call(
        functools.partial(compute_kernel, c), f"gradients_{c}", out_shape, inputs, scratch=scratch, vmem=16
    )


def combine_kernel(last, bit, own_ref, a_ref, b_ref, keep_ref, *refs):
    outs = refs[-5 - last : -1 - last]
    member, team = place()
    even = lax.rem(team, 2)
    width = own_ref.shape[1]
    start = outs[1].shape[1] - width
    if last:
        outs[1][:, :start] = refs[0][...]
    for k in range(TEAM):
        owner = jnp.bitwise_xor(member, k)
        row = rows(lax.rem(owner, 2), 1)
        from_a = owner // 2 != even
        column = slice(start, start + width) if k == 1 else slice(None)

        def add(part_ref, out=outs[k], owner=owner, row=row, column=column):
            part = part_ref[row, :width].astype(jnp.float32)
            out[:, column] = (own_ref[rows(owner, 1), :] + part).astype(out.dtype)

        pl.when(from_a)(functools.partial(add, a_ref))
        pl.when(jnp.logical_not(from_a))(functools.partial(add, b_ref))
    got = [a_ref[rows(row, 1), pl.ds(width, keep_ref.shape[1])].astype(jnp.float32) for row in range(2)]
    total = keep_ref[...] + got[0] + got[1]
    if last:
        earlier, clip_ref, both_ref = refs[1:4]
        first = earlier[...] + clip_ref[0] + both_ref[0]
        second = total + clip_ref[1] + both_ref[1]
        upper = bit_value(*bit) == 1
        refs[-2][...] = jnp.where(upper, second, first)
        refs[-1][...] = jnp.where(upper, first, second)
    else:
        refs[-1][...] = total


def combine(c, bit, own, a, b, keep, earlier, after):
    last = int(c + 1 == len(CHUNKS))
    block = jax.ShapeDtypeStruct((BLK, own.shape[1]), a.dtype)
    wide = jax.ShapeDtypeStruct((BLK, own.shape[1] + (earlier[0].shape[1] if last else 0)), a.dtype)
    term = jax.ShapeDtypeStruct(keep.shape, keep.dtype)
    specs = [VMEM] * (4 + len(earlier)) + [ANY] * len(after)
    inputs = [own, a, b, keep, *earlier, *after]
    kernel = functools.partial(combine_kernel, last, bit)
    return call(kernel, f"combine_{c}", [block, wide, block, block] + [term] * (1 + last), inputs, specs)


def unpack_kernel(*refs):
    blocks, other, arrived = refs[: 3 * len(CHUNKS)], refs[3 * len(CHUNKS)], refs[3 * len(CHUNKS) + 1 : -4]
    outs, terms = refs[-4:-2], refs[-2:]
    member, _ = place()
    before = 0
    for c, (_, count) in enumerate(spans()):
        sources = [(0, blocks[3 * c], 0), (1, other, before), (2, blocks[3 * c + 1], 0), (3, blocks[3 * c + 2], 0)]
        for k, ref, column in sources:
            head = first_head(c, jnp.bitwise_xor(member, k))
            for part, out in enumerate(outs):
                out[0, :, cols(head, count)] = ref[:, cols(column + part * count, count)]
        before += 2 * count
    if len(arrived[0].shape) == 3:
        arrived = [ref.at[0] for ref in arrived]
    for half, term in zip((slice(0, RANK), slice(RANK, 2 * RANK)), terms):
        term[...] = sum(ref[half, : term.shape[1]] for ref in arrived)


def unpack(home, other, arrived, width):
    flat = [block for chunk in home for block in chunk] + [other, *arrived]
    shape = jax.ShapeDtypeStruct((1, BLK, HEAD_COUNT * HEAD_WIDTH), other.dtype)
    term = jax.ShapeDtypeStruct((RANK, width), jnp.float32)
    return call(unpack_kernel, "unpack", [shape, shape, term, term], flat)


def bit_value(axis, bit, unit):
    return lax.rem(lax.axis_index(axis) // (bit * unit), 2)


def fold_kernel(bit, width, held_ref, got_ref, keep_ref, send_ref):
    half = keep_ref.shape[0]
    value = bit_value(*bit)
    if len(held_ref.shape) == 2:
        for j in range(half):
            low, high = (slice(i * width, (i + 1) * width) for i in (j, half + j))
            low, high = (held_ref[:, part] + got_ref[:, part] for part in (low, high))
            keep_ref[j, :, :width] = jnp.where(value == 1, high, low)
            send_ref[j, :, :width] = jnp.where(value == 1, low, high)
    else:
        for out, first in ((keep_ref, value * half), (send_ref, (1 - value) * half)):
            out[...] = held_ref[pl.ds(first, half)] + got_ref[pl.ds(first, half)]


def later_rounds():
    clips, teams = lax.axis_size("dp"), lax.axis_size("seq") // TEAM
    clip_bits = [clips >> s for s in range(2, clips.bit_length())]
    team_bits = [teams >> s for s in range(1, teams.bit_length() - 1)]
    return [("dp", bit, 1) for bit in clip_bits] + [("seq", bit, TEAM) for bit in team_bits]


def reduce_terms(held, sent):
    clips, seq = lax.axis_size("dp"), lax.axis_size("seq")
    teams = seq // TEAM
    pieces = clips * teams
    width = HEADS * HEAD_WIDTH // pieces
    rounds = later_rounds()

    def piece_of(clip, team):
        bits = [(clip if axis == "dp" else team) // bit % 2 for axis, bit, _ in rounds]
        bits[1:1] = [team % 2, clip // (clips // 2) % 2]
        return functools.reduce(lambda value, bit: 2 * value + bit, bits, 0)

    for index, (axis, bit, unit) in enumerate(rounds[:-1]):
        route = [(i, i ^ (bit * unit)) for i in range(lax.axis_size(axis))]
        got = lax.ppermute(sent, axis, route)
        shape = jax.ShapeDtypeStruct((pieces >> (index + 4), 2 * RANK, padded(width)), jnp.float32)
        kernel = functools.partial(fold_kernel, rounds[index + 1], width)
        held, sent = call(kernel, f"fold_{index}", [shape, shape], [held, got])
    arrived = []
    for flip, piece in enumerate((held, sent)):
        route = []
        for clip in range(clips):
            for position in range(seq):
                other = flip * (pieces // 2 if len(rounds) == 1 else 1)
                c, index = divmod(piece_of(clip, position // TEAM) ^ other, pieces // 2)
                route.append((clip * seq + position, (c * TEAM + position % TEAM) * pieces // 2 + index))
        arrived.append(lax.ppermute(piece, ("dp", "seq"), route))
    return arrived, width


def body(
    head_queries,
    head_keys,
    head_values,
    output_gradient,
    key_adapter_input,
    value_adapter_input,
    key_block_lists,
    live_block_counts,
):
    seq = lax.axis_size("seq")
    teams = seq // TEAM

    def partner(block, k):
        return lax.ppermute(block, "seq", [(i, i ^ k) for i in range(seq)]) if k else block

    near_route = []
    for p in range(seq):
        t = p // TEAM + (1 if p % TEAM >= TEAM // 2 else -1)
        if 0 <= t < teams:
            near_route.append((p, t * TEAM + p % TEAM))
    far_route = [(target, source) for source, target in near_route]
    swaps = []
    for start in (0, 1):
        pairs = []
        for t in range(start, teams - 1, 2):
            for m in range(TEAM):
                pairs += [(t * TEAM + m, (t + 1) * TEAM + m), ((t + 1) * TEAM + m, t * TEAM + m)]
        swaps.append(pairs)

    lists = key_block_lists.transpose(2, 1, 0)
    counts = live_block_counts.T
    adapters = (key_adapter_input.transpose(0, 2, 1), value_adapter_input.transpose(0, 2, 1))
    sides = pack("pack_side", (SIDE,), head_keys, head_values, adapters, at_once=True)
    kv_side = [partner(side, 1) for (side,) in sides]
    kv_out = pack("pack_kv", (OWN, ACROSS), head_keys, head_values, adapters)
    mask = make_mask(lists, counts, kv_out[0][0])
    qg_out = pack("pack_qg", (SIDE, OWN, ACROSS), head_queries, output_gradient, after=[mask])
    qg_side = [partner(side, 1) for side, _, _ in qg_out]
    kv, halo, qg = [], [], []
    for c in range(len(CHUNKS)):
        (mine, across), got = kv_out[c], kv_side[c]
        chip, send = route(f"route_kv_{c}", mine, across, got)
        kv.append((chip, partner(send, 2)))
    for c in range(len(CHUNKS)):
        (_, mine, across), got = qg_out[c], qg_side[c]
        chip, send = route(f"route_qg_{c}", mine, across, got, [kv[0][1]])
        qg.append((chip, partner(send, 2)))
        halo.append((lax.ppermute(kv[c][0], "seq", near_route), lax.ppermute(kv[c][1], "seq", far_route)))
    earlier, parts = [], []
    for c in range(len(CHUNKS)):
        own, to_a, to_b, keep, to_clip, to_both, *more = compute(c, mask, kv[c], halo[c], qg[c], earlier)
        earlier = [*more, to_clip, to_both]
        parts.append((own, lax.ppermute(to_a, "seq", swaps[0]), lax.ppermute(to_b, "seq", swaps[1]), keep))
    clips = lax.axis_size("dp")
    from_clip = lax.ppermute(to_clip, "dp", [(i, i ^ (clips // 2)) for i in range(clips)])
    both = []
    for clip in range(clips):
        both += [(clip * seq + p, (clip ^ (clips // 2)) * seq + (p ^ TEAM)) for p in range(seq)]
    from_both = lax.ppermute(to_both, ("dp", "seq"), both)
    home, earlier, after = [], [], []
    for c, part in enumerate(parts):
        last = c + 1 == len(CHUNKS)
        given = [*earlier, from_clip, from_both] if last else []
        blocks = combine(c, later_rounds()[0], *part, given, after)
        home.append([blocks[0], partner(blocks[2], 2), partner(blocks[3], 3)])
        earlier, after = [blocks[1], blocks[4]], home[-1][1:]
    key_gradient, value_gradient, key_term, value_term = unpack(
        home, partner(blocks[1], 1), *reduce_terms(blocks[4], blocks[5])
    )
    return key_gradient, value_gradient, key_term.T, value_term.T


def solution(mesh):
    tokens = P("dp", "seq", None)
    shares = P(("dp", "seq"), None)
    return jax.shard_map(
        body,
        mesh=mesh,
        in_specs=(tokens,) * 6 + (P(), P()),
        out_specs=(tokens, tokens, shares, shares),
        check_vma=False,
    )
```

```python
import functools

import jax
import jax.numpy as jnp
from jax import lax
from jax.experimental import pallas as pl
from jax.experimental.pallas import tpu as pltpu
from jax.sharding import PartitionSpec as P

HEAD_COUNT = 24
HEAD_WIDTH = 128
BLK = 128
REACH = 2
TILES = 5
RANK = 64
TEAM = 4
HEADS = HEAD_COUNT // TEAM
CHUNKS = (3, 3)
WINDOW = TEAM + 2 * REACH
SCALING = HEAD_WIDTH**-0.5
LOG2E = 1.4426950408889634
ANY = pl.BlockSpec(memory_space=pl.ANY)
PACK_VMEM = 56
VMEM = pl.BlockSpec(memory_space=pltpu.VMEM)
SMEM = pl.BlockSpec(memory_space=pltpu.SMEM)
MARK = jax.ShapeDtypeStruct((8, HEAD_WIDTH), jnp.float32)


def call(kernel, name, out_shape, inputs, in_specs=None, scratch=(), vmem=4):
    return pl.pallas_call(
        kernel,
        out_shape=out_shape,
        in_specs=in_specs or [VMEM] * len(inputs),
        out_specs=[VMEM] * len(out_shape),
        scratch_shapes=list(scratch),
        compiler_params=pltpu.CompilerParams(vmem_limit_bytes=vmem << 20),
        cost_estimate=pl.CostEstimate(flops=1, bytes_accessed=1, transcendentals=0),
        name=name,
    )(*inputs)


def cols(first, count):
    if not isinstance(first, int):
        first = pl.multiple_of(first * HEAD_WIDTH, HEAD_WIDTH)
    else:
        first = first * HEAD_WIDTH
    return pl.ds(first, count * HEAD_WIDTH)


def rows(first, count):
    if not isinstance(first, int):
        first = pl.multiple_of(first * BLK, BLK)
    else:
        first = first * BLK
    return pl.ds(first, count * BLK)


def padded(columns):
    return pl.cdiv(columns, HEAD_WIDTH) * HEAD_WIDTH


def first_head(c, member):
    return (c * TEAM + member) * CHUNKS[c]


def place():
    position = lax.axis_index("seq")
    return lax.rem(position, TEAM), position // TEAM


def spans():
    return [(sum(CHUNKS[:c]), count) for c, count in enumerate(CHUNKS)]


SIDE, OWN, ACROSS = (1, 3), (0,), (2,)


def pack_plan(kinds, adapters, chunks):
    return [(span, owners, bool(adapters) and span[0] == 0) for span in chunks for owners in kinds]


def fill(plan, a_ref, b_ref, outs, part):
    member, _ = place()
    for ((first, count), owners, _), out in zip(plan, outs):
        for index, k in enumerate(owners):
            head = first_head(first // count, jnp.bitwise_xor(member, k))
            out[part, cols(2 * index * count, count)] = a_ref[part, cols(head, count)]
            out[part, cols((2 * index + 1) * count, count)] = b_ref[part, cols(head, count)]


def fill_adapters(plan, key_tile, value_tile, outs):
    for (_, _, adapted), out in zip(plan, outs):
        if adapted:
            column = cols(out.shape[1] // HEAD_WIDTH - 1, 1)
            out[:RANK, column] = key_tile
            out[RANK:, column] = value_tile


def pack_first_kernel(plan, keys, values, key_in, value_in, *refs):
    outs, (small, sems) = refs[:-2], refs[-2:]
    member, _ = place()
    copies = [(key_in.at[0], small.at[0]), (value_in.at[0], small.at[1])]
    for ((first, count), owners, _), out in zip(plan, outs):
        for index, k in enumerate(owners):
            head = first_head(first // count, jnp.bitwise_xor(member, k))
            for part, source in enumerate((keys, values)):
                target = out.at[:, cols((2 * index + part) * count, count)]
                copies.append((source.at[0, :, cols(head, count)], target))
    copies = [pltpu.make_async_copy(*pair, sems.at[i]) for i, pair in enumerate(copies)]
    for copy in copies:
        copy.start()
    for copy in copies[:2]:
        copy.wait()
    fill_adapters(plan, small[0], small[1], outs)
    for copy in copies[2:]:
        copy.wait()


def pack_kernel(plan, adapters, a_ref, b_ref, *refs):
    outs = refs[-len(plan) :]
    fill(plan, a_ref.at[0], b_ref.at[0], outs, slice(None))
    if adapters:
        fill_adapters(plan, refs[0][0], refs[1][0], outs)


def pack(name, kinds, first, second, adapters=(), after=(), only=None):
    chunks = spans() if only is None else [spans()[only]]
    plan = pack_plan(kinds, adapters, chunks)
    kind = first.dtype
    out_shape = [
        jax.ShapeDtypeStruct((BLK, (2 * count * len(owners) + adapted) * HEAD_WIDTH), kind)
        for (_, count), owners, adapted in plan
    ]
    inputs = [first, second, *adapters, *after]
    if only is not None:
        scratch = [
            pltpu.VMEM((2, RANK, BLK), kind),
            pltpu.SemaphoreType.DMA((2 + sum(2 * len(owners) for _, owners, _ in plan),)),
        ]
        kernel = functools.partial(pack_first_kernel, plan)
        outs = call(kernel, name, out_shape, inputs, [ANY] * 4, scratch, PACK_VMEM)
    else:
        kernel = functools.partial(pack_kernel, plan, bool(adapters))
        specs = [VMEM] * (2 + len(adapters)) + [ANY] * len(after)
        outs = call(kernel, name, out_shape, inputs, specs)
    return [outs[len(kinds) * c : len(kinds) * (c + 1)] for c in range(len(chunks))]


def route_kernel(mine_ref, across_ref, got_ref, *refs):
    chip_ref, send_ref = refs[-2:]
    half, extra = 2 * HEAD_WIDTH, mine_ref.shape[1] % (2 * HEAD_WIDTH)
    half = mine_ref.shape[1] - extra
    chip_ref[rows(0, 1), :] = mine_ref[...]
    chip_ref[rows(1, 1), :half] = got_ref[:, :half]
    send_ref[rows(0, 1), :] = across_ref[...]
    send_ref[rows(1, 1), :half] = got_ref[:, half : 2 * half]
    if extra:
        for out in (chip_ref, send_ref):
            out[rows(1, 1), half:] = got_ref[:, 2 * half :]


def route(name, mine, across, got, after=()):
    shape = jax.ShapeDtypeStruct((2 * BLK, mine.shape[1]), mine.dtype)
    specs = [VMEM] * 3 + [ANY] * len(after)
    return call(route_kernel, name, [shape, shape], [mine, across, got, *after], specs)


def mask_kernel(lists_ref, counts_ref, _, mask_ref):
    member, team = place()
    for h in range(HEADS):
        head = first_head(h // CHUNKS[0], member) + h % CHUNKS[0]
        for b in range(TEAM):
            block = team * TEAM + b
            used = counts_ref[block, head]
            live = jnp.int32(0)
            for t in range(TILES):
                offset = lists_ref[t, block, head] - block + REACH
                live = live | jnp.where(t < used, jnp.left_shift(1, offset), 0)
            for t in range(TILES):
                value = jnp.where((live >> t) & 1 == 1, 0.0, -jnp.inf)
                row = (h * TEAM + b) * TILES + t
                mask_ref[row : row + 1, :] = jnp.full((1, BLK), value, jnp.float32)


def make_mask(lists, counts, after):
    shape = jax.ShapeDtypeStruct((HEADS * TEAM * TILES, BLK), jnp.float32)
    return call(mask_kernel, "mask", [shape], [lists, counts, after], [SMEM, SMEM, ANY])[0]


def compute_kernel(c, mask_ref, *refs):
    first, count = spans()[c]
    kv, halo, qg, rest = refs[:2], refs[2:4], refs[4:6], refs[6:]
    kw, vw, qs, gs, pm, dm, term = rest[-7:]
    if c == 0:
        own_ref, a_ref, b_ref, keep_ref, clip_ref, both_ref, adapt = rest[:-7]
    else:
        adapt, *earlier, own_ref, a_ref, b_ref, keep_ref, clip_ref, both_ref = rest[:-7]
    kind = adapt.dtype
    member, team = place()
    even = lax.rem(team, 2) == 0
    places = []
    for j in range(TEAM):
        owner = jnp.bitwise_xor(member, j)
        places.append((owner, owner + REACH, lax.rem(owner + REACH + TEAM, WINDOW)))

    def tile(refs, j, h, part):
        return refs[j // 2][rows(j % 2, 1), cols(part * count + h, 1)]

    if c == 0:
        for j, (_, near, far) in enumerate(places):
            adapt[:, rows(near, 1)] = tile(kv, j, 0, 2)
            adapt[:, rows(far, 1)] = tile(halo, j, 0, 2)

    zero = jnp.zeros((BLK, BLK), kind)
    for index in range(count * 2):
        for matrix in (pm, dm):
            matrix[index, rows(TILES, 1), :BLK] = zero
            matrix[index, rows(0, 1), BLK:] = zero

    on_last = (((1,), (1,)), ((), ()))

    def product(left, right, dims=(((1,), (0,)), ((), ()))):
        return lax.dot_general(left, right, dims, preferred_element_type=jnp.float32)

    def load(h):
        for j, (owner, near, far) in enumerate(places):
            kw[h, rows(near, 1), :] = tile(kv, j, h, 0)
            vw[h, rows(near, 1), :] = tile(kv, j, h, 1)
            kw[h, rows(far, 1), :] = tile(halo, j, h, 0)
            vw[h, rows(far, 1), :] = tile(halo, j, h, 1)
            qs[h, rows(owner, 1), :] = tile(qg, j, h, 0)
            gs[h, rows(owner, 1), :] = tile(qg, j, h, 1)

    def scored(h, pair):
        span, two = rows(2 * pair, TILES + 1), rows(2 * pair, 2)
        return product(kw[h, span, :], qs[h, two, :], on_last), product(vw[h, span, :], gs[h, two, :], on_last)

    def soften(h, pair, scores, dprobs):
        index = h * 2 + pair
        for u in range(2):
            base = ((first + h) * TEAM + 2 * pair + u) * TILES
            masks = [mask_ref[base + t : base + t + 1, :] for t in range(TILES)]
            lanes = slice(u * BLK, (u + 1) * BLK)
            tiles = [slice((u + t) * BLK, (u + t + 1) * BLK) for t in range(TILES)]
            top = jnp.full((1, BLK), -jnp.inf, jnp.float32)
            for mask, tile in zip(masks, tiles):
                top = jnp.maximum(top, jnp.max(scores[tile, lanes], axis=0, keepdims=True) + mask)
            top = top * (SCALING * LOG2E)
            weights = []
            for mask, tile in zip(masks, tiles):
                weights.append(jnp.exp2(scores[tile, lanes] * (SCALING * LOG2E) - (top - mask)))
            total = sum(jnp.sum(weight, axis=0, keepdims=True) for weight in weights)
            mixed = sum(
                jnp.sum(weight * dprobs[tile, lanes], axis=0, keepdims=True) for weight, tile in zip(weights, tiles)
            )
            inverse = 1.0 / total
            delta = mixed * inverse
            for weight, tile in zip(weights, tiles):
                probs = weight * inverse
                pm[index, tile, lanes] = probs.astype(kind)
                dm[index, tile, lanes] = (probs * (dprobs[tile, lanes] - delta)).astype(kind)

    def spread(h, pair):
        index, two = h * 2 + pair, rows(2 * pair, 2)
        return product(dm[index], qs[h, two, :]) * SCALING, product(pm[index], gs[h, two, :])

    def finish(h, adds):
        split, edge = TEAM * BLK, REACH * BLK
        for part, column, half in ((0, cols(h, 1), 0), (1, cols(count + h, 1), RANK)):
            low, high = adds[0][part], adds[1][part]
            middle = low[edge:] + high[:split]
            lower, upper = low[:edge].astype(kind), high[split:].astype(kind)
            own_ref[:, column] = middle
            a_ref[:, column] = jnp.where(even, upper, lower)
            b_ref[:, column] = jnp.where(even, lower, upper)
            window = jnp.concatenate([lower, middle.astype(kind), upper], axis=0)
            term[half : half + RANK, cols(h, 1)] = product(adapt[half : half + RANK, :], window)

    items = [(h, pair) for h in range(count) for pair in range(TEAM // 2)]
    for h in range(count):
        load(h)
    waiting, adds = scored(*items[0]), []
    for index, item in enumerate(items):
        current = waiting
        if index + 1 < len(items):
            waiting = scored(*items[index + 1])
        soften(*item, *current)
        adds.append(spread(*item))
        if len(adds) == TEAM // 2:
            finish(item[0], adds)
            adds = []
    width = term.shape[1] // 4
    quarters = [term[:, i * width : (i + 1) * width] for i in range(4)]
    upper = bit_value("dp", lax.axis_size("dp") // 2, 1) == 1

    def quarter(other_team, other_clip):
        odd, high = jnp.logical_not(even) ^ other_team, upper ^ other_clip
        return jnp.where(odd, jnp.where(high, *quarters[3:1:-1]), jnp.where(high, *quarters[1::-1]))

    keep_ref[:, :width] = quarter(False, False)
    leave = quarter(True, False)
    whole = leave.astype(kind)
    place_ = pl.ds(2 * count * HEAD_WIDTH, width)
    a_ref[rows(0, 1), place_] = whole
    a_ref[rows(1, 1), place_] = (leave - whole.astype(jnp.float32)).astype(kind)
    for out, part in ((clip_ref, quarter(False, True)), (both_ref, quarter(True, True))):
        if c == 0:
            out[:, :width] = part.astype(kind)
        else:
            out[1, :, :width] = part.astype(kind)
    if c == 1:
        clip_ref[0] = earlier[0][...]
        both_ref[0] = earlier[1][...]


def compute(c, mask, kv, halo, qg, earlier):
    count = CHUNKS[c]
    kind = kv[0].dtype
    width = 2 * count * HEAD_WIDTH
    tall, team = WINDOW * BLK, TEAM * BLK
    out_shape = [
        jax.ShapeDtypeStruct((team, width), jnp.float32),
        jax.ShapeDtypeStruct((REACH * BLK, width + HEAD_WIDTH), kind),
        jax.ShapeDtypeStruct((REACH * BLK, width), kind),
    ]
    part = (2 * RANK, padded(count * HEAD_WIDTH // 4))
    many = part if c == 0 else (2, *part)
    out_shape.append(jax.ShapeDtypeStruct(part, jnp.float32))
    out_shape += [jax.ShapeDtypeStruct(many, kind)] * 2
    if c == 0:
        out_shape.append(jax.ShapeDtypeStruct((2 * RANK, tall), kind))
    inputs = [mask, *kv, *halo, *qg, *earlier]
    scratch = [
        pltpu.VMEM((count, tall, HEAD_WIDTH), kind),
        pltpu.VMEM((count, tall, HEAD_WIDTH), kind),
        pltpu.VMEM((count, team, HEAD_WIDTH), kind),
        pltpu.VMEM((count, team, HEAD_WIDTH), kind),
        pltpu.VMEM((count * 2, (TILES + 1) * BLK, 2 * BLK), kind),
        pltpu.VMEM((count * 2, (TILES + 1) * BLK, 2 * BLK), kind),
        pltpu.VMEM((2 * RANK, count * HEAD_WIDTH), jnp.float32),
    ]
    return call(
        functools.partial(compute_kernel, c), f"gradients_{c}", out_shape, inputs, scratch=scratch, vmem=16
    )


def combine_kernel(last, bit, own_ref, a_ref, b_ref, keep_ref, *refs):
    outs = refs[-5 - last : -1 - last]
    member, team = place()
    even = lax.rem(team, 2)
    width = own_ref.shape[1]
    start = outs[1].shape[1] - width
    if last:
        outs[1][:, :start] = refs[0][...]
    for k in range(TEAM):
        owner = jnp.bitwise_xor(member, k)
        row = rows(lax.rem(owner, 2), 1)
        from_a = owner // 2 != even
        column = slice(start, start + width) if k == 1 else slice(None)

        def add(part_ref, out=outs[k], owner=owner, row=row, column=column):
            part = part_ref[row, :width].astype(jnp.float32)
            out[:, column] = (own_ref[rows(owner, 1), :] + part).astype(out.dtype)

        pl.when(from_a)(functools.partial(add, a_ref))
        pl.when(jnp.logical_not(from_a))(functools.partial(add, b_ref))
    got = [a_ref[rows(row, 1), pl.ds(width, keep_ref.shape[1])].astype(jnp.float32) for row in range(2)]
    total = keep_ref[...] + got[0] + got[1]
    if last:
        earlier, clip_ref, both_ref = refs[1:4]
        clip, both = clip_ref[...].astype(jnp.float32), both_ref[...].astype(jnp.float32)
        first = earlier[...] + clip[0] + both[0]
        second = total + clip[1] + both[1]
        upper = bit_value(*bit) == 1
        refs[-2][...] = jnp.where(upper, second, first).astype(refs[-2].dtype)
        refs[-1][...] = jnp.where(upper, first, second).astype(refs[-1].dtype)
    else:
        refs[-1][...] = total


def combine(c, bit, own, a, b, keep, earlier, after):
    last = int(c + 1 == len(CHUNKS))
    block = jax.ShapeDtypeStruct((BLK, own.shape[1]), a.dtype)
    wide = jax.ShapeDtypeStruct((BLK, own.shape[1] + (earlier[0].shape[1] if last else 0)), a.dtype)
    term = jax.ShapeDtypeStruct(keep.shape, a.dtype if last and len(later_rounds()) == 1 else keep.dtype)
    specs = [VMEM] * (4 + len(earlier)) + [ANY] * len(after)
    inputs = [own, a, b, keep, *earlier, *after]
    kernel = functools.partial(combine_kernel, last, bit)
    return call(kernel, f"combine_{c}", [block, wide, block, block] + [term] * (1 + last), inputs, specs)


def unpack_kernel(*refs):
    outs, other, blocks = refs[-3:-1], refs[-4], refs[:-4]
    refs[-1][...] = jnp.zeros_like(refs[-1])
    member, _ = place()
    before = 0
    for c, (first, count) in enumerate(spans()):
        sources = [(0, blocks[3 * c], 0), (1, other, before), (2, blocks[3 * c + 1], 0), (3, blocks[3 * c + 2], 0)]
        for k, ref, column in sources:
            head = first_head(c, jnp.bitwise_xor(member, k))
            for part, out in enumerate(outs):
                out[0, :, cols(head, count)] = ref[:, cols(column + part * count, count)]
        before += 2 * count


def unpack(home, other):
    flat = [block for chunk in home for block in chunk] + [other]
    shape = jax.ShapeDtypeStruct((1, BLK, HEAD_COUNT * HEAD_WIDTH), other.dtype)
    return call(unpack_kernel, "unpack", [shape, shape, MARK], flat)


def bit_value(axis, bit, unit):
    return lax.rem(lax.axis_index(axis) // (bit * unit), 2)


def fold_kernel(bit, width, held_ref, got_ref, keep_ref, send_ref):
    half = keep_ref.shape[0]
    value = bit_value(*bit)
    if len(held_ref.shape) == 2:
        for j in range(half):
            low, high = (slice(i * width, (i + 1) * width) for i in (j, half + j))
            low, high = (held_ref[:, part] + got_ref[:, part] for part in (low, high))
            keep_ref[j, :, :width] = jnp.where(value == 1, high, low).astype(keep_ref.dtype)
            send_ref[j, :, :width] = jnp.where(value == 1, low, high).astype(send_ref.dtype)
    else:
        for out, first in ((keep_ref, value * half), (send_ref, (1 - value) * half)):
            out[...] = (held_ref[pl.ds(first, half)] + got_ref[pl.ds(first, half)]).astype(out.dtype)


def final_kernel(first_ref, second_ref, _, key_ref, value_ref):
    width = key_ref.shape[1]
    if len(first_ref.shape) == 3:
        first_ref, second_ref = first_ref.at[0], second_ref.at[0]
    for half, out in ((slice(0, RANK), key_ref), (slice(RANK, 2 * RANK), value_ref)):
        out[...] = first_ref[half, :width].astype(jnp.float32) + second_ref[half, :width].astype(jnp.float32)


def later_rounds():
    clips, teams = lax.axis_size("dp"), lax.axis_size("seq") // TEAM
    clip_bits = [clips >> s for s in range(2, clips.bit_length())]
    team_bits = [teams >> s for s in range(1, teams.bit_length() - 1)]
    return [("dp", bit, 1) for bit in clip_bits] + [("seq", bit, TEAM) for bit in team_bits]


def reduce_terms(held, sent, after):
    clips, seq = lax.axis_size("dp"), lax.axis_size("seq")
    teams = seq // TEAM
    pieces = clips * teams
    width = HEADS * HEAD_WIDTH // pieces
    rounds = later_rounds()

    def piece_of(clip, team):
        bits = [(clip if axis == "dp" else team) // bit % 2 for axis, bit, _ in rounds]
        bits[1:1] = [team % 2, clip // (clips // 2) % 2]
        return functools.reduce(lambda value, bit: 2 * value + bit, bits, 0)

    for index, (axis, bit, unit) in enumerate(rounds[:-1]):
        route = [(i, i ^ (bit * unit)) for i in range(lax.axis_size(axis))]
        got = lax.ppermute(sent, axis, route)
        kind = jnp.bfloat16 if index + 2 == len(rounds) else jnp.float32
        shape = jax.ShapeDtypeStruct((pieces >> (index + 4), 2 * RANK, padded(width)), kind)
        kernel = functools.partial(fold_kernel, rounds[index + 1], width)
        held, sent = call(kernel, f"fold_{index}", [shape, shape], [held, got])
    arrived = []
    for flip, piece in enumerate((held, sent)):
        route = []
        for clip in range(clips):
            for position in range(seq):
                other = flip * (pieces // 2 if len(rounds) == 1 else 1)
                c, index = divmod(piece_of(clip, position // TEAM) ^ other, pieces // 2)
                route.append((clip * seq + position, (c * TEAM + position % TEAM) * pieces // 2 + index))
        arrived.append(lax.ppermute(piece, ("dp", "seq"), route))
    shape = jax.ShapeDtypeStruct((RANK, width), jnp.float32)
    return call(final_kernel, "final", [shape, shape], [*arrived, after], [VMEM, VMEM, ANY])


def body(
    head_queries,
    head_keys,
    head_values,
    output_gradient,
    key_adapter_input,
    value_adapter_input,
    key_block_lists,
    live_block_counts,
):
    seq = lax.axis_size("seq")
    teams = seq // TEAM

    def partner(block, k):
        return lax.ppermute(block, "seq", [(i, i ^ k) for i in range(seq)]) if k else block

    near_route = []
    for p in range(seq):
        t = p // TEAM + (1 if p % TEAM >= TEAM // 2 else -1)
        if 0 <= t < teams:
            near_route.append((p, t * TEAM + p % TEAM))
    far_route = [(target, source) for source, target in near_route]
    swaps = []
    for start in (0, 1):
        pairs = []
        for t in range(start, teams - 1, 2):
            for m in range(TEAM):
                pairs += [(t * TEAM + m, (t + 1) * TEAM + m), ((t + 1) * TEAM + m, t * TEAM + m)]
        swaps.append(pairs)

    lists = key_block_lists.transpose(2, 1, 0)
    counts = live_block_counts.T
    adapters = (key_adapter_input.transpose(0, 2, 1), value_adapter_input.transpose(0, 2, 1))
    ((side,),) = pack("pack_side", (SIDE,), head_keys, head_values, adapters, only=0)
    kv_out = pack("pack_kv", (SIDE, OWN, ACROSS), head_keys, head_values, adapters)
    kv_side = [partner(side if c == 0 else kv_out[c][0], 1) for c in range(len(CHUNKS))]
    mask = make_mask(lists, counts, kv_out[0][1])
    qg_out = pack("pack_qg", (SIDE, OWN, ACROSS), head_queries, output_gradient, after=[mask])
    qg_side = [partner(side, 1) for side, _, _ in qg_out]
    kv, halo, qg = [], [], []
    for c in range(len(CHUNKS)):
        (_, mine, across), got = kv_out[c], kv_side[c]
        chip, send = route(f"route_kv_{c}", mine, across, got)
        kv.append((chip, partner(send, 2)))
    for c in range(len(CHUNKS)):
        (_, mine, across), got = qg_out[c], qg_side[c]
        chip, send = route(f"route_qg_{c}", mine, across, got, [kv[0][1]])
        qg.append((chip, partner(send, 2)))
        halo.append((lax.ppermute(kv[c][0], "seq", near_route), lax.ppermute(kv[c][1], "seq", far_route)))
    earlier, parts = [], []
    for c in range(len(CHUNKS)):
        own, to_a, to_b, keep, to_clip, to_both, *more = compute(c, mask, kv[c], halo[c], qg[c], earlier)
        earlier = [*more, to_clip, to_both]
        parts.append((own, lax.ppermute(to_a, "seq", swaps[0]), lax.ppermute(to_b, "seq", swaps[1]), keep))
    clips = lax.axis_size("dp")
    from_clip = lax.ppermute(to_clip, "dp", [(i, i ^ (clips // 2)) for i in range(clips)])
    both = []
    for clip in range(clips):
        both += [(clip * seq + p, (clip ^ (clips // 2)) * seq + (p ^ TEAM)) for p in range(seq)]
    from_both = lax.ppermute(to_both, ("dp", "seq"), both)
    home, earlier, after = [], [], []
    for c, part in enumerate(parts):
        last = c + 1 == len(CHUNKS)
        given = [*earlier, from_clip, from_both] if last else []
        blocks = combine(c, later_rounds()[0], *part, given, after)
        home.append([blocks[0], partner(blocks[2], 2), partner(blocks[3], 3)])
        earlier, after = [blocks[1], blocks[4]], home[-1][1:]
    key_gradient, value_gradient, mark = unpack(home, partner(blocks[1], 1))
    key_term, value_term = reduce_terms(blocks[4], blocks[5], mark)
    return key_gradient, value_gradient, key_term.T, value_term.T


def solution(mesh):
    tokens = P("dp", "seq", None)
    shares = P(("dp", "seq"), None)
    return jax.shard_map(
        body,
        mesh=mesh,
        in_specs=(tokens,) * 6 + (P(), P()),
        out_specs=(tokens, tokens, shares, shares),
        check_vma=False,
    )
```

```python
import functools

import jax
import jax.numpy as jnp
from jax import lax
from jax.experimental import pallas as pl
from jax.experimental.pallas import tpu as pltpu
from jax.sharding import PartitionSpec as P

HEAD_COUNT = 24
HEAD_WIDTH = 128
BLK = 128
REACH = 2
TILES = 5
RANK = 64
TEAM = 4
HEADS = HEAD_COUNT // TEAM
CHUNKS = (3, 3)
WINDOW = TEAM + 2 * REACH
SCALING = HEAD_WIDTH**-0.5
LOG2E = 1.4426950408889634
ANY = pl.BlockSpec(memory_space=pl.ANY)
PACK_VMEM = 56
VMEM = pl.BlockSpec(memory_space=pltpu.VMEM)
SMEM = pl.BlockSpec(memory_space=pltpu.SMEM)
MARK = jax.ShapeDtypeStruct((8, HEAD_WIDTH), jnp.float32)


def call(kernel, name, out_shape, inputs, in_specs=None, scratch=(), vmem=4):
    return pl.pallas_call(
        kernel,
        out_shape=out_shape,
        in_specs=in_specs or [VMEM] * len(inputs),
        out_specs=[VMEM] * len(out_shape),
        scratch_shapes=list(scratch),
        compiler_params=pltpu.CompilerParams(vmem_limit_bytes=vmem << 20),
        cost_estimate=pl.CostEstimate(flops=1, bytes_accessed=1, transcendentals=0),
        name=name,
    )(*inputs)


def cols(first, count):
    if not isinstance(first, int):
        first = pl.multiple_of(first * HEAD_WIDTH, HEAD_WIDTH)
    else:
        first = first * HEAD_WIDTH
    return pl.ds(first, count * HEAD_WIDTH)


def rows(first, count):
    if not isinstance(first, int):
        first = pl.multiple_of(first * BLK, BLK)
    else:
        first = first * BLK
    return pl.ds(first, count * BLK)


def padded(columns):
    return pl.cdiv(columns, HEAD_WIDTH) * HEAD_WIDTH


def first_head(c, member):
    return (c * TEAM + member) * CHUNKS[c]


def place():
    position = lax.axis_index("seq")
    return lax.rem(position, TEAM), position // TEAM


def spans():
    return [(sum(CHUNKS[:c]), count) for c, count in enumerate(CHUNKS)]


SIDE, OWN, ACROSS = (1, 3), (0,), (2,)


def pack_plan(kinds, adapters, chunks):
    return [(span, owners, bool(adapters) and span[0] == 0) for span in chunks for owners in kinds]


def fill(plan, a_ref, b_ref, outs, part):
    member, _ = place()
    for ((first, count), owners, _), out in zip(plan, outs):
        for index, k in enumerate(owners):
            head = first_head(first // count, jnp.bitwise_xor(member, k))
            out[part, cols(2 * index * count, count)] = a_ref[part, cols(head, count)]
            out[part, cols((2 * index + 1) * count, count)] = b_ref[part, cols(head, count)]


def fill_adapters(plan, key_tile, value_tile, outs):
    for (_, _, adapted), out in zip(plan, outs):
        if adapted:
            column = cols(out.shape[1] // HEAD_WIDTH - 1, 1)
            out[:RANK, column] = key_tile
            out[RANK:, column] = value_tile


def pack_first_kernel(plan, keys, values, key_in, value_in, *refs):
    outs, (small, sems) = refs[:-2], refs[-2:]
    member, _ = place()
    copies = [(key_in.at[0], small.at[0]), (value_in.at[0], small.at[1])]
    for ((first, count), owners, _), out in zip(plan, outs):
        for index, k in enumerate(owners):
            head = first_head(first // count, jnp.bitwise_xor(member, k))
            for part, source in enumerate((keys, values)):
                target = out.at[:, cols((2 * index + part) * count, count)]
                copies.append((source.at[0, :, cols(head, count)], target))
    copies = [pltpu.make_async_copy(*pair, sems.at[i]) for i, pair in enumerate(copies)]
    for copy in copies:
        copy.start()
    for copy in copies[:2]:
        copy.wait()
    fill_adapters(plan, small[0], small[1], outs)
    for copy in copies[2:]:
        copy.wait()


def pack_kernel(plan, adapters, a_ref, b_ref, *refs):
    outs = refs[-len(plan) :]
    fill(plan, a_ref.at[0], b_ref.at[0], outs, slice(None))
    if adapters:
        fill_adapters(plan, refs[0][0], refs[1][0], outs)


def pack(name, kinds, first, second, adapters=(), after=(), only=None):
    chunks = spans() if only is None else [spans()[only]]
    plan = pack_plan(kinds, adapters, chunks)
    kind = first.dtype
    out_shape = [
        jax.ShapeDtypeStruct((BLK, (2 * count * len(owners) + adapted) * HEAD_WIDTH), kind)
        for (_, count), owners, adapted in plan
    ]
    inputs = [first, second, *adapters, *after]
    if only is not None:
        scratch = [
            pltpu.VMEM((2, RANK, BLK), kind),
            pltpu.SemaphoreType.DMA((2 + sum(2 * len(owners) for _, owners, _ in plan),)),
        ]
        kernel = functools.partial(pack_first_kernel, plan)
        outs = call(kernel, name, out_shape, inputs, [ANY] * 4, scratch, PACK_VMEM)
    else:
        kernel = functools.partial(pack_kernel, plan, bool(adapters))
        specs = [VMEM] * (2 + len(adapters)) + [ANY] * len(after)
        outs = call(kernel, name, out_shape, inputs, specs)
    return [outs[len(kinds) * c : len(kinds) * (c + 1)] for c in range(len(chunks))]


def route_kernel(mine_ref, across_ref, got_ref, *refs):
    chip_ref, send_ref = refs[-2:]
    half, extra = 2 * HEAD_WIDTH, mine_ref.shape[1] % (2 * HEAD_WIDTH)
    half = mine_ref.shape[1] - extra
    chip_ref[rows(0, 1), :] = mine_ref[...]
    chip_ref[rows(1, 1), :half] = got_ref[:, :half]
    send_ref[rows(0, 1), :] = across_ref[...]
    send_ref[rows(1, 1), :half] = got_ref[:, half : 2 * half]
    if extra:
        for out in (chip_ref, send_ref):
            out[rows(1, 1), half:] = got_ref[:, 2 * half :]


def route(name, mine, across, got, after=()):
    shape = jax.ShapeDtypeStruct((2 * BLK, mine.shape[1]), mine.dtype)
    specs = [VMEM] * 3 + [ANY] * len(after)
    return call(route_kernel, name, [shape, shape], [mine, across, got, *after], specs)


def mask_kernel(lists_ref, counts_ref, _, mask_ref):
    member, team = place()
    for h in range(HEADS):
        head = first_head(h // CHUNKS[0], member) + h % CHUNKS[0]
        for b in range(TEAM):
            block = team * TEAM + b
            used = counts_ref[block, head]
            live = jnp.int32(0)
            for t in range(TILES):
                offset = lists_ref[t, block, head] - block + REACH
                live = live | jnp.where(t < used, jnp.left_shift(1, offset), 0)
            for t in range(TILES):
                value = jnp.where((live >> t) & 1 == 1, 0.0, -jnp.inf)
                row = (h * TEAM + b) * TILES + t
                mask_ref[row : row + 1, :] = jnp.full((1, BLK), value, jnp.float32)


def make_mask(lists, counts, after):
    shape = jax.ShapeDtypeStruct((HEADS * TEAM * TILES, BLK), jnp.float32)
    return call(mask_kernel, "mask", [shape], [lists, counts, after], [SMEM, SMEM, ANY])[0]


def compute_kernel(c, mask_ref, *refs):
    first, count = spans()[c]
    kv, halo, qg, rest = refs[:2], refs[2:4], refs[4:6], refs[6:]
    kw, vw, qs, gs, pm, dm, term = rest[-7:]
    if c == 0:
        own_ref, a_ref, b_ref, keep_ref, team_ref, clip_ref, both_ref, adapt = rest[:-7]
    else:
        adapt, *earlier, own_ref, a_ref, b_ref, keep_ref, clip_ref, both_ref = rest[:-7]
    kind = adapt.dtype
    member, team = place()
    even = lax.rem(team, 2) == 0
    places = []
    for j in range(TEAM):
        owner = jnp.bitwise_xor(member, j)
        places.append((owner, owner + REACH, lax.rem(owner + REACH + TEAM, WINDOW)))

    def tile(refs, j, h, part):
        return refs[j // 2][rows(j % 2, 1), cols(part * count + h, 1)]

    if c == 0:
        for j, (_, near, far) in enumerate(places):
            adapt[:, rows(near, 1)] = tile(kv, j, 0, 2)
            adapt[:, rows(far, 1)] = tile(halo, j, 0, 2)

    zero = jnp.zeros((BLK, BLK), kind)
    for index in range(count * 2):
        for matrix in (pm, dm):
            matrix[index, rows(TILES, 1), :BLK] = zero
            matrix[index, rows(0, 1), BLK:] = zero

    on_last = (((1,), (1,)), ((), ()))

    def product(left, right, dims=(((1,), (0,)), ((), ()))):
        return lax.dot_general(left, right, dims, preferred_element_type=jnp.float32)

    def load(h):
        for j, (owner, near, far) in enumerate(places):
            kw[h, rows(near, 1), :] = tile(kv, j, h, 0)
            vw[h, rows(near, 1), :] = tile(kv, j, h, 1)
            kw[h, rows(far, 1), :] = tile(halo, j, h, 0)
            vw[h, rows(far, 1), :] = tile(halo, j, h, 1)
            qs[h, rows(owner, 1), :] = tile(qg, j, h, 0)
            gs[h, rows(owner, 1), :] = tile(qg, j, h, 1)

    def scored(h, pair):
        span, two = rows(2 * pair, TILES + 1), rows(2 * pair, 2)
        return product(kw[h, span, :], qs[h, two, :], on_last), product(vw[h, span, :], gs[h, two, :], on_last)

    def soften(h, pair, scores, dprobs):
        index = h * 2 + pair
        for u in range(2):
            base = ((first + h) * TEAM + 2 * pair + u) * TILES
            masks = [mask_ref[base + t : base + t + 1, :] for t in range(TILES)]
            lanes = slice(u * BLK, (u + 1) * BLK)
            tiles = [slice((u + t) * BLK, (u + t + 1) * BLK) for t in range(TILES)]
            top = jnp.full((1, BLK), -jnp.inf, jnp.float32)
            for mask, tile in zip(masks, tiles):
                top = jnp.maximum(top, jnp.max(scores[tile, lanes], axis=0, keepdims=True) + mask)
            top = top * (SCALING * LOG2E)
            weights = []
            for mask, tile in zip(masks, tiles):
                weights.append(jnp.exp2(scores[tile, lanes] * (SCALING * LOG2E) - (top - mask)))
            total = sum(jnp.sum(weight, axis=0, keepdims=True) for weight in weights)
            mixed = sum(
                jnp.sum(weight * dprobs[tile, lanes], axis=0, keepdims=True) for weight, tile in zip(weights, tiles)
            )
            inverse = 1.0 / total
            delta = mixed * inverse
            for weight, tile in zip(weights, tiles):
                probs = weight * inverse
                pm[index, tile, lanes] = probs.astype(kind)
                dm[index, tile, lanes] = (probs * (dprobs[tile, lanes] - delta)).astype(kind)

    def spread(h, pair):
        index, two = h * 2 + pair, rows(2 * pair, 2)
        return product(dm[index], qs[h, two, :]) * SCALING, product(pm[index], gs[h, two, :])

    def finish(h, adds):
        split, edge = TEAM * BLK, REACH * BLK
        for part, column, half in ((0, cols(h, 1), 0), (1, cols(count + h, 1), RANK)):
            low, high = adds[0][part], adds[1][part]
            middle = low[edge:] + high[:split]
            lower, upper = low[:edge].astype(kind), high[split:].astype(kind)
            own_ref[:, column] = middle
            a_ref[:, column] = jnp.where(even, upper, lower)
            b_ref[:, column] = jnp.where(even, lower, upper)
            window = jnp.concatenate([lower, middle.astype(kind), upper], axis=0)
            term[half : half + RANK, cols(h, 1)] = product(adapt[half : half + RANK, :], window)

    items = [(h, pair) for h in range(count) for pair in range(TEAM // 2)]
    for h in range(count):
        load(h)
    ahead, adds = [scored(*item) for item in items[:2]], []
    for index, item in enumerate(items):
        current = ahead.pop(0)
        if index + 2 < len(items):
            ahead.append(scored(*items[index + 2]))
        soften(*item, *current)
        adds.append(spread(*item))
        if len(adds) == TEAM // 2:
            finish(item[0], adds)
            adds = []
    width = term.shape[1] // 4
    quarters = [term[:, i * width : (i + 1) * width] for i in range(4)]
    upper = bit_value("dp", lax.axis_size("dp") // 2, 1) == 1

    def quarter(other_team, other_clip):
        odd, high = jnp.logical_not(even) ^ other_team, upper ^ other_clip
        return jnp.where(odd, jnp.where(high, *quarters[3:1:-1]), jnp.where(high, *quarters[1::-1]))

    keep_ref[:, :width] = quarter(False, False)
    leave = quarter(True, False).astype(kind)
    if c == 0:
        team_ref[:, :width] = leave
    else:
        column = pl.ds(2 * count * HEAD_WIDTH, width)
        a_ref[rows(0, 1), column] = earlier[0][:, :width]
        a_ref[rows(1, 1), column] = leave
    for out, part in ((clip_ref, quarter(False, True)), (both_ref, quarter(True, True))):
        if c == 0:
            out[:, :width] = part.astype(kind)
        else:
            out[1, :, :width] = part.astype(kind)
    if c == 1:
        clip_ref[0] = earlier[1][...]
        both_ref[0] = earlier[2][...]


def compute(c, mask, kv, halo, qg, earlier):
    count = CHUNKS[c]
    kind = kv[0].dtype
    width = 2 * count * HEAD_WIDTH
    tall, team = WINDOW * BLK, TEAM * BLK
    out_shape = [
        jax.ShapeDtypeStruct((team, width), jnp.float32),
        jax.ShapeDtypeStruct((REACH * BLK, width + (HEAD_WIDTH if c else 0)), kind),
        jax.ShapeDtypeStruct((REACH * BLK, width), kind),
    ]
    part = (2 * RANK, padded(count * HEAD_WIDTH // 4))
    many = part if c == 0 else (2, *part)
    out_shape.append(jax.ShapeDtypeStruct(part, jnp.float32))
    if c == 0:
        out_shape.append(jax.ShapeDtypeStruct(part, kind))
    out_shape += [jax.ShapeDtypeStruct(many, kind)] * 2
    if c == 0:
        out_shape.append(jax.ShapeDtypeStruct((2 * RANK, tall), kind))
    inputs = [mask, *kv, *halo, *qg, *earlier]
    scratch = [
        pltpu.VMEM((count, tall, HEAD_WIDTH), kind),
        pltpu.VMEM((count, tall, HEAD_WIDTH), kind),
        pltpu.VMEM((count, team, HEAD_WIDTH), kind),
        pltpu.VMEM((count, team, HEAD_WIDTH), kind),
        pltpu.VMEM((count * 2, (TILES + 1) * BLK, 2 * BLK), kind),
        pltpu.VMEM((count * 2, (TILES + 1) * BLK, 2 * BLK), kind),
        pltpu.VMEM((2 * RANK, count * HEAD_WIDTH), jnp.float32),
    ]
    return call(
        functools.partial(compute_kernel, c), f"gradients_{c}", out_shape, inputs, scratch=scratch, vmem=16
    )


def combine_kernel(last, bit, own_ref, a_ref, b_ref, keep_ref, *refs):
    outs = refs[-6:-2] if last else refs[-4:]
    member, team = place()
    even = lax.rem(team, 2)
    width = own_ref.shape[1]
    start = outs[1].shape[1] - width
    if last:
        outs[1][:, :start] = refs[0][...]
    for k in range(TEAM):
        owner = jnp.bitwise_xor(member, k)
        row = rows(lax.rem(owner, 2), 1)
        from_a = owner // 2 != even
        column = slice(start, start + width) if k == 1 else slice(None)

        def add(part_ref, out=outs[k], owner=owner, row=row, column=column):
            part = part_ref[row, :width].astype(jnp.float32)
            out[:, column] = (own_ref[rows(owner, 1), :] + part).astype(out.dtype)

        pl.when(from_a)(functools.partial(add, a_ref))
        pl.when(jnp.logical_not(from_a))(functools.partial(add, b_ref))
    if last:
        earlier, clip_ref, both_ref = refs[1:4]
        totals = []
        for index, keep in enumerate((earlier, keep_ref)):
            got = a_ref[rows(index, 1), pl.ds(width, keep.shape[1])].astype(jnp.float32)
            totals.append(keep[...] + got + clip_ref[index].astype(jnp.float32) + both_ref[index].astype(jnp.float32))
        upper = bit_value(*bit) == 1
        refs[-2][...] = jnp.where(upper, *totals[::-1]).astype(refs[-2].dtype)
        refs[-1][...] = jnp.where(upper, *totals).astype(refs[-1].dtype)


def combine(c, bit, own, a, b, keep, earlier, after):
    last = int(c + 1 == len(CHUNKS))
    block = jax.ShapeDtypeStruct((BLK, own.shape[1]), a.dtype)
    wide = jax.ShapeDtypeStruct((BLK, own.shape[1] + (earlier[0].shape[1] if last else 0)), a.dtype)
    term = jax.ShapeDtypeStruct(keep.shape, a.dtype if last and len(later_rounds()) == 1 else keep.dtype)
    specs = [VMEM] * (4 + len(earlier)) + [ANY] * len(after)
    inputs = [own, a, b, keep, *earlier, *after]
    kernel = functools.partial(combine_kernel, last, bit)
    return call(kernel, f"combine_{c}", [block, wide, block, block] + [term] * (2 * last), inputs, specs)


def unpack_kernel(c, *refs):
    count = CHUNKS[c]
    own_ref, across_ref, diagonal_ref, other_ref = refs[:4]
    last = c + 1 == len(CHUNKS)
    outs = refs[-4:-2] if last else refs[-2:]
    member, _ = place()
    before = 2 * sum(CHUNKS[:c])
    for k, ref, column in ((0, own_ref, 0), (1, other_ref, before), (2, across_ref, 0), (3, diagonal_ref, 0)):
        head = jnp.bitwise_xor(member, k) * count
        for part, out in enumerate(outs):
            out[0, :, cols(head, count)] = ref[:, cols(column + part * count, count)]
    if last:
        arrived = refs[4:6]
        if len(arrived[0].shape) == 3:
            arrived = [ref.at[0] for ref in arrived]
        for half, term in zip((slice(0, RANK), slice(RANK, 2 * RANK)), refs[-2:]):
            term[...] = sum(ref[half, : term.shape[1]].astype(jnp.float32) for ref in arrived)


def unpack(c, home, other, arrived, width, earlier):
    last = c + 1 == len(CHUNKS)
    block = (1, BLK, TEAM * CHUNKS[c] * HEAD_WIDTH)
    shape = jax.ShapeDtypeStruct((1, BLK, HEAD_COUNT * HEAD_WIDTH), other.dtype)
    out_shape, out_specs = [shape] * 2, [pl.BlockSpec(block, lambda i: (0, 0, c))] * 2
    if last:
        out_shape += [jax.ShapeDtypeStruct((RANK, width), jnp.float32)] * 2
        out_specs += [pl.BlockSpec((RANK, width), lambda i: (0, 0))] * 2
    inputs = [*home, other, *arrived]
    return pl.pallas_call(
        functools.partial(unpack_kernel, c),
        grid=(1,),
        out_shape=out_shape,
        in_specs=[VMEM] * len(inputs) + [ANY] * len(earlier),
        out_specs=out_specs,
        input_output_aliases={len(inputs) + i: i for i in range(len(earlier))},
        compiler_params=pltpu.CompilerParams(vmem_limit_bytes=8 << 20),
        cost_estimate=pl.CostEstimate(flops=1, bytes_accessed=1, transcendentals=0),
        name=f"unpack_{c}",
    )(*inputs, *earlier)


def bit_value(axis, bit, unit):
    return lax.rem(lax.axis_index(axis) // (bit * unit), 2)


def fold_kernel(bit, width, held_ref, got_ref, keep_ref, send_ref):
    half = keep_ref.shape[0]
    value = bit_value(*bit)
    if len(held_ref.shape) == 2:
        for j in range(half):
            low, high = (slice(i * width, (i + 1) * width) for i in (j, half + j))
            low, high = (held_ref[:, part] + got_ref[:, part] for part in (low, high))
            keep_ref[j, :, :width] = jnp.where(value == 1, high, low).astype(keep_ref.dtype)
            send_ref[j, :, :width] = jnp.where(value == 1, low, high).astype(send_ref.dtype)
    else:
        for out, first in ((keep_ref, value * half), (send_ref, (1 - value) * half)):
            out[...] = (held_ref[pl.ds(first, half)] + got_ref[pl.ds(first, half)]).astype(out.dtype)


def later_rounds():
    clips, teams = lax.axis_size("dp"), lax.axis_size("seq") // TEAM
    clip_bits = [clips >> s for s in range(2, clips.bit_length())]
    team_bits = [teams >> s for s in range(1, teams.bit_length() - 1)]
    return [("dp", bit, 1) for bit in clip_bits] + [("seq", bit, TEAM) for bit in team_bits]


def reduce_terms(held, sent):
    clips, seq = lax.axis_size("dp"), lax.axis_size("seq")
    teams = seq // TEAM
    pieces = clips * teams
    width = HEADS * HEAD_WIDTH // pieces
    rounds = later_rounds()

    def piece_of(clip, team):
        bits = [(clip if axis == "dp" else team) // bit % 2 for axis, bit, _ in rounds]
        bits[1:1] = [team % 2, clip // (clips // 2) % 2]
        return functools.reduce(lambda value, bit: 2 * value + bit, bits, 0)

    for index, (axis, bit, unit) in enumerate(rounds[:-1]):
        route = [(i, i ^ (bit * unit)) for i in range(lax.axis_size(axis))]
        got = lax.ppermute(sent, axis, route)
        kind = jnp.bfloat16 if index + 2 == len(rounds) else jnp.float32
        shape = jax.ShapeDtypeStruct((pieces >> (index + 4), 2 * RANK, padded(width)), kind)
        kernel = functools.partial(fold_kernel, rounds[index + 1], width)
        held, sent = call(kernel, f"fold_{index}", [shape, shape], [held, got])
    arrived = []
    for flip, piece in enumerate((held, sent)):
        route = []
        for clip in range(clips):
            for position in range(seq):
                other = flip * (pieces // 2 if len(rounds) == 1 else 1)
                c, index = divmod(piece_of(clip, position // TEAM) ^ other, pieces // 2)
                route.append((clip * seq + position, (c * TEAM + position % TEAM) * pieces // 2 + index))
        arrived.append(lax.ppermute(piece, ("dp", "seq"), route))
    return arrived, width


def body(
    head_queries,
    head_keys,
    head_values,
    output_gradient,
    key_adapter_input,
    value_adapter_input,
    key_block_lists,
    live_block_counts,
):
    seq = lax.axis_size("seq")
    teams = seq // TEAM

    def partner(block, k):
        return lax.ppermute(block, "seq", [(i, i ^ k) for i in range(seq)]) if k else block

    near_route = []
    for p in range(seq):
        t = p // TEAM + (1 if p % TEAM >= TEAM // 2 else -1)
        if 0 <= t < teams:
            near_route.append((p, t * TEAM + p % TEAM))
    far_route = [(target, source) for source, target in near_route]
    swaps = []
    for start in (0, 1):
        pairs = []
        for t in range(start, teams - 1, 2):
            for m in range(TEAM):
                pairs += [(t * TEAM + m, (t + 1) * TEAM + m), ((t + 1) * TEAM + m, t * TEAM + m)]
        swaps.append(pairs)

    lists = key_block_lists.transpose(2, 1, 0)
    counts = live_block_counts.T
    adapters = (key_adapter_input.transpose(0, 2, 1), value_adapter_input.transpose(0, 2, 1))
    ((side,),) = pack("pack_side", (SIDE,), head_keys, head_values, adapters, only=0)
    kv_out = pack("pack_kv", (SIDE, OWN, ACROSS), head_keys, head_values, adapters)
    kv_side = [partner(side if c == 0 else kv_out[c][0], 1) for c in range(len(CHUNKS))]
    mask = make_mask(lists, counts, kv_out[0][1])
    qg_out = pack("pack_qg", (SIDE, OWN, ACROSS), head_queries, output_gradient, after=[mask])
    qg_side = [partner(side, 1) for side, _, _ in qg_out]
    kv, halo, qg = [], [], []
    for c in range(len(CHUNKS)):
        (_, mine, across), got = kv_out[c], kv_side[c]
        chip, send = route(f"route_kv_{c}", mine, across, got)
        kv.append((chip, partner(send, 2)))
    for c in range(len(CHUNKS)):
        (_, mine, across), got = qg_out[c], qg_side[c]
        chip, send = route(f"route_qg_{c}", mine, across, got, [kv[0][1]])
        qg.append((chip, partner(send, 2)))
        halo.append((lax.ppermute(kv[c][0], "seq", near_route), lax.ppermute(kv[c][1], "seq", far_route)))
    earlier, parts = [], []
    for c in range(len(CHUNKS)):
        own, to_a, to_b, keep, *quarters = compute(c, mask, kv[c], halo[c], qg[c], earlier)
        if c == 0:
            to_team, to_clip, to_both, adapt = quarters
            earlier = [adapt, to_team, to_clip, to_both]
        from_b = lax.ppermute(to_b, "seq", swaps[1])
        parts.append((own, lax.ppermute(to_a, "seq", swaps[0]), from_b, keep))
    to_clip, to_both = quarters
    clips = lax.axis_size("dp")
    from_clip = lax.ppermute(to_clip, "dp", [(i, i ^ (clips // 2)) for i in range(clips)])
    both = []
    for clip in range(clips):
        both += [(clip * seq + p, (clip ^ (clips // 2)) * seq + (p ^ TEAM)) for p in range(seq)]
    from_both = lax.ppermute(to_both, ("dp", "seq"), both)
    home, earlier, after = [], [], []
    for c, part in enumerate(parts):
        last = c + 1 == len(CHUNKS)
        given = [*earlier, from_clip, from_both] if last else []
        blocks = combine(c, later_rounds()[0], *part, given, after)
        home.append([blocks[0], partner(blocks[2], 2), partner(blocks[3], 3)])
        earlier, after = [blocks[1], part[-1]], home[-1][1:]
    other, (arrived, width) = partner(blocks[1], 1), reduce_terms(blocks[4], blocks[5])
    results = []
    for c in range(len(CHUNKS)):
        results = unpack(c, home[c], other, arrived if c + 1 == len(CHUNKS) else [], width, results)
    key_gradient, value_gradient, key_term, value_term = results
    return key_gradient, value_gradient, key_term.T, value_term.T


def solution(mesh):
    tokens = P("dp", "seq", None)
    shares = P(("dp", "seq"), None)
    return jax.shard_map(
        body,
        mesh=mesh,
        in_specs=(tokens,) * 6 + (P(), P()),
        out_specs=(tokens, tokens, shares, shares),
        check_vma=False,
    )
```

```python
import functools

import jax
import jax.numpy as jnp
from jax import lax
from jax.experimental import pallas as pl
from jax.experimental.pallas import tpu as pltpu
from jax.sharding import PartitionSpec as P

HEAD_COUNT = 24
HEAD_WIDTH = 128
BLK = 128
REACH = 2
TILES = 5
RANK = 64
TEAM = 4
HEADS = HEAD_COUNT // TEAM
CHUNKS = (3, 3)
WINDOW = TEAM + 2 * REACH
SCALING = HEAD_WIDTH**-0.5
LOG2E = 1.4426950408889634
ANY = pl.BlockSpec(memory_space=pl.ANY)
PACK_VMEM = 56
VMEM = pl.BlockSpec(memory_space=pltpu.VMEM)
SMEM = pl.BlockSpec(memory_space=pltpu.SMEM)
MARK = jax.ShapeDtypeStruct((8, HEAD_WIDTH), jnp.float32)


def call(kernel, name, out_shape, inputs, in_specs=None, scratch=(), vmem=4):
    return pl.pallas_call(
        kernel,
        out_shape=out_shape,
        in_specs=in_specs or [VMEM] * len(inputs),
        out_specs=[VMEM] * len(out_shape),
        scratch_shapes=list(scratch),
        compiler_params=pltpu.CompilerParams(vmem_limit_bytes=vmem << 20),
        cost_estimate=pl.CostEstimate(flops=1, bytes_accessed=1, transcendentals=0),
        name=name,
    )(*inputs)


def cols(first, count):
    if not isinstance(first, int):
        first = pl.multiple_of(first * HEAD_WIDTH, HEAD_WIDTH)
    else:
        first = first * HEAD_WIDTH
    return pl.ds(first, count * HEAD_WIDTH)


def rows(first, count):
    if not isinstance(first, int):
        first = pl.multiple_of(first * BLK, BLK)
    else:
        first = first * BLK
    return pl.ds(first, count * BLK)


def padded(columns):
    return pl.cdiv(columns, HEAD_WIDTH) * HEAD_WIDTH


def first_head(c, member):
    return (c * TEAM + member) * CHUNKS[c]


def place():
    position = lax.axis_index("seq")
    return lax.rem(position, TEAM), position // TEAM


def spans():
    return [(sum(CHUNKS[:c]), count) for c, count in enumerate(CHUNKS)]


SIDE, OWN, ACROSS = (1, 3), (0,), (2,)


def pack_plan(kinds, adapters, chunks):
    return [(span, owners, bool(adapters) and span[0] == 0) for span in chunks for owners in kinds]


def fill(plan, a_ref, b_ref, outs, part):
    member, _ = place()
    for ((first, count), owners, _), out in zip(plan, outs):
        for index, k in enumerate(owners):
            head = first_head(first // count, jnp.bitwise_xor(member, k))
            out[part, cols(2 * index * count, count)] = a_ref[part, cols(head, count)]
            out[part, cols((2 * index + 1) * count, count)] = b_ref[part, cols(head, count)]


def fill_adapters(plan, key_tile, value_tile, outs):
    for (_, _, adapted), out in zip(plan, outs):
        if adapted:
            column = cols(out.shape[1] // HEAD_WIDTH - 1, 1)
            out[:RANK, column] = key_tile
            out[RANK:, column] = value_tile


def pack_first_kernel(plan, keys, values, key_in, value_in, *refs):
    outs, (small, sems) = refs[:-2], refs[-2:]
    member, _ = place()
    copies = [(key_in.at[0], small.at[0]), (value_in.at[0], small.at[1])]
    for ((first, count), owners, _), out in zip(plan, outs):
        for index, k in enumerate(owners):
            head = first_head(first // count, jnp.bitwise_xor(member, k))
            for part, source in enumerate((keys, values)):
                target = out.at[:, cols((2 * index + part) * count, count)]
                copies.append((source.at[0, :, cols(head, count)], target))
    copies = [pltpu.make_async_copy(*pair, sems.at[i]) for i, pair in enumerate(copies)]
    for copy in copies:
        copy.start()
    for copy in copies[:2]:
        copy.wait()
    fill_adapters(plan, small[0], small[1], outs)
    for copy in copies[2:]:
        copy.wait()


def pack_kernel(plan, adapters, a_ref, b_ref, *refs):
    outs = refs[-len(plan) :]
    fill(plan, a_ref.at[0], b_ref.at[0], outs, slice(None))
    if adapters:
        fill_adapters(plan, refs[0][0], refs[1][0], outs)


def pack(name, kinds, first, second, adapters=(), after=(), only=None):
    chunks = spans() if only is None else [spans()[only]]
    plan = pack_plan(kinds, adapters, chunks)
    kind = first.dtype
    out_shape = [
        jax.ShapeDtypeStruct((BLK, (2 * count * len(owners) + adapted) * HEAD_WIDTH), kind)
        for (_, count), owners, adapted in plan
    ]
    inputs = [first, second, *adapters, *after]
    if only is not None:
        scratch = [
            pltpu.VMEM((2, RANK, BLK), kind),
            pltpu.SemaphoreType.DMA((2 + sum(2 * len(owners) for _, owners, _ in plan),)),
        ]
        kernel = functools.partial(pack_first_kernel, plan)
        outs = call(kernel, name, out_shape, inputs, [ANY] * 4, scratch, PACK_VMEM)
    else:
        kernel = functools.partial(pack_kernel, plan, bool(adapters))
        specs = [VMEM] * (2 + len(adapters)) + [ANY] * len(after)
        outs = call(kernel, name, out_shape, inputs, specs)
    return [outs[len(kinds) * c : len(kinds) * (c + 1)] for c in range(len(chunks))]


def route_kernel(mine_ref, across_ref, got_ref, *refs):
    chip_ref, send_ref = refs[-2:]
    half, extra = 2 * HEAD_WIDTH, mine_ref.shape[1] % (2 * HEAD_WIDTH)
    half = mine_ref.shape[1] - extra
    chip_ref[rows(0, 1), :] = mine_ref[...]
    chip_ref[rows(1, 1), :half] = got_ref[:, :half]
    send_ref[rows(0, 1), :] = across_ref[...]
    send_ref[rows(1, 1), :half] = got_ref[:, half : 2 * half]
    if extra:
        for out in (chip_ref, send_ref):
            out[rows(1, 1), half:] = got_ref[:, 2 * half :]


def route(name, mine, across, got, after=()):
    shape = jax.ShapeDtypeStruct((2 * BLK, mine.shape[1]), mine.dtype)
    specs = [VMEM] * 3 + [ANY] * len(after)
    return call(route_kernel, name, [shape, shape], [mine, across, got, *after], specs)


def mask_kernel(lists_ref, counts_ref, _, mask_ref):
    member, team = place()
    for h in range(HEADS):
        head = first_head(h // CHUNKS[0], member) + h % CHUNKS[0]
        for b in range(TEAM):
            block = team * TEAM + b
            used = counts_ref[block, head]
            live = jnp.int32(0)
            for t in range(TILES):
                offset = lists_ref[t, block, head] - block + REACH
                live = live | jnp.where(t < used, jnp.left_shift(1, offset), 0)
            for t in range(TILES):
                value = jnp.where((live >> t) & 1 == 1, 0.0, -jnp.inf)
                row = (h * TEAM + b) * TILES + t
                mask_ref[row : row + 1, :] = jnp.full((1, BLK), value, jnp.float32)


def make_mask(lists, counts, after):
    shape = jax.ShapeDtypeStruct((HEADS * TEAM * TILES, BLK), jnp.float32)
    return call(mask_kernel, "mask", [shape], [lists, counts, after], [SMEM, SMEM, ANY])[0]


def compute_kernel(c, mask_ref, *refs):
    first, count = spans()[c]
    kv, halo, qg, rest = refs[:2], refs[2:4], refs[4:6], refs[6:]
    kw, vw, qs, gs, pm, dm, term, parts = rest[-8:]
    if c == 0:
        own_ref, a_ref, b_ref, keep_ref, team_ref, clip_ref, both_ref, adapt = rest[:-8]
    else:
        adapt, *earlier, own_ref, a_ref, b_ref, keep_ref, clip_ref, both_ref = rest[:-8]
    kind = adapt.dtype
    member, team = place()
    even = lax.rem(team, 2) == 0
    places = []
    for j in range(TEAM):
        owner = jnp.bitwise_xor(member, j)
        places.append((owner, owner + REACH, lax.rem(owner + REACH + TEAM, WINDOW)))

    def tile(refs, j, h, part):
        return refs[j // 2][rows(j % 2, 1), cols(part * count + h, 1)]

    if c == 0:
        for j, (_, near, far) in enumerate(places):
            adapt[:, rows(near, 1)] = tile(kv, j, 0, 2)
            adapt[:, rows(far, 1)] = tile(halo, j, 0, 2)

    zero = jnp.zeros((BLK, BLK), kind)
    for index in range(count * 2):
        for matrix in (pm, dm):
            matrix[index, rows(TILES, 1), :BLK] = zero
            matrix[index, rows(0, 1), BLK:] = zero

    on_last = (((1,), (1,)), ((), ()))

    def product(left, right, dims=(((1,), (0,)), ((), ()))):
        return lax.dot_general(left, right, dims, preferred_element_type=jnp.float32)

    def load(h):
        for j, (owner, near, far) in enumerate(places):
            kw[h, rows(near, 1), :] = tile(kv, j, h, 0)
            vw[h, rows(near, 1), :] = tile(kv, j, h, 1)
            kw[h, rows(far, 1), :] = tile(halo, j, h, 0)
            vw[h, rows(far, 1), :] = tile(halo, j, h, 1)
            qs[h, rows(owner, 1), :] = tile(qg, j, h, 0)
            gs[h, rows(owner, 1), :] = tile(qg, j, h, 1)

    def scored(h, pair):
        span, two = rows(2 * pair, TILES + 1), rows(2 * pair, 2)
        return product(kw[h, span, :], qs[h, two, :], on_last), product(vw[h, span, :], gs[h, two, :], on_last)

    def soften(h, pair, scores, dprobs):
        index = h * 2 + pair
        for u in range(2):
            base = ((first + h) * TEAM + 2 * pair + u) * TILES
            masks = [mask_ref[base + t : base + t + 1, :] for t in range(TILES)]
            lanes = slice(u * BLK, (u + 1) * BLK)
            tiles = [slice((u + t) * BLK, (u + t + 1) * BLK) for t in range(TILES)]
            top = jnp.full((1, BLK), -jnp.inf, jnp.float32)
            for mask, tile in zip(masks, tiles):
                top = jnp.maximum(top, jnp.max(scores[tile, lanes], axis=0, keepdims=True) + mask)
            top = top * (SCALING * LOG2E)
            weights = []
            for mask, tile in zip(masks, tiles):
                weights.append(jnp.exp2(scores[tile, lanes] * (SCALING * LOG2E) - (top - mask)))
            total = sum(jnp.sum(weight, axis=0, keepdims=True) for weight in weights)
            mixed = sum(
                jnp.sum(weight * dprobs[tile, lanes], axis=0, keepdims=True) for weight, tile in zip(weights, tiles)
            )
            inverse = 1.0 / total
            delta = mixed * inverse
            for weight, tile in zip(weights, tiles):
                probs = weight * inverse
                pm[index, tile, lanes] = probs.astype(kind)
                dm[index, tile, lanes] = (probs * (dprobs[tile, lanes] - delta)).astype(kind)

    def spread(h, pair):
        index, two = h * 2 + pair, rows(2 * pair, 2)
        return product(dm[index], qs[h, two, :]) * SCALING, product(pm[index], gs[h, two, :])

    def finish(h, adds):
        split, edge = TEAM * BLK, REACH * BLK
        for part, column, half in ((0, cols(h, 1), 0), (1, cols(count + h, 1), RANK)):
            low, high = adds[0][part], adds[1][part]
            middle = low[edge:] + high[:split]
            lower, upper = low[:edge].astype(kind), high[split:].astype(kind)
            own_ref[:, column] = middle
            a_ref[:, column] = jnp.where(even, upper, lower)
            b_ref[:, column] = jnp.where(even, lower, upper)
            window = jnp.concatenate([lower, middle.astype(kind), upper], axis=0)
            term[half : half + RANK, cols(h, 1)] = product(adapt[half : half + RANK, :], window)

    items = [(h, pair) for h in range(count) for pair in range(TEAM // 2)]
    for h in range(count):
        load(h)
    ahead, adds = [scored(*item) for item in items[:2]], []
    for index, item in enumerate(items):
        current = ahead.pop(0)
        if index + 2 < len(items):
            ahead.append(scored(*items[index + 2]))
        soften(*item, *current)
        adds.append(spread(*item))
        if len(adds) == TEAM // 2:
            finish(item[0], adds)
            adds = []
    width = term.shape[1] // 4
    for i in range(4):
        parts[i, :, :width] = term[:, i * width : (i + 1) * width]
    odd, high = lax.rem(team, 2), bit_value("dp", lax.axis_size("dp") // 2, 1)

    def quarter(other_team, other_clip):
        index = 2 * jnp.bitwise_xor(odd, int(other_team)) + jnp.bitwise_xor(high, int(other_clip))
        return parts[index, :, :width]

    keep_ref[:, :width] = quarter(False, False)
    leave = quarter(True, False).astype(kind)
    if c == 0:
        team_ref[:, :width] = leave
    else:
        column = pl.ds(2 * count * HEAD_WIDTH, width)
        a_ref[rows(0, 1), column] = earlier[0][:, :width]
        a_ref[rows(1, 1), column] = leave
    for out, part in ((clip_ref, quarter(False, True)), (both_ref, quarter(True, True))):
        if c == 0:
            out[:, :width] = part.astype(kind)
        else:
            out[1, :, :width] = part.astype(kind)
    if c == 1:
        clip_ref[0] = earlier[1][...]
        both_ref[0] = earlier[2][...]


def compute(c, mask, kv, halo, qg, earlier):
    count = CHUNKS[c]
    kind = kv[0].dtype
    width = 2 * count * HEAD_WIDTH
    tall, team = WINDOW * BLK, TEAM * BLK
    out_shape = [
        jax.ShapeDtypeStruct((team, width), jnp.float32),
        jax.ShapeDtypeStruct((REACH * BLK, width + (HEAD_WIDTH if c else 0)), kind),
        jax.ShapeDtypeStruct((REACH * BLK, width), kind),
    ]
    part = (2 * RANK, padded(count * HEAD_WIDTH // 4))
    many = part if c == 0 else (2, *part)
    out_shape.append(jax.ShapeDtypeStruct(part, jnp.float32))
    if c == 0:
        out_shape.append(jax.ShapeDtypeStruct(part, kind))
    out_shape += [jax.ShapeDtypeStruct(many, kind)] * 2
    if c == 0:
        out_shape.append(jax.ShapeDtypeStruct((2 * RANK, tall), kind))
    inputs = [mask, *kv, *halo, *qg, *earlier]
    scratch = [
        pltpu.VMEM((count, tall, HEAD_WIDTH), kind),
        pltpu.VMEM((count, tall, HEAD_WIDTH), kind),
        pltpu.VMEM((count, team, HEAD_WIDTH), kind),
        pltpu.VMEM((count, team, HEAD_WIDTH), kind),
        pltpu.VMEM((count * 2, (TILES + 1) * BLK, 2 * BLK), kind),
        pltpu.VMEM((count * 2, (TILES + 1) * BLK, 2 * BLK), kind),
        pltpu.VMEM((2 * RANK, count * HEAD_WIDTH), jnp.float32),
        pltpu.VMEM((4, *part), jnp.float32),
    ]
    return call(
        functools.partial(compute_kernel, c), f"gradients_{c}", out_shape, inputs, scratch=scratch, vmem=16
    )


def combine_kernel(last, bit, own_ref, a_ref, b_ref, keep_ref, *refs):
    outs = refs[-6:-2] if last else refs[-4:]
    member, team = place()
    even = lax.rem(team, 2)
    width = own_ref.shape[1]
    start = outs[1].shape[1] - width
    if last:
        outs[1][:, :start] = refs[0][...]
    for k in range(TEAM):
        owner = jnp.bitwise_xor(member, k)
        row = rows(lax.rem(owner, 2), 1)
        from_a = owner // 2 != even
        column = slice(start, start + width) if k == 1 else slice(None)

        def add(part_ref, out=outs[k], owner=owner, row=row, column=column):
            part = part_ref[row, :width].astype(jnp.float32)
            out[:, column] = (own_ref[rows(owner, 1), :] + part).astype(out.dtype)

        pl.when(from_a)(functools.partial(add, a_ref))
        pl.when(jnp.logical_not(from_a))(functools.partial(add, b_ref))
    if last:
        earlier, clip_ref, both_ref = refs[1:4]
        totals = []
        for index, keep in enumerate((earlier, keep_ref)):
            got = a_ref[rows(index, 1), pl.ds(width, keep.shape[1])].astype(jnp.float32)
            totals.append(keep[...] + got + clip_ref[index].astype(jnp.float32) + both_ref[index].astype(jnp.float32))
        upper = bit_value(*bit) == 1
        refs[-2][...] = jnp.where(upper, *totals[::-1]).astype(refs[-2].dtype)
        refs[-1][...] = jnp.where(upper, *totals).astype(refs[-1].dtype)


def combine(c, bit, own, a, b, keep, earlier, after):
    last = int(c + 1 == len(CHUNKS))
    block = jax.ShapeDtypeStruct((BLK, own.shape[1]), a.dtype)
    wide = jax.ShapeDtypeStruct((BLK, own.shape[1] + (earlier[0].shape[1] if last else 0)), a.dtype)
    term = jax.ShapeDtypeStruct(keep.shape, a.dtype if last and len(later_rounds()) == 1 else keep.dtype)
    specs = [VMEM] * (4 + len(earlier)) + [ANY] * len(after)
    inputs = [own, a, b, keep, *earlier, *after]
    kernel = functools.partial(combine_kernel, last, bit)
    return call(kernel, f"combine_{c}", [block, wide, block, block] + [term] * (2 * last), inputs, specs)


def unpack_kernel(c, *refs):
    count = CHUNKS[c]
    own_ref, across_ref, diagonal_ref, other_ref = refs[:4]
    last = c + 1 == len(CHUNKS)
    outs = refs[-4:-2] if last else refs[-2:]
    member, _ = place()
    before = 2 * sum(CHUNKS[:c])
    for k, ref, column in ((0, own_ref, 0), (1, other_ref, before), (2, across_ref, 0), (3, diagonal_ref, 0)):
        head = jnp.bitwise_xor(member, k) * count
        for part, out in enumerate(outs):
            out[0, :, cols(head, count)] = ref[:, cols(column + part * count, count)]
    if last:
        arrived = refs[4:6]
        if len(arrived[0].shape) == 3:
            arrived = [ref.at[0] for ref in arrived]
        for half, term in zip((slice(0, RANK), slice(RANK, 2 * RANK)), refs[-2:]):
            term[...] = sum(ref[half, : term.shape[1]].astype(jnp.float32) for ref in arrived)


def unpack(c, home, other, arrived, width, earlier):
    last = c + 1 == len(CHUNKS)
    block = (1, BLK, TEAM * CHUNKS[c] * HEAD_WIDTH)
    shape = jax.ShapeDtypeStruct((1, BLK, HEAD_COUNT * HEAD_WIDTH), other.dtype)
    out_shape, out_specs = [shape] * 2, [pl.BlockSpec(block, lambda i: (0, 0, c))] * 2
    if last:
        out_shape += [jax.ShapeDtypeStruct((RANK, width), jnp.float32)] * 2
        out_specs += [pl.BlockSpec((RANK, width), lambda i: (0, 0))] * 2
    inputs = [*home, other, *arrived]
    return pl.pallas_call(
        functools.partial(unpack_kernel, c),
        grid=(1,),
        out_shape=out_shape,
        in_specs=[VMEM] * len(inputs) + [ANY] * len(earlier),
        out_specs=out_specs,
        input_output_aliases={len(inputs) + i: i for i in range(len(earlier))},
        compiler_params=pltpu.CompilerParams(vmem_limit_bytes=8 << 20),
        cost_estimate=pl.CostEstimate(flops=1, bytes_accessed=1, transcendentals=0),
        name=f"unpack_{c}",
    )(*inputs, *earlier)


def bit_value(axis, bit, unit):
    return lax.rem(lax.axis_index(axis) // (bit * unit), 2)


def fold_kernel(bit, width, held_ref, got_ref, keep_ref, send_ref):
    half = keep_ref.shape[0]
    value = bit_value(*bit)
    if len(held_ref.shape) == 2:
        for j in range(half):
            low, high = (slice(i * width, (i + 1) * width) for i in (j, half + j))
            low, high = (held_ref[:, part] + got_ref[:, part] for part in (low, high))
            keep_ref[j, :, :width] = jnp.where(value == 1, high, low).astype(keep_ref.dtype)
            send_ref[j, :, :width] = jnp.where(value == 1, low, high).astype(send_ref.dtype)
    else:
        for out, first in ((keep_ref, value * half), (send_ref, (1 - value) * half)):
            out[...] = (held_ref[pl.ds(first, half)] + got_ref[pl.ds(first, half)]).astype(out.dtype)


def later_rounds():
    clips, teams = lax.axis_size("dp"), lax.axis_size("seq") // TEAM
    clip_bits = [clips >> s for s in range(2, clips.bit_length())]
    team_bits = [teams >> s for s in range(1, teams.bit_length() - 1)]
    return [("dp", bit, 1) for bit in clip_bits] + [("seq", bit, TEAM) for bit in team_bits]


def reduce_terms(held, sent):
    clips, seq = lax.axis_size("dp"), lax.axis_size("seq")
    teams = seq // TEAM
    pieces = clips * teams
    width = HEADS * HEAD_WIDTH // pieces
    rounds = later_rounds()

    def piece_of(clip, team):
        bits = [(clip if axis == "dp" else team) // bit % 2 for axis, bit, _ in rounds]
        bits[1:1] = [team % 2, clip // (clips // 2) % 2]
        return functools.reduce(lambda value, bit: 2 * value + bit, bits, 0)

    for index, (axis, bit, unit) in enumerate(rounds[:-1]):
        route = [(i, i ^ (bit * unit)) for i in range(lax.axis_size(axis))]
        got = lax.ppermute(sent, axis, route)
        kind = jnp.bfloat16 if index + 2 == len(rounds) else jnp.float32
        shape = jax.ShapeDtypeStruct((pieces >> (index + 4), 2 * RANK, padded(width)), kind)
        kernel = functools.partial(fold_kernel, rounds[index + 1], width)
        held, sent = call(kernel, f"fold_{index}", [shape, shape], [held, got])
    arrived = []
    for flip, piece in enumerate((held, sent)):
        route = []
        for clip in range(clips):
            for position in range(seq):
                other = flip * (pieces // 2 if len(rounds) == 1 else 1)
                c, index = divmod(piece_of(clip, position // TEAM) ^ other, pieces // 2)
                route.append((clip * seq + position, (c * TEAM + position % TEAM) * pieces // 2 + index))
        arrived.append(lax.ppermute(piece, ("dp", "seq"), route))
    return arrived, width


def body(
    head_queries,
    head_keys,
    head_values,
    output_gradient,
    key_adapter_input,
    value_adapter_input,
    key_block_lists,
    live_block_counts,
):
    seq = lax.axis_size("seq")
    teams = seq // TEAM

    def partner(block, k):
        return lax.ppermute(block, "seq", [(i, i ^ k) for i in range(seq)]) if k else block

    near_route = []
    for p in range(seq):
        t = p // TEAM + (1 if p % TEAM >= TEAM // 2 else -1)
        if 0 <= t < teams:
            near_route.append((p, t * TEAM + p % TEAM))
    far_route = [(target, source) for source, target in near_route]
    swaps = []
    for start in (0, 1):
        pairs = []
        for t in range(start, teams - 1, 2):
            for m in range(TEAM):
                pairs += [(t * TEAM + m, (t + 1) * TEAM + m), ((t + 1) * TEAM + m, t * TEAM + m)]
        swaps.append(pairs)

    lists = key_block_lists.transpose(2, 1, 0)
    counts = live_block_counts.T
    adapters = (key_adapter_input.transpose(0, 2, 1), value_adapter_input.transpose(0, 2, 1))
    ((side,),) = pack("pack_side", (SIDE,), head_keys, head_values, adapters, only=0)
    kv_out = pack("pack_kv", (SIDE, OWN, ACROSS), head_keys, head_values, adapters)
    kv_side = [partner(side if c == 0 else kv_out[c][0], 1) for c in range(len(CHUNKS))]
    mask = make_mask(lists, counts, kv_out[0][1])
    qg_out = pack("pack_qg", (SIDE, OWN, ACROSS), head_queries, output_gradient, after=[mask])
    qg_side = [partner(side, 1) for side, _, _ in qg_out]
    kv, halo, qg = [], [], []
    for c in range(len(CHUNKS)):
        (_, mine, across), got = kv_out[c], kv_side[c]
        chip, send = route(f"route_kv_{c}", mine, across, got)
        kv.append((chip, partner(send, 2)))
    for c in range(len(CHUNKS)):
        (_, mine, across), got = qg_out[c], qg_side[c]
        chip, send = route(f"route_qg_{c}", mine, across, got, [kv[0][1]])
        qg.append((chip, partner(send, 2)))
        halo.append((lax.ppermute(kv[c][0], "seq", near_route), lax.ppermute(kv[c][1], "seq", far_route)))
    earlier, parts = [], []
    for c in range(len(CHUNKS)):
        own, to_a, to_b, keep, *quarters = compute(c, mask, kv[c], halo[c], qg[c], earlier)
        if c == 0:
            to_team, to_clip, to_both, adapt = quarters
            earlier = [adapt, to_team, to_clip, to_both]
        from_b = lax.ppermute(to_b, "seq", swaps[1])
        parts.append((own, lax.ppermute(to_a, "seq", swaps[0]), from_b, keep))
    to_clip, to_both = quarters
    clips = lax.axis_size("dp")
    from_clip = lax.ppermute(to_clip, "dp", [(i, i ^ (clips // 2)) for i in range(clips)])
    both = []
    for clip in range(clips):
        both += [(clip * seq + p, (clip ^ (clips // 2)) * seq + (p ^ TEAM)) for p in range(seq)]
    from_both = lax.ppermute(to_both, ("dp", "seq"), both)
    home, earlier, after = [], [], []
    for c, part in enumerate(parts):
        last = c + 1 == len(CHUNKS)
        given = [*earlier, from_clip, from_both] if last else []
        blocks = combine(c, later_rounds()[0], *part, given, after)
        home.append([blocks[0], partner(blocks[2], 2), partner(blocks[3], 3)])
        earlier, after = [blocks[1], part[-1]], home[-1][1:]
    other, (arrived, width) = partner(blocks[1], 1), reduce_terms(blocks[4], blocks[5])
    results = []
    for c in range(len(CHUNKS)):
        results = unpack(c, home[c], other, arrived if c + 1 == len(CHUNKS) else [], width, results)
    key_gradient, value_gradient, key_term, value_term = results
    return key_gradient, value_gradient, key_term.T, value_term.T


def solution(mesh):
    tokens = P("dp", "seq", None)
    shares = P(("dp", "seq"), None)
    return jax.shard_map(
        body,
        mesh=mesh,
        in_specs=(tokens,) * 6 + (P(), P()),
        out_specs=(tokens, tokens, shares, shares),
        check_vma=False,
    )
```

```python
import functools

import jax
import jax.numpy as jnp
from jax import lax
from jax.experimental import pallas as pl
from jax.experimental.pallas import tpu as pltpu
from jax.sharding import PartitionSpec as P

HEAD_COUNT = 24
HEAD_WIDTH = 128
BLK = 128
REACH = 2
TILES = 5
RANK = 64
TEAM = 4
HEADS = HEAD_COUNT // TEAM
CHUNKS = (3, 3)
WINDOW = TEAM + 2 * REACH
SCALING = HEAD_WIDTH**-0.5
LOG2E = 1.4426950408889634
ANY = pl.BlockSpec(memory_space=pl.ANY)
PACK_VMEM = 56
VMEM = pl.BlockSpec(memory_space=pltpu.VMEM)
SMEM = pl.BlockSpec(memory_space=pltpu.SMEM)
MARK = jax.ShapeDtypeStruct((8, HEAD_WIDTH), jnp.float32)


def call(kernel, name, out_shape, inputs, in_specs=None, scratch=(), vmem=4):
    return pl.pallas_call(
        kernel,
        out_shape=out_shape,
        in_specs=in_specs or [VMEM] * len(inputs),
        out_specs=[VMEM] * len(out_shape),
        scratch_shapes=list(scratch),
        compiler_params=pltpu.CompilerParams(vmem_limit_bytes=vmem << 20),
        cost_estimate=pl.CostEstimate(flops=1, bytes_accessed=1, transcendentals=0),
        name=name,
    )(*inputs)


def cols(first, count):
    if not isinstance(first, int):
        first = pl.multiple_of(first * HEAD_WIDTH, HEAD_WIDTH)
    else:
        first = first * HEAD_WIDTH
    return pl.ds(first, count * HEAD_WIDTH)


def rows(first, count):
    if not isinstance(first, int):
        first = pl.multiple_of(first * BLK, BLK)
    else:
        first = first * BLK
    return pl.ds(first, count * BLK)


def padded(columns):
    return pl.cdiv(columns, HEAD_WIDTH) * HEAD_WIDTH


def first_head(c, member):
    return (c * TEAM + member) * CHUNKS[c]


def place():
    position = lax.axis_index("seq")
    return lax.rem(position, TEAM), position // TEAM


def spans():
    return [(sum(CHUNKS[:c]), count) for c, count in enumerate(CHUNKS)]


SIDE, OWN, ACROSS = (1, 3), (0,), (2,)


def pack_plan(kinds, adapters, chunks):
    return [(span, owners, bool(adapters) and span[0] == 0) for span in chunks for owners in kinds]


def fill(plan, a_ref, b_ref, outs, part):
    member, _ = place()
    for ((first, count), owners, _), out in zip(plan, outs):
        for index, k in enumerate(owners):
            head = first_head(first // count, jnp.bitwise_xor(member, k))
            out[part, cols(2 * index * count, count)] = a_ref[part, cols(head, count)]
            out[part, cols((2 * index + 1) * count, count)] = b_ref[part, cols(head, count)]


def fill_adapters(plan, key_tile, value_tile, outs):
    for (_, _, adapted), out in zip(plan, outs):
        if adapted:
            column = cols(out.shape[1] // HEAD_WIDTH - 1, 1)
            out[:RANK, column] = key_tile
            out[RANK:, column] = value_tile


def pack_first_kernel(plan, keys, values, key_in, value_in, *refs):
    outs, (small, sems) = refs[:-2], refs[-2:]
    member, _ = place()
    copies = [(key_in.at[0], small.at[0]), (value_in.at[0], small.at[1])]
    for ((first, count), owners, _), out in zip(plan, outs):
        for index, k in enumerate(owners):
            head = first_head(first // count, jnp.bitwise_xor(member, k))
            for part, source in enumerate((keys, values)):
                target = out.at[:, cols((2 * index + part) * count, count)]
                copies.append((source.at[0, :, cols(head, count)], target))
    copies = [pltpu.make_async_copy(*pair, sems.at[i]) for i, pair in enumerate(copies)]
    for copy in copies:
        copy.start()
    for copy in copies[:2]:
        copy.wait()
    fill_adapters(plan, small[0], small[1], outs)
    for copy in copies[2:]:
        copy.wait()


def pack_kernel(plan, adapters, a_ref, b_ref, *refs):
    outs = refs[-len(plan) :]
    fill(plan, a_ref.at[0], b_ref.at[0], outs, slice(None))
    if adapters:
        fill_adapters(plan, refs[0][0], refs[1][0], outs)


def pack(name, kinds, first, second, adapters=(), after=(), only=None):
    chunks = spans() if only is None else [spans()[only]]
    plan = pack_plan(kinds, adapters, chunks)
    kind = first.dtype
    out_shape = [
        jax.ShapeDtypeStruct((BLK, (2 * count * len(owners) + adapted) * HEAD_WIDTH), kind)
        for (_, count), owners, adapted in plan
    ]
    inputs = [first, second, *adapters, *after]
    if only is not None:
        scratch = [
            pltpu.VMEM((2, RANK, BLK), kind),
            pltpu.SemaphoreType.DMA((2 + sum(2 * len(owners) for _, owners, _ in plan),)),
        ]
        kernel = functools.partial(pack_first_kernel, plan)
        outs = call(kernel, name, out_shape, inputs, [ANY] * 4, scratch, PACK_VMEM)
    else:
        kernel = functools.partial(pack_kernel, plan, bool(adapters))
        specs = [VMEM] * (2 + len(adapters)) + [ANY] * len(after)
        outs = call(kernel, name, out_shape, inputs, specs)
    return [outs[len(kinds) * c : len(kinds) * (c + 1)] for c in range(len(chunks))]


def route_kernel(mine_ref, across_ref, got_ref, *refs):
    chip_ref, send_ref = refs[-2:]
    half, extra = 2 * HEAD_WIDTH, mine_ref.shape[1] % (2 * HEAD_WIDTH)
    half = mine_ref.shape[1] - extra
    chip_ref[rows(0, 1), :] = mine_ref[...]
    chip_ref[rows(1, 1), :half] = got_ref[:, :half]
    send_ref[rows(0, 1), :] = across_ref[...]
    send_ref[rows(1, 1), :half] = got_ref[:, half : 2 * half]
    if extra:
        for out in (chip_ref, send_ref):
            out[rows(1, 1), half:] = got_ref[:, 2 * half :]


def route(name, mine, across, got, after=()):
    shape = jax.ShapeDtypeStruct((2 * BLK, mine.shape[1]), mine.dtype)
    specs = [VMEM] * 3 + [ANY] * len(after)
    return call(route_kernel, name, [shape, shape], [mine, across, got, *after], specs)


def mask_kernel(lists_ref, counts_ref, _, mask_ref):
    member, team = place()
    for h in range(HEADS):
        head = first_head(h // CHUNKS[0], member) + h % CHUNKS[0]
        for b in range(TEAM):
            block = team * TEAM + b
            used = counts_ref[block, head]
            live = jnp.int32(0)
            for t in range(TILES):
                offset = lists_ref[t, block, head] - block + REACH
                live = live | jnp.where(t < used, jnp.left_shift(1, offset), 0)
            for t in range(TILES):
                value = jnp.where((live >> t) & 1 == 1, 0.0, -jnp.inf)
                row = (h * TEAM + b) * TILES + t
                mask_ref[row : row + 1, :] = jnp.full((1, BLK), value, jnp.float32)


def make_mask(lists, counts, after):
    shape = jax.ShapeDtypeStruct((HEADS * TEAM * TILES, BLK), jnp.float32)
    return call(mask_kernel, "mask", [shape], [lists, counts, after], [SMEM, SMEM, ANY])[0]


def compute_kernel(c, mask_ref, *refs):
    first, count = spans()[c]
    kv, halo, qg, rest = refs[:2], refs[2:4], refs[4:6], refs[6:]
    kw, vw, qs, gs, pm, dm, term, parts = rest[-8:]
    if c == 0:
        own_ref, a_ref, b_ref, keep_ref, team_ref, clip_ref, both_ref, adapt = rest[:-8]
    else:
        adapt, *earlier, own_ref, a_ref, b_ref, keep_ref, clip_ref, both_ref = rest[:-8]
    kind = adapt.dtype
    member, team = place()
    even = lax.rem(team, 2) == 0
    places = []
    for j in range(TEAM):
        owner = jnp.bitwise_xor(member, j)
        places.append((owner, owner + REACH, lax.rem(owner + REACH + TEAM, WINDOW)))

    def tile(refs, j, h, part):
        return refs[j // 2][rows(j % 2, 1), cols(part * count + h, 1)]

    if c == 0:
        for j, (_, near, far) in enumerate(places):
            adapt[:, rows(near, 1)] = tile(kv, j, 0, 2)
            adapt[:, rows(far, 1)] = tile(halo, j, 0, 2)

    zero = jnp.zeros((BLK, BLK), kind)
    for index in range(count * 2):
        for matrix in (pm, dm):
            matrix[index, rows(TILES, 1), :BLK] = zero
            matrix[index, rows(0, 1), BLK:] = zero

    on_last = (((1,), (1,)), ((), ()))

    def product(left, right, dims=(((1,), (0,)), ((), ()))):
        return lax.dot_general(left, right, dims, preferred_element_type=jnp.float32)

    def load(h):
        for j, (owner, near, far) in enumerate(places):
            kw[h, rows(near, 1), :] = tile(kv, j, h, 0)
            vw[h, rows(near, 1), :] = tile(kv, j, h, 1)
            kw[h, rows(far, 1), :] = tile(halo, j, h, 0)
            vw[h, rows(far, 1), :] = tile(halo, j, h, 1)
            qs[h, rows(owner, 1), :] = tile(qg, j, h, 0)
            gs[h, rows(owner, 1), :] = tile(qg, j, h, 1)

    def scored(h, pair):
        span, two = rows(2 * pair, TILES + 1), rows(2 * pair, 2)
        return product(kw[h, span, :], qs[h, two, :], on_last), product(vw[h, span, :], gs[h, two, :], on_last)

    def soften(h, pair, scores, dprobs):
        index = h * 2 + pair
        for u in range(2):
            base = ((first + h) * TEAM + 2 * pair + u) * TILES
            masks = [mask_ref[base + t : base + t + 1, :] for t in range(TILES)]
            lanes = slice(u * BLK, (u + 1) * BLK)
            tiles = [slice((u + t) * BLK, (u + t + 1) * BLK) for t in range(TILES)]
            top = jnp.full((1, BLK), -jnp.inf, jnp.float32)
            for mask, tile in zip(masks, tiles):
                top = jnp.maximum(top, jnp.max(scores[tile, lanes], axis=0, keepdims=True) + mask)
            top = top * (SCALING * LOG2E)
            weights = []
            for mask, tile in zip(masks, tiles):
                weights.append(jnp.exp2(scores[tile, lanes] * (SCALING * LOG2E) - (top - mask)))
            total = sum(jnp.sum(weight, axis=0, keepdims=True) for weight in weights)
            mixed = sum(
                jnp.sum(weight * dprobs[tile, lanes], axis=0, keepdims=True) for weight, tile in zip(weights, tiles)
            )
            inverse = 1.0 / total
            delta = mixed * inverse
            for weight, tile in zip(weights, tiles):
                probs = weight * inverse
                pm[index, tile, lanes] = probs.astype(kind)
            for weight, tile in zip(weights, tiles):
                dm[index, tile, lanes] = (weight * inverse * (dprobs[tile, lanes] - delta)).astype(kind)

    def spread(h, pair):
        index, two = h * 2 + pair, rows(2 * pair, 2)
        return product(dm[index], qs[h, two, :]) * SCALING, product(pm[index], gs[h, two, :])

    def finish(h, adds):
        split, edge = TEAM * BLK, REACH * BLK
        for part, column, half in ((0, cols(h, 1), 0), (1, cols(count + h, 1), RANK)):
            low, high = adds[0][part], adds[1][part]
            middle = low[edge:] + high[:split]
            lower, upper = low[:edge].astype(kind), high[split:].astype(kind)
            own_ref[:, column] = middle
            a_ref[:, column] = jnp.where(even, upper, lower)
            b_ref[:, column] = jnp.where(even, lower, upper)
            window = jnp.concatenate([lower, middle.astype(kind), upper], axis=0)
            term[half : half + RANK, cols(h, 1)] = product(adapt[half : half + RANK, :], window)

    items = [(h, pair) for h in range(count) for pair in range(TEAM // 2)]
    for h in range(count):
        load(h)
    ahead, adds = [scored(*item) for item in items[:2]], []
    for index, item in enumerate(items):
        current = ahead.pop(0)
        if index + 2 < len(items):
            ahead.append(scored(*items[index + 2]))
        soften(*item, *current)
        adds.append(spread(*item))
        if len(adds) == TEAM // 2:
            finish(item[0], adds)
            adds = []
    width = term.shape[1] // 4
    for i in range(4):
        parts[i, :, :width] = term[:, i * width : (i + 1) * width]
    odd, high = lax.rem(team, 2), bit_value("dp", lax.axis_size("dp") // 2, 1)

    def quarter(other_team, other_clip):
        index = 2 * jnp.bitwise_xor(odd, int(other_team)) + jnp.bitwise_xor(high, int(other_clip))
        return parts[index, :, :width]

    keep_ref[:, :width] = quarter(False, False)
    leave = quarter(True, False).astype(kind)
    if c == 0:
        team_ref[:, :width] = leave
    else:
        column = pl.ds(2 * count * HEAD_WIDTH, width)
        a_ref[rows(0, 1), column] = earlier[0][:, :width]
        a_ref[rows(1, 1), column] = leave
    for out, part in ((clip_ref, quarter(False, True)), (both_ref, quarter(True, True))):
        if c == 0:
            out[:, :width] = part.astype(kind)
        else:
            out[1, :, :width] = part.astype(kind)
    if c == 1:
        clip_ref[0] = earlier[1][...]
        both_ref[0] = earlier[2][...]


def compute(c, mask, kv, halo, qg, earlier):
    count = CHUNKS[c]
    kind = kv[0].dtype
    width = 2 * count * HEAD_WIDTH
    tall, team = WINDOW * BLK, TEAM * BLK
    out_shape = [
        jax.ShapeDtypeStruct((team, width), jnp.float32),
        jax.ShapeDtypeStruct((REACH * BLK, width + (HEAD_WIDTH if c else 0)), kind),
        jax.ShapeDtypeStruct((REACH * BLK, width), kind),
    ]
    part = (2 * RANK, padded(count * HEAD_WIDTH // 4))
    many = part if c == 0 else (2, *part)
    out_shape.append(jax.ShapeDtypeStruct(part, jnp.float32))
    if c == 0:
        out_shape.append(jax.ShapeDtypeStruct(part, kind))
    out_shape += [jax.ShapeDtypeStruct(many, kind)] * 2
    if c == 0:
        out_shape.append(jax.ShapeDtypeStruct((2 * RANK, tall), kind))
    inputs = [mask, *kv, *halo, *qg, *earlier]
    scratch = [
        pltpu.VMEM((count, tall, HEAD_WIDTH), kind),
        pltpu.VMEM((count, tall, HEAD_WIDTH), kind),
        pltpu.VMEM((count, team, HEAD_WIDTH), kind),
        pltpu.VMEM((count, team, HEAD_WIDTH), kind),
        pltpu.VMEM((count * 2, (TILES + 1) * BLK, 2 * BLK), kind),
        pltpu.VMEM((count * 2, (TILES + 1) * BLK, 2 * BLK), kind),
        pltpu.VMEM((2 * RANK, count * HEAD_WIDTH), jnp.float32),
        pltpu.VMEM((4, *part), jnp.float32),
    ]
    return call(
        functools.partial(compute_kernel, c), f"gradients_{c}", out_shape, inputs, scratch=scratch, vmem=16
    )


def combine_kernel(last, bit, own_ref, a_ref, b_ref, keep_ref, *refs):
    outs = refs[-6:-2] if last else refs[-4:]
    member, team = place()
    even = lax.rem(team, 2)
    width = own_ref.shape[1]
    start = outs[1].shape[1] - width
    if last:
        outs[1][:, :start] = refs[0][...]
    for k in range(TEAM):
        owner = jnp.bitwise_xor(member, k)
        row = rows(lax.rem(owner, 2), 1)
        from_a = owner // 2 != even
        column = slice(start, start + width) if k == 1 else slice(None)

        def add(part_ref, out=outs[k], owner=owner, row=row, column=column):
            part = part_ref[row, :width].astype(jnp.float32)
            out[:, column] = (own_ref[rows(owner, 1), :] + part).astype(out.dtype)

        pl.when(from_a)(functools.partial(add, a_ref))
        pl.when(jnp.logical_not(from_a))(functools.partial(add, b_ref))
    if last:
        earlier, clip_ref, both_ref = refs[1:4]
        totals = []
        for index, keep in enumerate((earlier, keep_ref)):
            got = a_ref[rows(index, 1), pl.ds(width, keep.shape[1])].astype(jnp.float32)
            totals.append(keep[...] + got + clip_ref[index].astype(jnp.float32) + both_ref[index].astype(jnp.float32))
        upper = bit_value(*bit) == 1
        refs[-2][...] = jnp.where(upper, *totals[::-1]).astype(refs[-2].dtype)
        refs[-1][...] = jnp.where(upper, *totals).astype(refs[-1].dtype)


def combine(c, bit, own, a, b, keep, earlier, after):
    last = int(c + 1 == len(CHUNKS))
    block = jax.ShapeDtypeStruct((BLK, own.shape[1]), a.dtype)
    wide = jax.ShapeDtypeStruct((BLK, own.shape[1] + (earlier[0].shape[1] if last else 0)), a.dtype)
    term = jax.ShapeDtypeStruct(keep.shape, a.dtype if last and len(later_rounds()) == 1 else keep.dtype)
    specs = [VMEM] * (4 + len(earlier)) + [ANY] * len(after)
    inputs = [own, a, b, keep, *earlier, *after]
    kernel = functools.partial(combine_kernel, last, bit)
    return call(kernel, f"combine_{c}", [block, wide, block, block] + [term] * (2 * last), inputs, specs)


def unpack_kernel(c, *refs):
    count = CHUNKS[c]
    own_ref, across_ref, diagonal_ref, other_ref = refs[:4]
    last = c + 1 == len(CHUNKS)
    outs = refs[-4:-2] if last else refs[-2:]
    member, _ = place()
    before = 2 * sum(CHUNKS[:c])
    for k, ref, column in ((0, own_ref, 0), (1, other_ref, before), (2, across_ref, 0), (3, diagonal_ref, 0)):
        head = jnp.bitwise_xor(member, k) * count
        for part, out in enumerate(outs):
            out[0, :, cols(head, count)] = ref[:, cols(column + part * count, count)]
    if last:
        arrived = refs[4:6]
        if len(arrived[0].shape) == 3:
            arrived = [ref.at[0] for ref in arrived]
        for half, term in zip((slice(0, RANK), slice(RANK, 2 * RANK)), refs[-2:]):
            term[...] = sum(ref[half, : term.shape[1]].astype(jnp.float32) for ref in arrived)


def unpack(c, home, other, arrived, width, earlier):
    last = c + 1 == len(CHUNKS)
    block = (1, BLK, TEAM * CHUNKS[c] * HEAD_WIDTH)
    shape = jax.ShapeDtypeStruct((1, BLK, HEAD_COUNT * HEAD_WIDTH), other.dtype)
    out_shape, out_specs = [shape] * 2, [pl.BlockSpec(block, lambda i: (0, 0, c))] * 2
    if last:
        out_shape += [jax.ShapeDtypeStruct((RANK, width), jnp.float32)] * 2
        out_specs += [pl.BlockSpec((RANK, width), lambda i: (0, 0))] * 2
    inputs = [*home, other, *arrived]
    return pl.pallas_call(
        functools.partial(unpack_kernel, c),
        grid=(1,),
        out_shape=out_shape,
        in_specs=[VMEM] * len(inputs) + [ANY] * len(earlier),
        out_specs=out_specs,
        input_output_aliases={len(inputs) + i: i for i in range(len(earlier))},
        compiler_params=pltpu.CompilerParams(vmem_limit_bytes=8 << 20),
        cost_estimate=pl.CostEstimate(flops=1, bytes_accessed=1, transcendentals=0),
        name=f"unpack_{c}",
    )(*inputs, *earlier)


def bit_value(axis, bit, unit):
    return lax.rem(lax.axis_index(axis) // (bit * unit), 2)


def fold_kernel(bit, width, held_ref, got_ref, keep_ref, send_ref):
    half = keep_ref.shape[0]
    value = bit_value(*bit)
    if len(held_ref.shape) == 2:
        for j in range(half):
            low, high = (slice(i * width, (i + 1) * width) for i in (j, half + j))
            low, high = (held_ref[:, part] + got_ref[:, part] for part in (low, high))
            keep_ref[j, :, :width] = jnp.where(value == 1, high, low).astype(keep_ref.dtype)
            send_ref[j, :, :width] = jnp.where(value == 1, low, high).astype(send_ref.dtype)
    else:
        for out, first in ((keep_ref, value * half), (send_ref, (1 - value) * half)):
            out[...] = (held_ref[pl.ds(first, half)] + got_ref[pl.ds(first, half)]).astype(out.dtype)


def later_rounds():
    clips, teams = lax.axis_size("dp"), lax.axis_size("seq") // TEAM
    clip_bits = [clips >> s for s in range(2, clips.bit_length())]
    team_bits = [teams >> s for s in range(1, teams.bit_length() - 1)]
    return [("dp", bit, 1) for bit in clip_bits] + [("seq", bit, TEAM) for bit in team_bits]


def reduce_terms(held, sent):
    clips, seq = lax.axis_size("dp"), lax.axis_size("seq")
    teams = seq // TEAM
    pieces = clips * teams
    width = HEADS * HEAD_WIDTH // pieces
    rounds = later_rounds()

    def piece_of(clip, team):
        bits = [(clip if axis == "dp" else team) // bit % 2 for axis, bit, _ in rounds]
        bits[1:1] = [team % 2, clip // (clips // 2) % 2]
        return functools.reduce(lambda value, bit: 2 * value + bit, bits, 0)

    for index, (axis, bit, unit) in enumerate(rounds[:-1]):
        route = [(i, i ^ (bit * unit)) for i in range(lax.axis_size(axis))]
        got = lax.ppermute(sent, axis, route)
        kind = jnp.bfloat16 if index + 2 == len(rounds) else jnp.float32
        shape = jax.ShapeDtypeStruct((pieces >> (index + 4), 2 * RANK, padded(width)), kind)
        kernel = functools.partial(fold_kernel, rounds[index + 1], width)
        held, sent = call(kernel, f"fold_{index}", [shape, shape], [held, got])
    arrived = []
    for flip, piece in enumerate((held, sent)):
        route = []
        for clip in range(clips):
            for position in range(seq):
                other = flip * (pieces // 2 if len(rounds) == 1 else 1)
                c, index = divmod(piece_of(clip, position // TEAM) ^ other, pieces // 2)
                route.append((clip * seq + position, (c * TEAM + position % TEAM) * pieces // 2 + index))
        arrived.append(lax.ppermute(piece, ("dp", "seq"), route))
    return arrived, width


def body(
    head_queries,
    head_keys,
    head_values,
    output_gradient,
    key_adapter_input,
    value_adapter_input,
    key_block_lists,
    live_block_counts,
):
    seq = lax.axis_size("seq")
    teams = seq // TEAM

    def partner(block, k):
        return lax.ppermute(block, "seq", [(i, i ^ k) for i in range(seq)]) if k else block

    near_route = []
    for p in range(seq):
        t = p // TEAM + (1 if p % TEAM >= TEAM // 2 else -1)
        if 0 <= t < teams:
            near_route.append((p, t * TEAM + p % TEAM))
    far_route = [(target, source) for source, target in near_route]
    swaps = []
    for start in (0, 1):
        pairs = []
        for t in range(start, teams - 1, 2):
            for m in range(TEAM):
                pairs += [(t * TEAM + m, (t + 1) * TEAM + m), ((t + 1) * TEAM + m, t * TEAM + m)]
        swaps.append(pairs)

    lists = key_block_lists.transpose(2, 1, 0)
    counts = live_block_counts.T
    adapters = (key_adapter_input.transpose(0, 2, 1), value_adapter_input.transpose(0, 2, 1))
    ((side,),) = pack("pack_side", (SIDE,), head_keys, head_values, adapters, only=0)
    kv_out = pack("pack_kv", (SIDE, OWN, ACROSS), head_keys, head_values, adapters)
    kv_side = [partner(side if c == 0 else kv_out[c][0], 1) for c in range(len(CHUNKS))]
    mask = make_mask(lists, counts, kv_out[0][1])
    qg_out = pack("pack_qg", (SIDE, OWN, ACROSS), head_queries, output_gradient, after=[mask])
    qg_side = [partner(side, 1) for side, _, _ in qg_out]
    kv, halo, qg = [], [], []
    for c in range(len(CHUNKS)):
        (_, mine, across), got = kv_out[c], kv_side[c]
        chip, send = route(f"route_kv_{c}", mine, across, got)
        kv.append((chip, partner(send, 2)))
    for c in range(len(CHUNKS)):
        (_, mine, across), got = qg_out[c], qg_side[c]
        chip, send = route(f"route_qg_{c}", mine, across, got, [kv[0][1]])
        qg.append((chip, partner(send, 2)))
        halo.append((lax.ppermute(kv[c][0], "seq", near_route), lax.ppermute(kv[c][1], "seq", far_route)))
    earlier, parts = [], []
    for c in range(len(CHUNKS)):
        own, to_a, to_b, keep, *quarters = compute(c, mask, kv[c], halo[c], qg[c], earlier)
        if c == 0:
            to_team, to_clip, to_both, adapt = quarters
            earlier = [adapt, to_team, to_clip, to_both]
        from_b = lax.ppermute(to_b, "seq", swaps[1])
        parts.append((own, lax.ppermute(to_a, "seq", swaps[0]), from_b, keep))
    to_clip, to_both = quarters
    clips = lax.axis_size("dp")
    from_clip = lax.ppermute(to_clip, "dp", [(i, i ^ (clips // 2)) for i in range(clips)])
    both = []
    for clip in range(clips):
        both += [(clip * seq + p, (clip ^ (clips // 2)) * seq + (p ^ TEAM)) for p in range(seq)]
    from_both = lax.ppermute(to_both, ("dp", "seq"), both)
    home, earlier, after = [], [], []
    for c, part in enumerate(parts):
        last = c + 1 == len(CHUNKS)
        given = [*earlier, from_clip, from_both] if last else []
        blocks = combine(c, later_rounds()[0], *part, given, after)
        home.append([blocks[0], partner(blocks[2], 2), partner(blocks[3], 3)])
        earlier, after = [blocks[1], part[-1]], home[-1][1:]
    other, (arrived, width) = partner(blocks[1], 1), reduce_terms(blocks[4], blocks[5])
    results = []
    for c in range(len(CHUNKS)):
        results = unpack(c, home[c], other, arrived if c + 1 == len(CHUNKS) else [], width, results)
    key_gradient, value_gradient, key_term, value_term = results
    return key_gradient, value_gradient, key_term.T, value_term.T


def solution(mesh):
    tokens = P("dp", "seq", None)
    shares = P(("dp", "seq"), None)
    return jax.shard_map(
        body,
        mesh=mesh,
        in_specs=(tokens,) * 6 + (P(), P()),
        out_specs=(tokens, tokens, shares, shares),
        check_vma=False,
    )
```
